32 devices in a mesh: wide: 8 (over z, y), narrow: 4 (over x, core).
Axes of the slice: x: 2, y: 2, z: 4, core: 2. Of those that a mesh axis runs over, the one named last changes fastest.
Arguments:
- activations: bfloat16 [512, 8192], P(('wide', 'narrow')), may hold values from -6 to 6
- cotangent: bfloat16 [512, 8192], P('wide', 'narrow'), may hold values from -6 to 6
- gate_proj: bfloat16 [8192, 26624], P('narrow', 'wide'), may hold values from -0.0625 to 0.0625
- up_proj: bfloat16 [8192, 26624], P('narrow', 'wide'), may hold values from -0.0625 to 0.0625
- down_proj: bfloat16 [26624, 8192], P('wide', 'narrow'), may hold values from -0.0390625 to 0.0390625
Outputs:
- block_output: bfloat16 [512, 8192], P('wide', 'narrow')
- input_gradient: bfloat16 [512, 8192], P(('wide', 'narrow'))
- gate_gradient: bfloat16 [8192, 26624], P('narrow', 'wide')
- up_gradient: bfloat16 [8192, 26624], P('narrow', 'wide')
- down_gradient: bfloat16 [26624, 8192], P('wide', 'narrow')
The draws below stay inside these ranges and needn't reach their ends.
All inputs are finite; a program needn't handle non-finite values.
Results may differ from the reference program's by a relative error of at most 0.005.
Values may be sent and summed in bfloat16 or wider, within the bound.
No kernel may reach another device: no remote copies, remote signals or barrier semaphores. Data moves between devices by JAX's collectives and lax.ppermute only.
A program may use at most 192 MiB of HBM per device.

```python
import jax
import jax.numpy as jnp

D = 8192
FF = 26624
TOKENS = 512


def steps_of(key, dims, split, smallest, high):
    def one(axis_at, parts):
        steps = jax.random.uniform(jax.random.fold_in(jax.random.fold_in(key, 6), axis_at), (parts,), jnp.float32, smallest / len(split), high / len(split))
        return jnp.repeat(jnp.exp(steps), dims[axis_at] // parts).reshape((-1,) + (1,) * (len(dims) - axis_at - 1))

    level = one(*split[0])
    for cut in split[1:]:
        level = level * one(*cut)
    return level


def noise(rng, extent, deviation, reach, cuts=(), dtype=jnp.bfloat16):
    values = jax.random.normal(rng, extent, jnp.float32) * deviation
    if len(cuts) > 0:
        values = steps_of(rng, extent, cuts, -0.22, 0.18) * values
    return jnp.clip(values, min=-reach, max=reach).astype(dtype)


def setup_inputs(seed: int = 0) -> dict:
    seeds = jax.random.split(jax.random.key(seed), 6)
    activations = noise(seeds[0], (TOKENS, D), 1.0, 6.0, ((0, 32),))
    cotangent = noise(seeds[1], (TOKENS, D), 1.0, 6.0, ((0, 8), (1, 4)))
    gate_proj = noise(seeds[2], (D, FF), D ** -0.5, 0.0625, ((0, 4), (1, 8)))
    up_proj = noise(seeds[3], (D, FF), D ** -0.5, 0.0625, ((0, 4), (1, 8)))
    down_proj = noise(seeds[4], (FF, D), FF ** -0.5, 0.0390625, ((0, 8), (1, 4)))
    return dict(activations=activations, cotangent=cotangent, gate_proj=gate_proj, up_proj=up_proj, down_proj=down_proj)


def silu_parts(gate):
    sigma = jax.nn.sigmoid(gate)
    return gate * sigma, sigma * (1.0 + gate * (1.0 - sigma))


def reference(activations, cotangent, gate_proj, up_proj, down_proj):
    gate = jnp.dot(activations, gate_proj, preferred_element_type=jnp.float32)
    up = jnp.dot(activations, up_proj, preferred_element_type=jnp.float32)
    active, slope = silu_parts(gate)
    hidden = (active * up).astype(jnp.bfloat16)
    block_output = jnp.dot(hidden, down_proj, preferred_element_type=jnp.float32).astype(jnp.bfloat16)
    back = jnp.dot(cotangent, down_proj.T, preferred_element_type=jnp.float32)
    gate_delta = (back * up * slope).astype(jnp.bfloat16)
    up_delta = (back * active).astype(jnp.bfloat16)
    down_gradient = jnp.dot(hidden.T, cotangent, preferred_element_type=jnp.float32).astype(jnp.bfloat16)
    gate_gradient = jnp.dot(activations.T, gate_delta, preferred_element_type=jnp.float32).astype(jnp.bfloat16)
    up_gradient = jnp.dot(activations.T, up_delta, preferred_element_type=jnp.float32).astype(jnp.bfloat16)
    input_gradient = (jnp.dot(gate_delta, gate_proj.T, preferred_element_type=jnp.float32)
                      + jnp.dot(up_delta, up_proj.T, preferred_element_type=jnp.float32)).astype(jnp.bfloat16)
    return block_output, input_gradient, gate_gradient, up_gradient, down_gradient
```

```python
import jax
import jax.numpy as jnp
from jax import lax
from jax.sharding import PartitionSpec as P

CHUNKS = 2


def silu_parts(gate):
    sigma = jax.nn.sigmoid(gate)
    return (gate * sigma, sigma * (1.0 + gate * (1.0 - sigma)))


def contract_rows(left, right):
    return lax.dot_general(
        left, right, (((0,), (0,)), ((), ())), preferred_element_type=jnp.float32
    )


def contract_cols(left, right):
    return lax.dot_general(
        left, right, (((1,), (1,)), ((), ())), preferred_element_type=jnp.float32
    )


def swap(value, mask):
    return lax.ppermute(value, "narrow", [(i, i ^ mask) for i in range(4)])


def scatter_sum(part, wide):
    split = part.reshape(wide, 4, -1, part.shape[-1])
    got = swap(jnp.stack([split[:, 1], split[:, 3]]), 1)
    away = (split[:, 2] + got[1]).astype(jnp.bfloat16)
    return (split[:, 0] + got[0]) + swap(away, 2).astype(jnp.float32)


def spread(own):
    far = swap(own, 2)
    pair = swap(jnp.stack([own, far]), 1)
    whole = jnp.stack([own, pair[0], far, pair[1]], axis=1)
    return whole.reshape(-1, own.shape[-1])


def local(activations, cotangent, gate_proj, up_proj, down_proj):
    wide = lax.axis_size("wide")
    me = lax.axis_index("narrow")
    rows = activations.shape[0]
    tile = activations.shape[1] // 4
    half = rows // CHUNKS

    pieces = [lax.dynamic_slice_in_dim(activations, (me ^ g) * tile, tile, 1) for g in range(4)]
    pieces = [pieces[0]] + [swap(pieces[g], g) for g in range(1, 4)]
    cots = [lax.dynamic_slice_in_dim(cotangent, (me ^ g) * rows, rows, 0) for g in range(4)]

    def gathered(parts, c):
        mine = jnp.stack([p[c * half : (c + 1) * half] for p in parts])
        return lax.all_gather(mine, "wide", axis=0, tiled=True).reshape(-1, tile)

    features, upstream = [], []
    for c in range(CHUNKS):
        features.append(gathered(pieces, c))
        upstream.append(gathered(cots, c))

    hidden, gate_delta, up_delta, outs, tiles = [], [], [], [], []
    for c in range(CHUNKS):
        gate = scatter_sum(jnp.dot(features[c], gate_proj, preferred_element_type=jnp.float32), wide)
        up = scatter_sum(jnp.dot(features[c], up_proj, preferred_element_type=jnp.float32), wide)
        back = scatter_sum(contract_cols(upstream[c], down_proj), wide)
        active, slope = silu_parts(gate)
        gate_delta.append(spread((back * up * slope).astype(jnp.bfloat16)))
        up_delta.append(spread((back * active).astype(jnp.bfloat16)))
        hidden.append(spread((active * up).astype(jnp.bfloat16)))

    def landed(total):
        got = lax.psum_scatter(total, "wide", scatter_dimension=0, tiled=True)
        return got.astype(jnp.bfloat16).reshape(4, half, tile)

    for c in range(CHUNKS):
        tiles.append(
            landed(contract_cols(gate_delta[c], gate_proj) + contract_cols(up_delta[c], up_proj))
        )
        outs.append(landed(jnp.dot(hidden[c], down_proj, preferred_element_type=jnp.float32)))

    features, upstream = jnp.concatenate(features), jnp.concatenate(upstream)
    gate_gradient = contract_rows(features, jnp.concatenate(gate_delta)).astype(jnp.bfloat16)
    up_gradient = contract_rows(features, jnp.concatenate(up_delta)).astype(jnp.bfloat16)
    down_gradient = contract_rows(jnp.concatenate(hidden), upstream).astype(jnp.bfloat16)

    out = jnp.concatenate(outs, axis=1)
    block_output = jnp.concatenate(
        [lax.dynamic_index_in_dim(out, me ^ g, 0, keepdims=False) for g in range(4)]
    )
    grad = jnp.concatenate(tiles, axis=1)
    grads = jnp.stack([grad[0]] + [swap(grad[g], g) for g in range(1, 4)])
    input_gradient = jnp.concatenate(
        [lax.dynamic_index_in_dim(grads, me ^ g, 0, keepdims=False) for g in range(4)], axis=1
    )
    return (block_output, input_gradient, gate_gradient, up_gradient, down_gradient)


def solution(mesh):
    placed = (
        P(("wide", "narrow"), None),
        P("wide", "narrow"),
        P("narrow", "wide"),
        P("narrow", "wide"),
        P("wide", "narrow"),
    )
    return jax.shard_map(
        local,
        mesh=mesh,
        in_specs=placed,
        out_specs=(
            P("wide", "narrow"),
            P(("wide", "narrow"), None),
            P("narrow", "wide"),
            P("narrow", "wide"),
            P("wide", "narrow"),
        ),
        check_vma=False,
    )
```

```python
import functools

import jax
import jax.numpy as jnp
from jax import lax
from jax.experimental import pallas as pl
from jax.experimental.pallas import tpu as pltpu
from jax.sharding import PartitionSpec as P

BF16, F32 = jnp.bfloat16, jnp.float32
BLOCK = 256
VMEM_LIMIT = 48 * 1024 * 1024
NN = (((1,), (0,)), ((), ()))
NT = (((1,), (1,)), ((), ()))
TN = (((0,), (0,)), ((), ()))


def dot(left, right, dims):
    return lax.dot_general(left, right, dims, preferred_element_type=F32)


def silu_parts(gate):
    sigma = jax.nn.sigmoid(gate)
    return (gate * sigma, sigma * (1.0 + gate * (1.0 - sigma)))


def swap(value, mask):
    return lax.ppermute(value, "narrow", [(i, i ^ mask) for i in range(4)])


def swap_wide(value, mask):
    return lax.ppermute(value, "wide", [(i, i ^ mask) for i in range(8)])


class Chain:
    def __init__(self):
        self.token = None
        self.waits = []

    def after(self, *arrays):
        self.waits += arrays

    def __call__(self, body, grid, ins, outs, scratch=(), flops=0, alias=None, scalar=None):
        lead = 0 if scalar is None else 1
        arrays = [a for a, _, _ in ins]
        specs = [pl.BlockSpec(block, index) for _, block, index in ins]
        unread = self.waits + ([] if self.token is None else [self.token])
        self.waits = []
        arrays += unread
        specs += [pl.BlockSpec(memory_space=pl.ANY)] * len(unread)
        shapes = [jax.ShapeDtypeStruct(shape, dtype) for shape, dtype, _, _ in outs]
        out_specs = [pl.BlockSpec(block, index) for _, _, block, index in outs]
        shapes.append(jax.ShapeDtypeStruct((8, 128), F32))
        out_specs.append(pl.BlockSpec((8, 128), lambda *i: (0, 0)))
        n_in, n_out = len(ins), len(outs)

        def kernel(*refs):
            head, refs = refs[:lead], refs[lead:]
            in_refs = refs[:n_in]
            rest = refs[n_in + len(unread) :]
            out_refs, token, scratch_refs = rest[:n_out], rest[n_out], rest[n_out + 1 :]
            token[...] = jnp.zeros(token.shape, F32)
            body(*head, *in_refs, *out_refs, *scratch_refs)

        res = pl.pallas_call(
            kernel,
            grid_spec=pltpu.PrefetchScalarGridSpec(
                num_scalar_prefetch=lead,
                grid=grid,
                in_specs=specs,
                out_specs=out_specs,
                scratch_shapes=list(scratch),
            ),
            out_shape=shapes,
            input_output_aliases={k + lead: v for k, v in (alias or {}).items()},
            compiler_params=pltpu.CompilerParams(vmem_limit_bytes=VMEM_LIMIT),
            cost_estimate=pl.CostEstimate(flops=1, bytes_accessed=1, transcendentals=0),
        )(*(() if scalar is None else (scalar,)), *arrays)
        self.token = res[-1]
        return res[:-1]


def arrange(chain, me, pieces, rows, tile):
    def body(_, *refs):
        out = refs[8]
        for k in range(8):
            out[0, k] = refs[k][...]

    (out,) = chain(
        body,
        (4,),
        [(p, (rows, tile), lambda g, s: (s[0] ^ g, 0)) for p in pieces],
        [((4, 8, rows, tile), BF16, (1, 8, rows, tile), lambda g, s: (g, 0, 0, 0))],
        scalar=me,
    )
    return out.reshape(32 * rows, tile)


def parted(acc, q, keep, send):
    for i in range(2):
        keep[i] = acc[2 * i * q : (2 * i + 1) * q]
        send[i] = acc[(2 * i + 1) * q : (2 * i + 2) * q]


def back_part(chain, cot, down, base, blocks):
    tokens, tile = cot.shape
    q, n = tokens // 4, blocks * BLOCK

    def body(c, w, keep, send):
        parted(dot(c[...], w[...], NT), q, keep, send)

    out = ((2, q, n), F32, (2, q, BLOCK), lambda j: (0, 0, j))
    return chain(
        body,
        (blocks,),
        [(cot, cot.shape, lambda j: (0, 0)), (down, (BLOCK, tile), lambda j: (base + j, 0))],
        [out, out],
        flops=2 * tokens * tile * n,
    )


def gate_up_part(chain, act, gate, up, base, blocks):
    tokens, tile = act.shape
    q, n = tokens // 4, blocks * BLOCK

    def body(a, wg, wu, keep, send):
        parted(dot(a[...], wg[...], NN), q, keep.at[:, 0], send.at[:, 0])
        parted(dot(a[...], wu[...], NN), q, keep.at[:, 1], send.at[:, 1])

    weight = ((tile, BLOCK), lambda j: (0, base + j))
    out = ((2, 2, q, n), F32, (2, 2, q, BLOCK), lambda j: (0, 0, 0, j))
    return chain(
        body,
        (blocks,),
        [(act, act.shape, lambda j: (0, 0)), (gate, *weight), (up, *weight)],
        [out, out],
        flops=4 * tokens * tile * n,
    )


def add_away(chain, keep, got):
    shape = keep.shape[1:]
    zeros = (0,) * (len(shape) - 1)
    block = (1, *shape[:-1], BLOCK)

    def body(a, b, out):
        out[...] = (a[0] + b[0]).astype(BF16)

    def at(j):
        return (1, *zeros, j)

    (out,) = chain(
        body,
        (shape[-1] // BLOCK,),
        [(keep, block, at), (got, block, at)],
        [(shape, BF16, block[1:], lambda j: (*zeros, j))],
    )
    return out


def activate(chain, keep_gu, got_gu, far_gu, keep_b, got_b, far_b, merged):
    q, n = far_b.shape

    def body(kg, gg, fg, kb, gb, fb, deltas, *rest):
        gate = kg[0, 0] + gg[0, 0] + fg[0].astype(F32)
        up = kg[0, 1] + gg[0, 1] + fg[1].astype(F32)
        back = kb[0] + gb[0] + fb[...].astype(F32)
        active, slope = silu_parts(gate)
        if merged:
            deltas[2] = (active * up).astype(BF16)
        else:
            rest[0][0] = (active * up).astype(BF16)
        deltas[0] = (back * up * slope).astype(BF16)
        deltas[1] = (back * active).astype(BF16)

    four = ((1, 2, q, BLOCK), lambda j: (0, 0, 0, j))
    three = ((1, q, BLOCK), lambda j: (0, 0, j))
    return chain(
        body,
        (n // BLOCK,),
        [
            (keep_gu, *four),
            (got_gu, *four),
            (far_gu, (2, q, BLOCK), lambda j: (0, 0, j)),
            (keep_b, *three),
            (got_b, *three),
            (far_b, (q, BLOCK), lambda j: (0, j)),
        ],
        [
            ((k, q, n), BF16, (k, q, BLOCK), lambda j: (0, 0, j))
            for k in ((3,) if merged else (2, 1))
        ],
    )


def split_slots(acc, rows, keep, sends):
    view = acc.reshape(4, 8, rows, acc.shape[-1])
    for s in range(4):
        keep[s] = view[:, 2 * s]
        sends[s][...] = view[:, 2 * s + 1].astype(BF16)


def summed(chain, quarters, at, weights, base, blocks, dims, prev, last, tile):
    count = len(weights)
    q, n = quarters[0].shape[-2:]
    rows = q // 8
    wide_block = min(2 * BLOCK, tile)

    def body(*refs):
        parts, w = refs[:4], refs[4 : 4 + count * blocks]
        rest = refs[4 + count * blocks :]
        scratch = rest[-1]
        if prev is not None:
            total, rest = rest[0][...], rest[1:]
        else:
            total = None

        @pl.when(pl.program_id(0) == 0)
        def _():
            for g in range(4):
                for k in range(count):
                    scratch[k, g * q : (g + 1) * q] = parts[g][k]

        for k in range(count):
            for i in range(blocks):
                left = scratch[k, :, i * BLOCK : (i + 1) * BLOCK]
                term = dot(left, w[k * blocks + i][...], dims)
                total = term if total is None else total + term
        if last:
            split_slots(total, rows, rest[0], rest[1:5])
        else:
            rest[0][...] = total

    ins = [(p, (count, q, n), lambda j: (at, 0, 0)) for p in quarters]
    for w in weights:
        for i in range(blocks):
            if dims is NN:
                ins.append((w, (BLOCK, wide_block), functools.partial(lambda i, j: (base + i, j), i)))
            else:
                ins.append((w, (wide_block, BLOCK), functools.partial(lambda i, j: (j, base + i), i)))
    whole = ((4 * q, tile), F32, (4 * q, wide_block), lambda j: (0, j))
    alias = {}
    if prev is not None:
        ins.append((prev, whole[2], whole[3]))
        if not last:
            alias = {len(ins) - 1: 0}
    if last:
        outs = [((4, 4, rows, tile), F32, (4, 4, rows, wide_block), lambda j: (0, 0, 0, j))]
        outs += [((4, rows, tile), BF16, (4, rows, wide_block), lambda j: (0, 0, j))] * 4
    else:
        outs = [whole]
    return chain(
        body,
        (tile // wide_block,),
        ins,
        outs,
        scratch=[pltpu.VMEM((count, 4 * q, n), BF16)],
        flops=2 * count * 4 * q * n * tile,
        alias=alias,
    )


def delta_gradients(chain, act_t, quarters, base, blocks, prev, hidden_units):
    tile, tokens = act_t.shape
    q, n = quarters[0].shape[-2:]

    def body(*refs):
        a, parts = refs[0], refs[1:5]
        outs = refs[-2:]
        for k in range(2):
            right = jnp.concatenate([p[k] for p in parts], axis=0)
            outs[k][...] = dot(a[...], right, NN).astype(BF16)

    ins = [(act_t, act_t.shape, lambda j: (0, 0))]
    ins += [(p, (2, q, BLOCK), lambda j: (0, 0, j)) for p in quarters]
    out = ((tile, hidden_units), BF16, (tile, BLOCK), lambda j: (0, base + j))
    return filled(chain, body, blocks, ins, [out, out], prev, 4 * tokens * tile * n)


def down_gradient_rows(chain, cot, quarters, at, base, blocks, prev, hidden_units):
    tokens, tile = cot.shape
    q, n = quarters[0].shape[-2:]

    def body(*refs):
        c, parts = refs[0], refs[1:5]
        left = jnp.concatenate([p[0] for p in parts], axis=0)
        refs[-1][...] = dot(left, c[...], TN).astype(BF16)

    ins = [(cot, cot.shape, lambda j: (0, 0))]
    ins += [(p, (1, q, BLOCK), lambda j: (at, 0, j)) for p in quarters]
    out = ((hidden_units, tile), BF16, (BLOCK, tile), lambda j: (base + j, 0))
    return filled(chain, body, blocks, ins, [out], prev, 2 * tokens * tile * n)


def filled(chain, body, blocks, ins, outs, prev, flops):
    lead = len(ins)
    if prev is None:
        return chain(body, (blocks,), ins, outs, flops=flops)

    def aliased(*refs):
        body(*refs[:lead], *refs[lead + len(prev) :])

    spot = ((16, 128), lambda j: (0, 0))
    return chain(
        aliased,
        (blocks,),
        ins + [(p, *spot) for p in prev],
        outs,
        flops=flops,
        alias={lead + i: i for i in range(len(prev))},
    )


def over_z(chain, keep, got):
    _, four, rows, tile = keep.shape
    block = min(tile, 512)

    def body(k, *refs):
        g, outs = refs[:4], refs[4:]
        for s in range(4):
            outs[s][...] = (k[s] + g[s][...].astype(F32)).astype(outs[s].dtype)

    one = ((four, rows, block), lambda j: (0, 0, j))
    return chain(
        body,
        (tile // block,),
        [(keep, (4, four, rows, block), lambda j: (0, 0, 0, j))] + [(x, *one) for x in got],
        [((four, rows, tile), F32 if s == 0 else BF16, *one) for s in range(4)],
    )


def finish_rows(chain, me, own, got):
    four, rows, tile = own.shape

    def body(s, o, *refs):
        total = o[...]
        for x in refs[:3]:
            total = total + x[...].astype(F32)
        refs[3][...] = total.astype(BF16)

    one = ((1, rows, tile), lambda g, s: (g, 0, 0))
    (out,) = chain(
        body,
        (4,),
        [(x, *one) for x in (own, *got)],
        [((four, rows, tile), BF16, (1, rows, tile), lambda g, s: (s[0] ^ g, 0, 0))],
        scalar=me,
    )
    return out.reshape(four * rows, tile)


def finish_groups(chain, own, got):
    four, rows, tile = own.shape
    block = min(tile, 512)

    def body(o, *refs):
        total = o[...]
        for x in refs[:3]:
            total = total + x[...].astype(F32)
        for g in range(4):
            refs[3 + g][...] = total[g].astype(BF16)

    one = ((four, rows, block), lambda j: (0, 0, j))
    return chain(
        body,
        (tile // block,),
        [(x, *one) for x in (own, *got)],
        [((rows, tile), BF16, (rows, block), lambda j: (0, j))] * 4,
    )


def place_columns(chain, me, groups):
    rows, tile = groups[0].shape

    def body(s, *refs):
        for g in range(4):

            @pl.when(pl.program_id(0) == g)
            def _():
                refs[4][...] = refs[g][...]

    (out,) = chain(
        body,
        (4,),
        [(x, (rows, tile), lambda g, s: (0, 0)) for x in groups],
        [((rows, 4 * tile), BF16, (rows, tile), lambda g, s: (0, s[0] ^ g))],
        scalar=me,
    )
    return out


def gather_wide(own):
    pieces = {0: own}
    pieces[1] = swap_wide(own, 1)
    for k in (2, 4, 6):
        pieces[k] = swap_wide(own, k)
    for k in (2, 4, 6):
        pieces[k + 1] = swap_wide(pieces[k], 1)
    return [pieces[k] for k in range(8)]


def spread(own):
    far = swap(own, 2)
    return [own, swap(own, 1), far, swap(far, 1)]


def chunk_sizes(total):
    count = min(4, total)
    return [total // count + (1 if i < total % count else 0) for i in range(count)]


def local_eight(activations, cotangent, gate_proj, up_proj, down_proj):
    me = lax.axis_index("narrow").astype(jnp.int32).reshape(1)
    rows = activations.shape[0]
    tile, units = gate_proj.shape
    sizes = chunk_sizes(units // BLOCK)
    count = len(sizes)
    bases = [sum(sizes[:c]) for c in range(count)]
    chunks = list(zip(bases, sizes))
    chain = Chain()

    cot_pieces = gather_wide(cotangent)
    tiles = lax.all_to_all(activations, "narrow", split_axis=1, concat_axis=0, tiled=True)
    act_pieces = gather_wide(tiles)

    keep_b, got_b, far_b = {}, {}, {}
    keep_gu, got_gu, far_gu = {}, {}, {}
    hid, delta, at = {}, {}, {}
    out = grad = down_grad = None
    gate_up_grads = None
    last = count - 1

    def back(c):
        keep_b[c], send = back_part(chain, cot, down_proj, *chunks[c])
        got_b[c] = swap(send, 1)

    def back_x(c):
        far_b[c] = swap(add_away(chain, keep_b[c], got_b[c]), 2)

    def gate_up(c):
        keep_gu[c], send = gate_up_part(chain, act, gate_proj, up_proj, *chunks[c])
        got_gu[c] = swap(send, 1)

    def gate_up_x(c):
        far_gu[c] = swap(add_away(chain, keep_gu[c], got_gu[c]), 2)

    def elementwise(c):
        merged = c < count - 2
        res = activate(
            chain, keep_gu[c], got_gu[c], far_gu[c], keep_b[c], got_b[c], far_b[c], merged
        )
        delta[c] = spread(res[0])
        hid[c], at[c] = (delta[c], 2) if merged else (spread(res[1]), 0)

    def add_out(c):
        nonlocal out
        res = summed(chain, hid[c], at[c], [down_proj], *chunks[c], NN, out, c == last, tile)
        out = res if c == last else res[0]

    def add_grad(c):
        nonlocal grad
        weights = [gate_proj, up_proj]
        res = summed(chain, delta[c], 0, weights, *chunks[c], NT, grad, c == last, tile)
        grad = res if c == last else res[0]

    def down_grads(c):
        nonlocal down_grad
        down_grad = down_gradient_rows(chain, cot, hid[c], at[c], *chunks[c], down_grad, units)

    def delta_grads(c):
        nonlocal gate_up_grads
        gate_up_grads = delta_gradients(chain, act_t, delta[c], *chunks[c], gate_up_grads, units)

    def over_y(sends):
        return [swap_wide(s, 1) for s in sends]

    def across_z(keep, got):
        own, *away = over_z(chain, keep, got)
        return own, [swap_wide(a, 2 * (i + 1)) for i, a in enumerate(away)]

    chain.after(tiles)
    cot = arrange(chain, me, cot_pieces, rows, tile)
    arrived = [act_pieces[k] for k in (2, 4, 1, 6, 3, 5, 7)]
    for c in range(count):
        chain.after(*arrived[:1])
        arrived = arrived[1:]
        back(c)
        if c > 0:
            chain.after(*arrived[:1])
            arrived = arrived[1:]
            if c > 2:
                chain.after(far_b[c - 3])
            back_x(c - 1)
    if count > 2:
        chain.after(far_b[count - 3])
    back_x(last)
    if last > 0:
        chain.after(far_b[last - 1])
    act = arrange(chain, me, act_pieces, rows, tile)
    chain.after(far_b[last])
    act_t = act.T
    for c in range(count):
        gate_up(c)
        if c >= 1:
            gate_up_x(c - 1)
        if c >= 2:
            elementwise(c - 2)
    gate_up_x(last)
    if last >= 1:
        elementwise(last - 1)
    todo = list(range(count))
    early = todo[: max(count - 2, 0)]
    late = todo[max(count - 2, 0) :]
    for i, c in enumerate(early):
        if i == len(early) - 1:
            elementwise(last)
        add_out(c)
        add_grad(c)
        if i == len(early) - 1:
            chain.after(hid[late[0]][2])
        down_grads(c)
        if i == len(early) - 1:
            chain.after(hid[last][2])
        delta_grads(c)
    if not early:
        elementwise(last)
    for c in late:
        if c == last:
            chain.after(delta[late[0]][2])
        add_out(c)
    out_keep, *out_sends = out
    out_got = over_y(out_sends)
    for c in late[:-1]:
        add_grad(c)
    down_grads(late[0])
    chain.after(delta[last][2])
    out_own, out_far = across_z(out_keep, out_got)
    add_grad(last)
    grad_keep, *grad_sends = grad
    grad_got = over_y(grad_sends)
    for c in late[1:]:
        down_grads(c)
    delta_grads(late[0])
    block_output = finish_rows(chain, me, out_own, out_far)
    for c in late[1:]:
        delta_grads(c)
    grad_own, grad_far = across_z(grad_keep, grad_got)
    groups = finish_groups(chain, grad_own, grad_far)
    groups = [groups[0]] + [swap(groups[g], g) for g in range(1, 4)]
    input_gradient = place_columns(chain, me, groups)
    return (block_output, input_gradient, *gate_up_grads, down_grad[0])


def scatter_sum(part):
    split = part.reshape(-1, 4, part.shape[0] // 4 // lax.axis_size("wide"), part.shape[-1])
    got = swap(jnp.stack([split[:, 1], split[:, 3]]), 1)
    away = (split[:, 2] + got[1]).astype(BF16)
    return (split[:, 0] + got[0]) + swap(away, 2).astype(F32)


def spread_rows(own):
    return jnp.stack(spread(own), axis=1).reshape(-1, own.shape[-1])


def local_any(activations, cotangent, gate_proj, up_proj, down_proj):
    me = lax.axis_index("narrow")
    rows = activations.shape[0]
    tile = gate_proj.shape[0]
    pieces = [lax.dynamic_slice_in_dim(activations, (me ^ g) * tile, tile, 1) for g in range(4)]
    pieces = [pieces[0]] + [swap(pieces[g], g) for g in range(1, 4)]
    cots = [lax.dynamic_slice_in_dim(cotangent, (me ^ g) * rows, rows, 0) for g in range(4)]

    def gathered(parts):
        return lax.all_gather(jnp.stack(parts), "wide", axis=0, tiled=True).reshape(-1, tile)

    features, upstream = gathered(pieces), gathered(cots)
    gate = scatter_sum(dot(features, gate_proj, NN))
    up = scatter_sum(dot(features, up_proj, NN))
    back = scatter_sum(dot(upstream, down_proj, NT))
    active, slope = silu_parts(gate)
    gate_delta = spread_rows((back * up * slope).astype(BF16))
    up_delta = spread_rows((back * active).astype(BF16))
    hidden = spread_rows((active * up).astype(BF16))

    def landed(total):
        got = lax.psum_scatter(total, "wide", scatter_dimension=0, tiled=True)
        return got.astype(BF16).reshape(4, rows, tile)

    grad = landed(dot(gate_delta, gate_proj, NT) + dot(up_delta, up_proj, NT))
    out = landed(dot(hidden, down_proj, NN))
    gate_gradient = dot(features, gate_delta, TN).astype(BF16)
    up_gradient = dot(features, up_delta, TN).astype(BF16)
    down_gradient = dot(hidden, upstream, TN).astype(BF16)

    block_output = jnp.concatenate(
        [lax.dynamic_index_in_dim(out, me ^ g, 0, keepdims=False) for g in range(4)]
    )
    grads = jnp.stack([grad[0]] + [swap(grad[g], g) for g in range(1, 4)])
    input_gradient = jnp.concatenate(
        [lax.dynamic_index_in_dim(grads, me ^ g, 0, keepdims=False) for g in range(4)], axis=1
    )
    return (block_output, input_gradient, gate_gradient, up_gradient, down_gradient)


def local(activations, cotangent, gate_proj, up_proj, down_proj):
    args = (activations, cotangent, gate_proj, up_proj, down_proj)
    rows, (tile, units) = activations.shape[0], gate_proj.shape
    fits = lax.axis_size("wide") == 8 and rows % 16 == 0
    if fits and tile % BLOCK == 0 and units % BLOCK == 0:
        return local_eight(*args)
    return local_any(*args)


def solution(mesh):
    placed = (
        P(("wide", "narrow"), None),
        P("wide", "narrow"),
        P("narrow", "wide"),
        P("narrow", "wide"),
        P("wide", "narrow"),
    )
    return jax.shard_map(
        local,
        mesh=mesh,
        in_specs=placed,
        out_specs=(
            P("wide", "narrow"),
            P(("wide", "narrow"), None),
            P("narrow", "wide"),
            P("narrow", "wide"),
            P("wide", "narrow"),
        ),
        check_vma=False,
    )
```

```python
import functools

import jax
import jax.numpy as jnp
from jax import lax
from jax.experimental import pallas as pl
from jax.experimental.pallas import tpu as pltpu
from jax.sharding import PartitionSpec as P

BF16, F32 = jnp.bfloat16, jnp.float32
BLOCK = 256
VMEM_LIMIT = 64 * 1024 * 1024 - 256 * 1024
NN = (((1,), (0,)), ((), ()))
NT = (((1,), (1,)), ((), ()))
TN = (((0,), (0,)), ((), ()))


def dot(left, right, dims):
    return lax.dot_general(left, right, dims, preferred_element_type=F32)


def silu_parts(gate):
    sigma = jax.nn.sigmoid(gate)
    return (gate * sigma, sigma * (1.0 + gate * (1.0 - sigma)))


def swap(value, mask):
    return lax.ppermute(value, "narrow", [(i, i ^ mask) for i in range(4)])


def swap_wide(value, mask):
    return lax.ppermute(value, "wide", [(i, i ^ mask) for i in range(8)])


class Chain:
    def __init__(self):
        self.token = None
        self.waits = []

    def after(self, *arrays):
        self.waits += arrays

    def __call__(self, body, grid, ins, outs, scratch=(), flops=0, alias=None, scalar=None):
        lead = 0 if scalar is None else 1
        arrays = [a for a, _, _ in ins]
        specs = [pl.BlockSpec(block, index) for _, block, index in ins]
        unread = self.waits + ([] if self.token is None else [self.token])
        self.waits = []
        arrays += unread
        specs += [pl.BlockSpec(memory_space=pltpu.HBM)] * len(unread)
        shapes = [jax.ShapeDtypeStruct(shape, dtype) for shape, dtype, _, _ in outs]
        out_specs = [pl.BlockSpec(block, index) for _, _, block, index in outs]
        shapes.append(jax.ShapeDtypeStruct((8, 128), F32))
        out_specs.append(pl.BlockSpec((8, 128), lambda *i: (0, 0)))
        n_in, n_out = len(ins), len(outs)

        def kernel(*refs):
            head, refs = refs[:lead], refs[lead:]
            in_refs = refs[:n_in]
            rest = refs[n_in + len(unread) :]
            out_refs, token, scratch_refs = rest[:n_out], rest[n_out], rest[n_out + 1 :]
            token[...] = jnp.zeros(token.shape, F32)
            body(*head, *in_refs, *out_refs, *scratch_refs)

        res = pl.pallas_call(
            kernel,
            grid_spec=pltpu.PrefetchScalarGridSpec(
                num_scalar_prefetch=lead,
                grid=grid,
                in_specs=specs,
                out_specs=out_specs,
                scratch_shapes=list(scratch),
            ),
            out_shape=shapes,
            input_output_aliases={k + lead: v for k, v in (alias or {}).items()},
            compiler_params=pltpu.CompilerParams(vmem_limit_bytes=VMEM_LIMIT),
            cost_estimate=pl.CostEstimate(flops=1, bytes_accessed=1, transcendentals=0),
        )(*(() if scalar is None else (scalar,)), *arrays)
        self.token = res[-1]
        return res[:-1]


def join(chain, parts):
    rows, tile = parts[0].shape
    count, step = len(parts), rows // 4

    def body(*refs):
        for i in range(count):
            refs[count][i] = refs[i][...]

    (out,) = chain(
        body,
        (4,),
        [(p, (step, tile), lambda j: (j, 0)) for p in parts],
        [((count, rows, tile), BF16, (count, step, tile), lambda j: (0, j, 0))],
    )
    return out


def arrange(chain, me, even, first, odd, rows, tile, turned=False):
    q = 8 * rows

    def body(_, *refs):
        out = refs[8]
        for k in range(8):
            out[0, k] = refs[k][...]
        if turned:
            refs[9][...] = out[0].reshape(q, tile).T

    slots = [(even[0], 0), (first, 0), (even[1], 0), odd[0]]
    slots += [(even[2], 0), odd[1], (even[3], 0), odd[2]]
    outs = [((4, 8, rows, tile), BF16, (1, 8, rows, tile), lambda g, s: (g, 0, 0, 0))]
    if turned:
        outs.append(((tile, 4 * q), BF16, (tile, q), lambda g, s: (0, g)))
    out, *rest = chain(
        body,
        (4,),
        [
            (p, (rows, tile), functools.partial(lambda at, g, s: (at + (s[0] ^ g), 0), at))
            for p, at in slots
        ],
        outs,
        scalar=me,
    )
    return [out.reshape(4 * q, tile), *rest]


def parted(acc, q, keep, send):
    for i in range(2):
        keep[i] = acc[2 * i * q : (2 * i + 1) * q]
        send[i] = acc[(2 * i + 1) * q : (2 * i + 2) * q]


def back_part(chain, cot, down, base, blocks):
    tokens, tile = cot.shape
    q, n = tokens // 4, blocks * BLOCK

    def body(c, w, keep, send):
        parted(dot(c[...], w[...], NT), q, keep, send)

    out = ((2, q, n), F32, (2, q, BLOCK), lambda j: (0, 0, j))
    return chain(
        body,
        (blocks,),
        [(cot, cot.shape, lambda j: (0, 0)), (down, (BLOCK, tile), lambda j: (base + j, 0))],
        [out, out],
        flops=2 * tokens * tile * n,
    )


def gate_up_part(chain, act, gate, up, base, blocks):
    tokens, tile = act.shape
    q, n = tokens // 4, blocks * BLOCK

    def body(a, wg, wu, keep, send):
        parted(dot(a[...], wg[...], NN), q, keep.at[:, 0], send.at[:, 0])
        parted(dot(a[...], wu[...], NN), q, keep.at[:, 1], send.at[:, 1])

    weight = ((tile, BLOCK), lambda j: (0, base + j))
    out = ((2, 2, q, n), F32, (2, 2, q, BLOCK), lambda j: (0, 0, 0, j))
    return chain(
        body,
        (blocks,),
        [(act, act.shape, lambda j: (0, 0)), (gate, *weight), (up, *weight)],
        [out, out],
        flops=4 * tokens * tile * n,
    )


def add_away(chain, keep, got):
    shape = keep.shape[1:]
    zeros = (0,) * (len(shape) - 1)
    block = (1, *shape[:-1], BLOCK)

    def body(a, b, out):
        out[...] = (a[0] + b[0]).astype(BF16)

    def at(j):
        return (1, *zeros, j)

    (out,) = chain(
        body,
        (shape[-1] // BLOCK,),
        [(keep, block, at), (got, block, at)],
        [(shape, BF16, block[1:], lambda j: (*zeros, j))],
    )
    return out


def activate(chain, keep_gu, got_gu, far_gu, keep_b, got_b, far_b, off):
    n, q = far_gu.shape[-1], far_gu.shape[1]

    def body(kg, gg, fg, kb, gb, fb, deltas, hidden):
        gate = kg[0, 0] + gg[0, 0] + fg[0].astype(F32)
        up = kg[0, 1] + gg[0, 1] + fg[1].astype(F32)
        back = kb[0] + gb[0] + fb[...].astype(F32)
        active, slope = silu_parts(gate)
        deltas[0] = (back * up * slope).astype(BF16)
        deltas[1] = (back * active).astype(BF16)
        hidden[0] = (active * up).astype(BF16)

    four = ((1, 2, q, BLOCK), lambda j: (0, 0, 0, j))
    three = ((1, q, BLOCK), lambda j: (0, 0, off + j))
    return chain(
        body,
        (n // BLOCK,),
        [
            (keep_gu, *four),
            (got_gu, *four),
            (far_gu, (2, q, BLOCK), lambda j: (0, 0, j)),
            (keep_b, *three),
            (got_b, *three),
            (far_b, (q, BLOCK), lambda j: (0, off + j)),
        ],
        [((k, q, n), BF16, (k, q, BLOCK), lambda j: (0, 0, j)) for k in (2, 1)],
    )


def split_slots(acc, rows, keep, send):
    view = acc.reshape(4, 8, rows, acc.shape[-1])
    for s in range(4):
        keep[s] = view[:, 2 * s]
        send[s] = view[:, 2 * s + 1].astype(BF16)


def summed(chain, terms, base, blocks, halves=1, half=0, split=False):
    kinds = sum(len(t[1]) for t in terms)
    q, n = terms[0][0][0].shape[1:]
    rows = q // 8
    first_weight, dims = terms[0][1][0], terms[0][2]
    tile = first_weight.shape[1 if dims is NN else 0]
    width = tile // halves
    step = min(2 * BLOCK, width)
    off = half * (width // step)
    ins, outs, alias, plan, moves = [], [], {}, [], []
    for quarters, weights, dims, prev in terms:
        refs, first = [], len(moves) // 4
        for k in range(len(weights)):
            moves += [(first + k, g, len(ins) + g, k) for g in range(4)]
        ins += [(p, p.shape, lambda j: (0, 0, 0)) for p in quarters]
        for w in weights:
            for i in range(blocks):
                refs.append(len(ins))
                if dims is NN:
                    index = functools.partial(lambda i, j: (base + i, off + j), i)
                    ins.append((w, (BLOCK, step), index))
                else:
                    index = functools.partial(lambda i, j: (off + j, base + i), i)
                    ins.append((w, (step, BLOCK), index))
        before = None
        if prev is not None:
            before = len(ins)
            ins.append((prev, (4 * q, step), lambda j: (0, off + j)))
            if not split:
                alias[before] = len(outs)
        plan.append((first, len(weights), dims, refs, before, len(outs)))
        if split:
            shape, block = (4, 4, rows, width), (4, 4, rows, step)
            outs.append((shape, F32, block, lambda j: (0, 0, 0, j)))
            outs.append((shape, BF16, block, lambda j: (0, 0, 0, j)))
        else:
            outs.append(((4 * q, tile), F32, (4 * q, step), lambda j: (0, j)))
    n_in = len(ins)

    def body(*refs):
        out_refs, scratch = refs[n_in:-1], refs[-1]

        @pl.when(pl.program_id(0) == 0)
        def _():
            for to, g, at, k in moves:
                scratch[to, g * q : (g + 1) * q] = refs[at][k]

        for first, count, dims, at, before, out in plan:
            total = None if before is None else refs[before][...]
            for k in range(count):
                for i in range(blocks):
                    left = scratch[first + k, :, i * BLOCK : (i + 1) * BLOCK]
                    term = dot(left, refs[at[k * blocks + i]][...], dims)
                    total = term if total is None else total + term
            if split:
                split_slots(total, rows, out_refs[out], out_refs[out + 1])
            else:
                out_refs[out][...] = total

    return chain(
        body,
        (width // step,),
        ins,
        outs,
        scratch=[pltpu.VMEM((kinds, 4 * q, n), BF16)],
        flops=2 * kinds * 4 * q * n * width,
        alias=alias,
    )


def gradients(chain, act_t, cot, hidden, deltas, base, blocks, prev, units):
    tile, tokens = act_t.shape
    q = deltas[0].shape[1]
    lead = 10

    def body(*refs):
        a, c, hid, dl = refs[0], refs[1], refs[2:6], refs[6:10]
        outs = refs[-3:]
        for k in range(2):
            right = jnp.concatenate([p[k] for p in dl], axis=0)
            outs[k][...] = dot(a[...], right, NN).astype(BF16)
        left = jnp.concatenate([p[0] for p in hid], axis=0)
        outs[2][...] = dot(left, c[...], TN).astype(BF16)

    ins = [(act_t, act_t.shape, lambda j: (0, 0)), (cot, cot.shape, lambda j: (0, 0))]
    ins += [(p, (1, q, BLOCK), lambda j: (0, 0, j)) for p in hidden]
    ins += [(p, (2, q, BLOCK), lambda j: (0, 0, j)) for p in deltas]
    column = ((tile, units), BF16, (tile, BLOCK), lambda j: (0, base + j))
    outs = [column, column, ((units, tile), BF16, (BLOCK, tile), lambda j: (base + j, 0))]
    alias = {}
    if prev is not None:
        ins += [(p, (16, 128), lambda j: (0, 0)) for p in prev]
        alias = {lead + i: i for i in range(3)}
    return chain(body, (blocks,), ins, outs, flops=6 * tokens * tile * blocks * BLOCK, alias=alias)


def over_z(chain, keep, got):
    _, four, rows, width = keep.shape
    step = min(width, 512)

    def body(k, g, *outs):
        for s in range(4):
            outs[s][...] = (k[s] + g[s].astype(F32)).astype(outs[s].dtype)

    four_slots = ((4, four, rows, step), lambda j: (0, 0, 0, j))
    one = ((four, rows, step), lambda j: (0, 0, j))
    return chain(
        body,
        (width // step,),
        [(keep, *four_slots), (got, *four_slots)],
        [((four, rows, width), F32 if s == 0 else BF16, *one) for s in range(4)],
    )


def finish(chain, me, halves, by_rows):
    four, rows, width = halves[0][0].shape
    tile = width * len(halves)

    def body(s, *refs):
        outs = refs[4 * len(halves) :]
        for h in range(len(halves)):
            total = refs[4 * h][...]
            for x in refs[4 * h + 1 : 4 * h + 4]:
                total = total + x[...].astype(F32)
            columns = slice(h * width, (h + 1) * width)
            for g in range(4):
                rounded = total[g].astype(BF16)
                if by_rows:
                    outs[0][s[0] ^ g, :, columns] = rounded
                else:
                    outs[g][:, columns] = rounded

    ins = []
    for own, got in halves:
        ins += [(x, (four, rows, width), lambda j, s: (0, 0, 0)) for x in (own, *got)]
    if by_rows:
        outs = [((four, rows, tile), BF16, (four, rows, tile), lambda j, s: (0, 0, 0))]
    else:
        outs = [((rows, tile), BF16, (rows, tile), lambda j, s: (0, 0))] * 4
    res = chain(body, (1,), ins, outs, scalar=me)
    return res[0].reshape(four * rows, tile) if by_rows else res


def place_columns(chain, me, groups):
    rows, tile = groups[0].shape

    def body(s, *refs):
        for g in range(4):

            @pl.when(pl.program_id(0) == g)
            def _():
                refs[4][...] = refs[g][...]

    (out,) = chain(
        body,
        (4,),
        [(x, (rows, tile), lambda g, s: (0, 0)) for x in groups],
        [((rows, 4 * tile), BF16, (rows, tile), lambda g, s: (0, s[0] ^ g))],
        scalar=me,
    )
    return out


def gather_z(own):
    return [own] + [swap_wide(own, k) for k in (2, 4, 6)]


def spread(own):
    far = swap(own, 2)
    return [own, swap(own, 1), far, swap(far, 1)]


def chunk_sizes(total):
    first = max(1, total // 6)
    rest = total - first
    return [first, (rest + 2) // 3, (rest + 1) // 3, rest // 3]


def local_eight(activations, cotangent, gate_proj, up_proj, down_proj):
    me = lax.axis_index("narrow").astype(jnp.int32).reshape(1)
    rows = activations.shape[0]
    tile, units = gate_proj.shape
    sizes = chunk_sizes(units // BLOCK)
    chunks = [(sum(sizes[:c]), sizes[c]) for c in range(4)]
    backs = [(0, sizes[0] + sizes[1]), chunks[2], chunks[3]]
    back_of = [(0, 0), (0, sizes[0]), (1, 0), (2, 0)]
    chain = Chain()

    keep_b, got_b, far_b = {}, {}, {}
    keep_gu, got_gu, far_gu = {}, {}, {}
    own, near, far, diag = {}, {}, {}, {}
    out = grad = grads = None

    def back(p):
        keep_b[p], send = back_part(chain, cot, down_proj, *backs[p])
        got_b[p] = swap(send, 1)

    def back_x(p):
        far_b[p] = swap(add_away(chain, keep_b[p], got_b[p]), 2)

    def gate_up(c):
        keep_gu[c], send = gate_up_part(chain, act, gate_proj, up_proj, *chunks[c])
        got_gu[c] = swap(send, 1)

    def gate_up_x(c):
        far_gu[c] = swap(add_away(chain, keep_gu[c], got_gu[c]), 2)

    def elementwise(c):
        p, off = back_of[c]
        res = activate(
            chain, keep_gu[c], got_gu[c], far_gu[c], keep_b[p], got_b[p], far_b[p], off
        )
        for kind, value in zip("dh", res):
            name = (kind, c)
            own[name], near[name], far[name] = value, swap(value, 1), swap(value, 2)
            diag[name] = swap(far[name], 1)

    def gathered(kind, c):
        return [x[kind, c] for x in (own, near, far, diag)]

    def out_term(c):
        return (gathered("h", c), [down_proj], NN, out)

    def grad_term(c):
        return (gathered("d", c), [gate_proj, up_proj], NT, grad)

    def add_both(c):
        nonlocal out, grad
        out, grad = summed(chain, [out_term(c), grad_term(c)], *chunks[c])

    def all_grads(c):
        nonlocal grads
        hid, delta = gathered("h", c), gathered("d", c)
        grads = gradients(chain, act_t, cot, hid, delta, *chunks[c], grads, units)

    def last_part(term, half):
        keep, send = summed(chain, [term], *chunks[3], 2, half, True)
        return keep, swap_wide(send, 1)

    def across_z(keep, got):
        mine, *away = over_z(chain, keep, got)
        return mine, [swap_wide(a, 2 * (i + 1)) for i, a in enumerate(away)]

    cot_even, cot_first = gather_z(cotangent), swap_wide(cotangent, 1)
    tiles = lax.all_to_all(activations, "narrow", split_axis=1, concat_axis=0, tiled=True)
    act_even, act_first = gather_z(tiles), swap_wide(tiles, 1)
    act_odd = [swap_wide(x, 1) for x in act_even[1:]]
    chain.after(tiles, cot_first, act_first)
    cot_odd = swap_wide(join(chain, cot_even[1:]), 1)
    cot_odd = [(cot_odd.reshape(12 * rows, tile), 4 * i) for i in range(3)]
    chain.after(*act_even[1:])
    (cot,) = arrange(chain, me, cot_even, cot_first, cot_odd, rows, tile)
    back(0)
    chain.after(act_odd[0], act_odd[1])
    back(1)
    chain.after(act_odd[2])
    back_x(0)
    act_odd = [(x, 0) for x in act_odd]
    act, act_t = arrange(chain, me, act_even, act_first, act_odd, rows, tile, True)
    gate_up(0)
    chain.after(far_b[0])
    back_x(1)
    back(2)
    chain.after(far_b[1])
    gate_up_x(0)
    gate_up(1)
    chain.after(far_gu[0])
    back_x(2)
    elementwise(0)
    gate_up(2)
    chain.after(far["d", 0], far["h", 0], near["d", 0], near["h", 0])
    gate_up_x(1)
    chain.after(diag["d", 0], diag["h", 0])
    gate_up(3)
    chain.after(far_gu[1], far_b[2])
    gate_up_x(2)
    elementwise(1)
    add_both(0)
    chain.after(far["d", 1], near["d", 1], near["h", 1])
    gate_up_x(3)
    all_grads(0)
    chain.after(far["h", 1], far_gu[2], diag["d", 1])
    elementwise(2)
    chain.after(diag["h", 1])
    add_both(1)
    chain.after(far_gu[3], far["h", 2], near["h", 2], near["d", 2])
    elementwise(3)
    chain.after(diag["h", 2])
    all_grads(1)
    chain.after(far["h", 3], far["d", 2], near["h", 3], near["d", 3])
    (out,) = summed(chain, [out_term(2)], *chunks[2])
    chain.after(diag["h", 3], diag["d", 2], far["d", 3])
    pieces = [last_part(out_term(3), 0)]
    chain.after(diag["d", 3])
    (grad,) = summed(chain, [grad_term(2)], *chunks[2])
    landed = [across_z(*pieces[0])]
    pieces.append(last_part(out_term(3), 1))
    pieces.append(last_part(grad_term(3), 0))
    chain.after(*landed[-1][1])
    landed.append(across_z(*pieces[1]))
    pieces.append(last_part(grad_term(3), 1))
    chain.after(*landed[-1][1])
    landed.append(across_z(*pieces[2]))
    all_grads(2)
    chain.after(*landed[-1][1])
    landed.append(across_z(*pieces[3]))
    all_grads(3)
    chain.after(*landed[-1][1])
    block_output = finish(chain, me, landed[:2], True)
    groups = finish(chain, me, landed[2:], False)
    groups = [groups[0]] + [swap(groups[g], g) for g in range(1, 4)]
    input_gradient = place_columns(chain, me, groups)
    return (block_output, input_gradient, *grads)


def scatter_sum(part):
    split = part.reshape(-1, 4, part.shape[0] // 4 // lax.axis_size("wide"), part.shape[-1])
    got = swap(jnp.stack([split[:, 1], split[:, 3]]), 1)
    away = (split[:, 2] + got[1]).astype(BF16)
    return (split[:, 0] + got[0]) + swap(away, 2).astype(F32)


def spread_rows(own):
    return jnp.stack(spread(own), axis=1).reshape(-1, own.shape[-1])


def local_any(activations, cotangent, gate_proj, up_proj, down_proj):
    me = lax.axis_index("narrow")
    rows = activations.shape[0]
    tile = gate_proj.shape[0]
    pieces = [lax.dynamic_slice_in_dim(activations, (me ^ g) * tile, tile, 1) for g in range(4)]
    pieces = [pieces[0]] + [swap(pieces[g], g) for g in range(1, 4)]
    cots = [lax.dynamic_slice_in_dim(cotangent, (me ^ g) * rows, rows, 0) for g in range(4)]

    def gathered(parts):
        return lax.all_gather(jnp.stack(parts), "wide", axis=0, tiled=True).reshape(-1, tile)

    features, upstream = gathered(pieces), gathered(cots)
    gate = scatter_sum(dot(features, gate_proj, NN))
    up = scatter_sum(dot(features, up_proj, NN))
    back = scatter_sum(dot(upstream, down_proj, NT))
    active, slope = silu_parts(gate)
    gate_delta = spread_rows((back * up * slope).astype(BF16))
    up_delta = spread_rows((back * active).astype(BF16))
    hidden = spread_rows((active * up).astype(BF16))

    def landed(total):
        got = lax.psum_scatter(total, "wide", scatter_dimension=0, tiled=True)
        return got.astype(BF16).reshape(4, rows, tile)

    grad = landed(dot(gate_delta, gate_proj, NT) + dot(up_delta, up_proj, NT))
    out = landed(dot(hidden, down_proj, NN))
    gate_gradient = dot(features, gate_delta, TN).astype(BF16)
    up_gradient = dot(features, up_delta, TN).astype(BF16)
    down_gradient = dot(hidden, upstream, TN).astype(BF16)

    block_output = jnp.concatenate(
        [lax.dynamic_index_in_dim(out, me ^ g, 0, keepdims=False) for g in range(4)]
    )
    grads = jnp.stack([grad[0]] + [swap(grad[g], g) for g in range(1, 4)])
    input_gradient = jnp.concatenate(
        [lax.dynamic_index_in_dim(grads, me ^ g, 0, keepdims=False) for g in range(4)], axis=1
    )
    return (block_output, input_gradient, gate_gradient, up_gradient, down_gradient)


def local(activations, cotangent, gate_proj, up_proj, down_proj):
    args = (activations, cotangent, gate_proj, up_proj, down_proj)
    rows, (tile, units) = activations.shape[0], gate_proj.shape
    fits = lax.axis_size("wide") == 8 and rows % 16 == 0
    if fits and tile % (2 * BLOCK) == 0 and units % BLOCK == 0 and units >= 6 * BLOCK:
        return local_eight(*args)
    return local_any(*args)


def solution(mesh):
    placed = (
        P(("wide", "narrow"), None),
        P("wide", "narrow"),
        P("narrow", "wide"),
        P("narrow", "wide"),
        P("wide", "narrow"),
    )
    return jax.shard_map(
        local,
        mesh=mesh,
        in_specs=placed,
        out_specs=(
            P("wide", "narrow"),
            P(("wide", "narrow"), None),
            P("narrow", "wide"),
            P("narrow", "wide"),
            P("wide", "narrow"),
        ),
        check_vma=False,
    )
```

```python
import functools

import jax
import jax.numpy as jnp
from jax import lax
from jax.experimental import pallas as pl
from jax.experimental.pallas import tpu as pltpu
from jax.sharding import PartitionSpec as P

BF16, F32 = jnp.bfloat16, jnp.float32
BLOCK = 256
VMEM_LIMIT = 64 * 1024 * 1024 - 256 * 1024
ORDER = (0, 2, 1, 3)
NN = (((1,), (0,)), ((), ()))
NT = (((1,), (1,)), ((), ()))
TN = (((0,), (0,)), ((), ()))


def dot(left, right, dims):
    return lax.dot_general(left, right, dims, preferred_element_type=F32)


def silu_parts(gate):
    sigma = jax.nn.sigmoid(gate)
    return (gate * sigma, sigma * (1.0 + gate * (1.0 - sigma)))


def swap(value, mask):
    return lax.ppermute(value, "narrow", [(i, i ^ mask) for i in range(4)])


def swap_wide(value, mask):
    return lax.ppermute(value, "wide", [(i, i ^ mask) for i in range(8)])


class Chain:
    def __init__(self):
        self.token = None
        self.waits = []

    def after(self, *arrays):
        self.waits += arrays

    def __call__(self, body, grid, ins, outs, scratch=(), flops=0, alias=None, scalar=None):
        lead = 0 if scalar is None else 1
        arrays = [a for a, _, _ in ins]
        specs = [pl.BlockSpec(block, index) for _, block, index in ins]
        unread = self.waits + ([] if self.token is None else [self.token])
        self.waits = []
        arrays += unread
        specs += [pl.BlockSpec(memory_space=pltpu.HBM)] * len(unread)
        shapes = [jax.ShapeDtypeStruct(shape, dtype) for shape, dtype, _, _ in outs]
        out_specs = [pl.BlockSpec(block, index) for _, _, block, index in outs]
        shapes.append(jax.ShapeDtypeStruct((8, 128), F32))
        out_specs.append(pl.BlockSpec((8, 128), lambda *i: (0, 0)))
        n_in, n_out = len(ins), len(outs)

        def kernel(*refs):
            head, refs = refs[:lead], refs[lead:]
            in_refs = refs[:n_in]
            rest = refs[n_in + len(unread) :]
            out_refs, token, scratch_refs = rest[:n_out], rest[n_out], rest[n_out + 1 :]
            token[...] = jnp.zeros(token.shape, F32)
            body(*head, *in_refs, *out_refs, *scratch_refs)

        res = pl.pallas_call(
            kernel,
            grid_spec=pltpu.PrefetchScalarGridSpec(
                num_scalar_prefetch=lead,
                grid=grid,
                in_specs=specs,
                out_specs=out_specs,
                scratch_shapes=list(scratch),
            ),
            out_shape=shapes,
            input_output_aliases={k + lead: v for k, v in (alias or {}).items()},
            compiler_params=pltpu.CompilerParams(vmem_limit_bytes=VMEM_LIMIT),
            cost_estimate=pl.CostEstimate(flops=1, bytes_accessed=1, transcendentals=0),
        )(*(() if scalar is None else (scalar,)), *arrays)
        self.token = res[-1]
        return res[:-1]


def group(i):
    return (i & 1) * 2 + (i >> 1)


def join(chain, parts):
    rows, tile = parts[0].shape
    count, step = len(parts), rows // 4

    def body(*refs):
        for i in range(count):
            refs[count][i] = refs[i][...]

    (out,) = chain(
        body,
        (4,),
        [(p, (step, tile), lambda j: (j, 0)) for p in parts],
        [((count, rows, tile), BF16, (count, step, tile), lambda j: (0, j, 0))],
    )
    return out


def arrange(chain, me, even, first, odd, rows, tile, turned=False):
    q = 8 * rows

    def body(_, *refs):
        out = refs[8]
        for k in range(8):
            out[0, k] = refs[k][...]
        if turned:
            refs[9][...] = out[0].reshape(q, tile).T

    slots = [(even[0], 0), (first, 0), (even[1], 0), odd[0]]
    slots += [(even[2], 0), odd[1], (even[3], 0), odd[2]]
    outs = [((4, 8, rows, tile), BF16, (1, 8, rows, tile), lambda g, s: (g, 0, 0, 0))]
    if turned:
        outs.append(((tile, 4 * q), BF16, (tile, q), lambda g, s: (0, g)))
    out, *rest = chain(
        body,
        (4,),
        [
            (p, (rows, tile), functools.partial(lambda at, i, s: (at + (s[0] ^ group(i)), 0), at))
            for p, at in slots
        ],
        outs,
        scalar=me,
    )
    return [out.reshape(4 * q, tile), *rest]


def back_part(chain, cot, down, base, blocks):
    tokens, tile = cot.shape
    half, n = tokens // 2, blocks * BLOCK

    def body(c, w, keep, send):
        acc = dot(c[...], w[...], NT)
        keep[...] = acc[:half]
        send[...] = acc[half:].astype(BF16)

    block, at = (half, BLOCK), lambda j: (0, j)
    outs = [((half, n), dtype, block, at) for dtype in (F32, BF16)]
    return chain(
        body,
        (blocks,),
        [(cot, cot.shape, lambda j: (0, 0)), (down, (BLOCK, tile), lambda j: (base + j, 0))],
        outs,
        flops=2 * tokens * tile * n,
    )


def gate_up_part(chain, act, gate, up, base, blocks):
    tokens, tile = act.shape
    half, n = tokens // 2, blocks * BLOCK

    def body(a, wg, wu, keep, send):
        for k, w in enumerate((wg, wu)):
            acc = dot(a[...], w[...], NN)
            keep[k] = acc[:half]
            send[k] = acc[half:].astype(BF16)

    weight = ((tile, BLOCK), lambda j: (0, base + j))
    block, at = (2, half, BLOCK), lambda j: (0, 0, j)
    outs = [((2, half, n), dtype, block, at) for dtype in (F32, BF16)]
    return chain(
        body,
        (blocks,),
        [(act, act.shape, lambda j: (0, 0)), (gate, *weight), (up, *weight)],
        outs,
        flops=4 * tokens * tile * n,
    )


def add_away(chain, keep, got):
    lead, (half, n) = keep.shape[:-2], keep.shape[-2:]
    zeros = (0,) * len(lead)
    block = (*lead, half // 2, n)

    def body(a, b, out):
        out[...] = (a[...] + b[...].astype(F32)).astype(BF16)

    (out,) = chain(
        body,
        (2,),
        [(x, block, lambda i: (*zeros, 1 - i, 0)) for x in (keep, got)],
        [(keep.shape, BF16, block, lambda i: (*zeros, i, 0))],
    )
    return out


def activate(chain, keep_gu, got_gu, far_gu, keep_b, got_b, far_b, off, blocks):
    half, n = far_gu.shape[1:]
    q = half // 2

    def body(kg, gg, fg, kb, gb, fb, out):
        gate = kg[0] + gg[0].astype(F32) + fg[0].astype(F32)
        up = kg[1] + gg[1].astype(F32) + fg[1].astype(F32)
        back = kb[...] + gb[...].astype(F32) + fb[...].astype(F32)
        active, slope = silu_parts(gate)
        out[0] = (back * up * slope).astype(BF16)
        out[1] = (back * active).astype(BF16)
        out[2] = (active * up).astype(BF16)

    two = ((2, half, BLOCK), lambda j: (0, 0, j))
    one = ((half, BLOCK), lambda j: (0, off + j))
    (out,) = chain(
        body,
        (n // BLOCK,),
        [(x, *two) for x in (keep_gu, got_gu, far_gu)] + [(x, *one) for x in (keep_b, got_b, far_b)],
        [((3, half, n), BF16, (3, half, BLOCK), lambda j: (0, 0, j))],
    )
    return out


def split_slots(acc, rows, keep, send):
    view = acc.reshape(4, 8, rows, acc.shape[-1])
    for s in range(4):
        keep[s] = view[:, 2 * s]
        send[s] = view[:, 2 * s + 1].astype(BF16)


def summed(chain, parts, terms, base, blocks, halves=1, half=0, split=False):
    kinds = parts[0].shape[0]
    half_rows, n = parts[0].shape[1:]
    q = half_rows // 2
    rows = q // 8
    first_weight, dims = terms[0][1][0], terms[0][2]
    tile = first_weight.shape[1 if dims is NN else 0]
    width = tile // halves
    step = min(2 * BLOCK, width)
    off = half * (width // step)
    ins = [(p, p.shape, lambda j: (0, 0, 0)) for p in parts]
    outs, alias, plan = [], {}, []
    for first, weights, dims, prev in terms:
        refs = []
        for w in weights:
            for i in range(blocks):
                refs.append(len(ins))
                if dims is NN:
                    index = functools.partial(lambda i, j: (base + i, off + j), i)
                    ins.append((w, (BLOCK, step), index))
                else:
                    index = functools.partial(lambda i, j: (off + j, base + i), i)
                    ins.append((w, (step, BLOCK), index))
        before = None
        if prev is not None:
            before = len(ins)
            ins.append((prev, (4 * q, step), lambda j: (0, off + j)))
            if not split:
                alias[before] = len(outs)
        plan.append((first, len(weights), dims, refs, before, len(outs)))
        if split:
            shape, block = (4, 4, rows, width), (4, 4, rows, step)
            outs.append((shape, F32, block, lambda j: (0, 0, 0, j)))
            outs.append((shape, BF16, block, lambda j: (0, 0, 0, j)))
        else:
            outs.append(((4 * q, tile), F32, (4 * q, step), lambda j: (0, j)))
    n_in = len(ins)

    def body(*refs):
        out_refs, scratch = refs[n_in:-1], refs[-1]

        @pl.when(pl.program_id(0) == 0)
        def _():
            for g in range(2):
                for k in range(kinds):
                    scratch[k, g * half_rows : (g + 1) * half_rows] = refs[g][k]

        for first, count, dims, at, before, out in plan:
            total = None if before is None else refs[before][...]
            for k in range(count):
                for i in range(blocks):
                    left = scratch[first + k, :, i * BLOCK : (i + 1) * BLOCK]
                    term = dot(left, refs[at[k * blocks + i]][...], dims)
                    total = term if total is None else total + term
            if split:
                split_slots(total, rows, out_refs[out], out_refs[out + 1])
            else:
                out_refs[out][...] = total

    return chain(
        body,
        (width // step,),
        ins,
        outs,
        scratch=[pltpu.VMEM((kinds, 4 * q, n), BF16)],
        flops=6 * 4 * q * n * width,
        alias=alias,
    )


def gradients(chain, act_t, cot, parts, base, blocks, prev, units):
    tile, tokens = act_t.shape
    half = tokens // 2
    lead = 4

    def body(*refs):
        a, c, own, near = refs[:lead]
        outs = refs[-3:]
        for k in range(2):
            right = jnp.concatenate([own[k], near[k]], axis=0)
            outs[k][...] = dot(a[...], right, NN).astype(BF16)
        left = jnp.concatenate([own[2], near[2]], axis=0)
        outs[2][...] = dot(left, c[...], TN).astype(BF16)

    ins = [(act_t, act_t.shape, lambda j: (0, 0)), (cot, cot.shape, lambda j: (0, 0))]
    ins += [(p, (3, half, BLOCK), lambda j: (0, 0, j)) for p in parts]
    column = ((tile, units), BF16, (tile, BLOCK), lambda j: (0, base + j))
    outs = [column, column, ((units, tile), BF16, (BLOCK, tile), lambda j: (base + j, 0))]
    alias = {}
    if prev is not None:
        ins += [(p, (16, 128), lambda j: (0, 0)) for p in prev]
        alias = {lead + i: i for i in range(3)}
    return chain(body, (blocks,), ins, outs, flops=6 * tokens * tile * blocks * BLOCK, alias=alias)


def over_z(chain, keep, got):
    _, four, rows, width = keep.shape
    step = min(width, 512)

    def body(k, g, *outs):
        for s in range(4):
            outs[s][...] = (k[s] + g[s].astype(F32)).astype(outs[s].dtype)

    four_slots = ((4, four, rows, step), lambda j: (0, 0, 0, j))
    one = ((four, rows, step), lambda j: (0, 0, j))
    return chain(
        body,
        (width // step,),
        [(keep, *four_slots), (got, *four_slots)],
        [((four, rows, width), F32 if s == 0 else BF16, *one) for s in range(4)],
    )


def finish(chain, me, halves, by_rows):
    four, rows, width = halves[0][0].shape
    tile = width * len(halves)

    def body(s, *refs):
        outs = refs[4 * len(halves) :]
        for h in range(len(halves)):
            total = refs[4 * h][...]
            for x in refs[4 * h + 1 : 4 * h + 4]:
                total = total + x[...].astype(F32)
            columns = slice(h * width, (h + 1) * width)
            for i, g in enumerate(ORDER):
                rounded = total[i].astype(BF16)
                if by_rows:
                    outs[0][s[0] ^ g, :, columns] = rounded
                else:
                    outs[g][:, columns] = rounded

    ins = []
    for own, got in halves:
        ins += [(x, (four, rows, width), lambda j, s: (0, 0, 0)) for x in (own, *got)]
    if by_rows:
        outs = [((four, rows, tile), BF16, (four, rows, tile), lambda j, s: (0, 0, 0))]
    else:
        outs = [((rows, tile), BF16, (rows, tile), lambda j, s: (0, 0))] * 4
    res = chain(body, (1,), ins, outs, scalar=me)
    return res[0].reshape(four * rows, tile) if by_rows else res


def place_columns(chain, me, groups):
    rows, tile = groups[0].shape

    def body(s, *refs):
        for g in range(4):

            @pl.when(pl.program_id(0) == g)
            def _():
                refs[4][...] = refs[g][...]

    (out,) = chain(
        body,
        (4,),
        [(x, (rows, tile), lambda g, s: (0, 0)) for x in groups],
        [((rows, 4 * tile), BF16, (rows, tile), lambda g, s: (0, s[0] ^ g))],
        scalar=me,
    )
    return out


def gather_z(own):
    return [own] + [swap_wide(own, k) for k in (2, 4, 6)]


def spread(own):
    far = swap(own, 2)
    return [own, swap(own, 1), far, swap(far, 1)]


def chunk_sizes(total):
    first = max(1, total // 6)
    rest = total - first
    return [first, (rest + 2) // 3, (rest + 1) // 3, rest // 3]


def local_eight(activations, cotangent, gate_proj, up_proj, down_proj):
    me = lax.axis_index("narrow").astype(jnp.int32).reshape(1)
    rows = activations.shape[0]
    tile, units = gate_proj.shape
    sizes = chunk_sizes(units // BLOCK)
    chunks = [(sum(sizes[:c]), sizes[c]) for c in range(4)]
    backs = [(0, chunks[2][0]), (chunks[2][0], sizes[2] + sizes[3])]
    back_of = [(0, 0), (0, sizes[0]), (1, 0), (1, sizes[2])]
    chain = Chain()

    keep_b, got_b, far_b = {}, {}, {}
    keep_gu, got_gu, far_gu = {}, {}, {}
    own, near = {}, {}
    out = grad = grads = None

    def back(p):
        keep_b[p], send = back_part(chain, cot, down_proj, *backs[p])
        got_b[p] = swap(send, 1)

    def back_x(p):
        far_b[p] = swap(add_away(chain, keep_b[p], got_b[p]), 2)

    def gate_up(c):
        keep_gu[c], send = gate_up_part(chain, act, gate_proj, up_proj, *chunks[c])
        got_gu[c] = swap(send, 1)

    def gate_up_x(c):
        far_gu[c] = swap(add_away(chain, keep_gu[c], got_gu[c]), 2)

    def elementwise(c):
        p, off = back_of[c]
        own[c] = activate(
            chain, keep_gu[c], got_gu[c], far_gu[c], keep_b[p], got_b[p], far_b[p], off, sizes[c]
        )
        near[c] = swap(own[c], 1)

    def out_term():
        return (2, [down_proj], NN, out)

    def grad_term():
        return (0, [gate_proj, up_proj], NT, grad)

    def add_both(c):
        nonlocal out, grad
        out, grad = summed(chain, (own[c], near[c]), [out_term(), grad_term()], *chunks[c])

    def all_grads(c):
        nonlocal grads
        grads = gradients(chain, act_t, cot, (own[c], near[c]), *chunks[c], grads, units)

    def last_part(term, half):
        keep, send = summed(chain, (own[3], near[3]), [term], *chunks[3], 2, half, True)
        return keep, swap_wide(send, 1)

    def across_z(keep, got):
        mine, *away = over_z(chain, keep, got)
        return mine, [swap_wide(a, 2 * (i + 1)) for i, a in enumerate(away)]

    cot_even, cot_first = gather_z(cotangent), swap_wide(cotangent, 1)
    tiles = lax.all_to_all(activations, "narrow", split_axis=1, concat_axis=0, tiled=True)
    act_even, act_first = gather_z(tiles), swap_wide(tiles, 1)
    act_odd = [swap_wide(x, 1) for x in act_even[1:]]
    chain.after(tiles, cot_first, act_first)
    cot_odd = swap_wide(join(chain, cot_even[1:]), 1)
    cot_odd = [(cot_odd.reshape(12 * rows, tile), 4 * i) for i in range(3)]
    chain.after(*act_even[1:])
    (cot,) = arrange(chain, me, cot_even, cot_first, cot_odd, rows, tile)
    back(0)
    chain.after(act_odd[0])
    back(1)
    chain.after(act_odd[1], act_odd[2])
    act_odd = [(x, 0) for x in act_odd]
    act, act_t = arrange(chain, me, act_even, act_first, act_odd, rows, tile, True)
    gate_up(0)
    back_x(0)
    gate_up(1)
    chain.after(far_b[0])
    back_x(1)
    gate_up_x(0)
    gate_up(2)
    chain.after(far_b[1])
    gate_up_x(1)
    elementwise(0)
    gate_up(3)
    gate_up_x(2)
    chain.after(near[0])
    elementwise(1)
    add_both(0)
    gate_up_x(3)
    chain.after(near[1])
    all_grads(0)
    elementwise(2)
    add_both(1)
    chain.after(far_gu[3], near[2])
    elementwise(3)
    all_grads(1)
    chain.after(near[3])
    pieces = []
    add_both(2)
    pieces.append(last_part(out_term(), 0))
    pieces.append(last_part(out_term(), 1))
    pieces.append(last_part(grad_term(), 0))
    pieces.append(last_part(grad_term(), 1))
    landed = [across_z(*pieces[0])]
    all_grads(2)
    chain.after(*landed[-1][1])
    landed.append(across_z(*pieces[1]))
    all_grads(3)
    chain.after(*landed[-1][1])
    landed.append(across_z(*pieces[2]))
    landed.append(across_z(*pieces[3]))
    block_output = finish(chain, me, landed[:2], True)
    groups = finish(chain, me, landed[2:], False)
    groups = [groups[0]] + [swap(groups[g], g) for g in range(1, 4)]
    input_gradient = place_columns(chain, me, groups)
    return (block_output, input_gradient, *grads)


def scatter_sum(part):
    split = part.reshape(-1, 4, part.shape[0] // 4 // lax.axis_size("wide"), part.shape[-1])
    got = swap(jnp.stack([split[:, 1], split[:, 3]]), 1)
    away = (split[:, 2] + got[1]).astype(BF16)
    return (split[:, 0] + got[0]) + swap(away, 2).astype(F32)


def spread_rows(own):
    return jnp.stack(spread(own), axis=1).reshape(-1, own.shape[-1])


def local_any(activations, cotangent, gate_proj, up_proj, down_proj):
    me = lax.axis_index("narrow")
    rows = activations.shape[0]
    tile = gate_proj.shape[0]
    pieces = [lax.dynamic_slice_in_dim(activations, (me ^ g) * tile, tile, 1) for g in range(4)]
    pieces = [pieces[0]] + [swap(pieces[g], g) for g in range(1, 4)]
    cots = [lax.dynamic_slice_in_dim(cotangent, (me ^ g) * rows, rows, 0) for g in range(4)]

    def gathered(parts):
        return lax.all_gather(jnp.stack(parts), "wide", axis=0, tiled=True).reshape(-1, tile)

    features, upstream = gathered(pieces), gathered(cots)
    gate = scatter_sum(dot(features, gate_proj, NN))
    up = scatter_sum(dot(features, up_proj, NN))
    back = scatter_sum(dot(upstream, down_proj, NT))
    active, slope = silu_parts(gate)
    gate_delta = spread_rows((back * up * slope).astype(BF16))
    up_delta = spread_rows((back * active).astype(BF16))
    hidden = spread_rows((active * up).astype(BF16))

    def landed(total):
        got = lax.psum_scatter(total, "wide", scatter_dimension=0, tiled=True)
        return got.astype(BF16).reshape(4, rows, tile)

    grad = landed(dot(gate_delta, gate_proj, NT) + dot(up_delta, up_proj, NT))
    out = landed(dot(hidden, down_proj, NN))
    gate_gradient = dot(features, gate_delta, TN).astype(BF16)
    up_gradient = dot(features, up_delta, TN).astype(BF16)
    down_gradient = dot(hidden, upstream, TN).astype(BF16)

    block_output = jnp.concatenate(
        [lax.dynamic_index_in_dim(out, me ^ g, 0, keepdims=False) for g in range(4)]
    )
    grads = jnp.stack([grad[0]] + [swap(grad[g], g) for g in range(1, 4)])
    input_gradient = jnp.concatenate(
        [lax.dynamic_index_in_dim(grads, me ^ g, 0, keepdims=False) for g in range(4)], axis=1
    )
    return (block_output, input_gradient, gate_gradient, up_gradient, down_gradient)


def local(activations, cotangent, gate_proj, up_proj, down_proj):
    args = (activations, cotangent, gate_proj, up_proj, down_proj)
    rows, (tile, units) = activations.shape[0], gate_proj.shape
    fits = lax.axis_size("wide") == 8 and rows % 16 == 0
    if fits and tile % (2 * BLOCK) == 0 and units % BLOCK == 0 and units >= 6 * BLOCK:
        return local_eight(*args)
    return local_any(*args)


def solution(mesh):
    placed = (
        P(("wide", "narrow"), None),
        P("wide", "narrow"),
        P("narrow", "wide"),
        P("narrow", "wide"),
        P("wide", "narrow"),
    )
    return jax.shard_map(
        local,
        mesh=mesh,
        in_specs=placed,
        out_specs=(
            P("wide", "narrow"),
            P(("wide", "narrow"), None),
            P("narrow", "wide"),
            P("narrow", "wide"),
            P("wide", "narrow"),
        ),
        check_vma=False,
    )
```

```python
import functools

import jax
import jax.numpy as jnp
from jax import lax
from jax.experimental import pallas as pl
from jax.experimental.pallas import tpu as pltpu
from jax.sharding import PartitionSpec as P

BF16, F32 = jnp.bfloat16, jnp.float32
BLOCK = 256
VMEM_LIMIT = 64 * 1024 * 1024 - 256 * 1024
ORDER = (0, 2, 1, 3)
NN = (((1,), (0,)), ((), ()))
NT = (((1,), (1,)), ((), ()))
TN = (((0,), (0,)), ((), ()))


def dot(left, right, dims):
    return lax.dot_general(left, right, dims, preferred_element_type=F32)


def silu_parts(gate):
    sigma = jax.nn.sigmoid(gate)
    return (gate * sigma, sigma * (1.0 + gate * (1.0 - sigma)))


def swap(value, mask):
    return lax.ppermute(value, "narrow", [(i, i ^ mask) for i in range(4)])


def swap_wide(value, mask):
    return lax.ppermute(value, "wide", [(i, i ^ mask) for i in range(8)])


class Chain:
    def __init__(self):
        self.token = None
        self.waits = []

    def after(self, *arrays):
        self.waits += arrays

    def __call__(self, body, grid, ins, outs, scratch=(), flops=0, alias=None, scalar=None):
        lead = 0 if scalar is None else 1
        arrays = [a for a, _, _ in ins]
        specs = [pl.BlockSpec(block, index) for _, block, index in ins]
        unread = self.waits + ([] if self.token is None else [self.token])
        self.waits = []
        arrays += unread
        specs += [pl.BlockSpec(memory_space=pltpu.HBM)] * len(unread)
        shapes = [jax.ShapeDtypeStruct(shape, dtype) for shape, dtype, _, _ in outs]
        out_specs = [pl.BlockSpec(block, index) for _, _, block, index in outs]
        shapes.append(jax.ShapeDtypeStruct((8, 128), F32))
        out_specs.append(pl.BlockSpec((8, 128), lambda *i: (0, 0)))
        n_in, n_out = len(ins), len(outs)

        def kernel(*refs):
            head, refs = refs[:lead], refs[lead:]
            in_refs = refs[:n_in]
            rest = refs[n_in + len(unread) :]
            out_refs, token, scratch_refs = rest[:n_out], rest[n_out], rest[n_out + 1 :]
            token[...] = jnp.zeros(token.shape, F32)
            body(*head, *in_refs, *out_refs, *scratch_refs)

        res = pl.pallas_call(
            kernel,
            grid_spec=pltpu.PrefetchScalarGridSpec(
                num_scalar_prefetch=lead,
                grid=grid,
                in_specs=specs,
                out_specs=out_specs,
                scratch_shapes=list(scratch),
            ),
            out_shape=shapes,
            input_output_aliases={k + lead: v for k, v in (alias or {}).items()},
            compiler_params=pltpu.CompilerParams(vmem_limit_bytes=VMEM_LIMIT),
            cost_estimate=pl.CostEstimate(flops=1, bytes_accessed=1, transcendentals=0),
        )(*(() if scalar is None else (scalar,)), *arrays)
        self.token = res[-1]
        return res[:-1]


def group(i):
    return (i & 1) * 2 + (i >> 1)


def arrange(chain, place, slots, rows, tile, turned=False):
    q = 8 * rows

    def body(_, *refs):
        out = refs[8]
        for k in range(8):
            out[0, k] = refs[k][...]
        if turned:
            refs[9][...] = out[0].reshape(q, tile).T

    outs = [((4, 8, rows, tile), BF16, (1, 8, rows, tile), lambda g, s: (g, 0, 0, 0))]
    if turned:
        outs.append(((tile, 4 * q), BF16, (tile, q), lambda g, s: (0, g)))
    out, *rest = chain(
        body,
        (4,),
        [
            (p, (rows, tile), functools.partial(lambda at, i, s: (at(s) + (s[0] ^ group(i)), 0), at))
            for p, at in slots
        ],
        outs,
        scalar=place,
    )
    return [out.reshape(4 * q, tile), *rest]


def back_part(chain, cot, down, base, blocks):
    tokens, tile = cot.shape
    half, n = tokens // 2, blocks * BLOCK

    def body(c, w, keep, send):
        acc = dot(c[...], w[...], NT)
        keep[...] = acc[:half]
        send[...] = acc[half:].astype(BF16)

    block, at = (half, BLOCK), lambda j: (0, j)
    outs = [((half, n), dtype, block, at) for dtype in (F32, BF16)]
    return chain(
        body,
        (blocks,),
        [(cot, cot.shape, lambda j: (0, 0)), (down, (BLOCK, tile), lambda j: (base + j, 0))],
        outs,
        flops=2 * tokens * tile * n,
    )


def gate_up_part(chain, act, gate, up, base, blocks):
    tokens, tile = act.shape
    half, n = tokens // 2, blocks * BLOCK

    def body(a, wg, wu, keep, send):
        for k, w in enumerate((wg, wu)):
            acc = dot(a[...], w[...], NN)
            keep[k] = acc[:half]
            send[k] = acc[half:].astype(BF16)

    weight = ((tile, BLOCK), lambda j: (0, base + j))
    block, at = (2, half, BLOCK), lambda j: (0, 0, j)
    outs = [((2, half, n), dtype, block, at) for dtype in (F32, BF16)]
    return chain(
        body,
        (blocks,),
        [(act, act.shape, lambda j: (0, 0)), (gate, *weight), (up, *weight)],
        outs,
        flops=4 * tokens * tile * n,
    )


def add_away(chain, keep, got):
    lead, (half, n) = keep.shape[:-2], keep.shape[-2:]
    zeros = (0,) * len(lead)
    block = (*lead, half // 2, n)

    def body(a, b, out):
        out[...] = (a[...] + b[...].astype(F32)).astype(BF16)

    (out,) = chain(
        body,
        (2,),
        [(x, block, lambda i: (*zeros, 1 - i, 0)) for x in (keep, got)],
        [(keep.shape, BF16, block, lambda i: (*zeros, i, 0))],
    )
    return out


def activate(chain, keep_gu, got_gu, far_gu, keep_b, got_b, far_b, off, blocks):
    half, n = far_gu.shape[1:]
    q = half // 2

    def body(kg, gg, fg, kb, gb, fb, out):
        gate = kg[0] + gg[0].astype(F32) + fg[0].astype(F32)
        up = kg[1] + gg[1].astype(F32) + fg[1].astype(F32)
        back = kb[...] + gb[...].astype(F32) + fb[...].astype(F32)
        active, slope = silu_parts(gate)
        out[0] = (back * up * slope).astype(BF16)
        out[1] = (back * active).astype(BF16)
        out[2] = (active * up).astype(BF16)

    two = ((2, half, BLOCK), lambda j: (0, 0, j))
    one = ((half, BLOCK), lambda j: (0, off + j))
    (out,) = chain(
        body,
        (n // BLOCK,),
        [(x, *two) for x in (keep_gu, got_gu, far_gu)] + [(x, *one) for x in (keep_b, got_b, far_b)],
        [((3, half, n), BF16, (3, half, BLOCK), lambda j: (0, 0, j))],
    )
    return out


def split_slots(acc, rows, keep, send):
    view = acc.reshape(4, 8, rows, acc.shape[-1])
    for s in range(4):
        keep[s] = view[:, 2 * s]
        send[s] = view[:, 2 * s + 1].astype(BF16)


def summed(chain, parts, terms, base, blocks, halves=1, half=0, split=False):
    kinds = parts[0].shape[0]
    half_rows, n = parts[0].shape[1:]
    q = half_rows // 2
    rows = q // 8
    first_weight, dims = terms[0][1][0], terms[0][2]
    tile = first_weight.shape[1 if dims is NN else 0]
    width = tile // halves
    step = min(2 * BLOCK, width)
    off = half * (width // step)
    ins = [(p, p.shape, lambda j: (0, 0, 0)) for p in parts]
    outs, alias, plan = [], {}, []
    for first, weights, dims, prev in terms:
        refs = []
        for w in weights:
            for i in range(blocks):
                refs.append(len(ins))
                if dims is NN:
                    index = functools.partial(lambda i, j: (base + i, off + j), i)
                    ins.append((w, (BLOCK, step), index))
                else:
                    index = functools.partial(lambda i, j: (off + j, base + i), i)
                    ins.append((w, (step, BLOCK), index))
        before = None
        if prev is not None:
            before = len(ins)
            ins.append((prev, (4 * q, step), lambda j: (0, off + j)))
            if not split:
                alias[before] = len(outs)
        plan.append((first, len(weights), dims, refs, before, len(outs)))
        if split:
            shape, block = (4, 4, rows, width), (4, 4, rows, step)
            outs.append((shape, F32, block, lambda j: (0, 0, 0, j)))
            outs.append((shape, BF16, block, lambda j: (0, 0, 0, j)))
        else:
            outs.append(((4 * q, tile), F32, (4 * q, step), lambda j: (0, j)))
    n_in = len(ins)

    def body(*refs):
        out_refs, scratch = refs[n_in:-1], refs[-1]

        @pl.when(pl.program_id(0) == 0)
        def _():
            for g in range(2):
                for k in range(kinds):
                    scratch[k, g * half_rows : (g + 1) * half_rows] = refs[g][k]

        for first, count, dims, at, before, out in plan:
            total = None if before is None else refs[before][...]
            for k in range(count):
                for i in range(blocks):
                    left = scratch[first + k, :, i * BLOCK : (i + 1) * BLOCK]
                    term = dot(left, refs[at[k * blocks + i]][...], dims)
                    total = term if total is None else total + term
            if split:
                split_slots(total, rows, out_refs[out], out_refs[out + 1])
            else:
                out_refs[out][...] = total

    return chain(
        body,
        (width // step,),
        ins,
        outs,
        scratch=[pltpu.VMEM((kinds, 4 * q, n), BF16)],
        flops=6 * 4 * q * n * width,
        alias=alias,
    )


def gradients(chain, act_t, cot, parts, base, blocks, prev, units):
    tile, tokens = act_t.shape
    half = tokens // 2
    lead = 4

    def body(*refs):
        a, c, own, near = refs[:lead]
        outs = refs[-3:]
        for k in range(2):
            right = jnp.concatenate([own[k], near[k]], axis=0)
            outs[k][...] = dot(a[...], right, NN).astype(BF16)
        left = jnp.concatenate([own[2], near[2]], axis=0)
        outs[2][...] = dot(left, c[...], TN).astype(BF16)

    ins = [(act_t, act_t.shape, lambda j: (0, 0)), (cot, cot.shape, lambda j: (0, 0))]
    ins += [(p, (3, half, BLOCK), lambda j: (0, 0, j)) for p in parts]
    column = ((tile, units), BF16, (tile, BLOCK), lambda j: (0, base + j))
    outs = [column, column, ((units, tile), BF16, (BLOCK, tile), lambda j: (base + j, 0))]
    alias = {}
    if prev is not None:
        ins += [(p, (16, 128), lambda j: (0, 0)) for p in prev]
        alias = {lead + i: i for i in range(3)}
    return chain(body, (blocks,), ins, outs, flops=6 * tokens * tile * blocks * BLOCK, alias=alias)


def pass_on(chain, keep, got):
    slots = keep.shape[0]
    rest = keep.shape[1:]
    zeros = (0,) * len(rest)

    def body(k, g, *outs):
        for i in range(slots // 2):
            for out, s in zip(outs, (2 * i, 2 * i + 1)):
                out[i] = (k[s] + g[s].astype(F32)).astype(out.dtype)

    whole = ((slots, *rest), lambda j: (0, *zeros))
    half = ((slots // 2, *rest), lambda j: (0, *zeros))
    return chain(
        body,
        (1,),
        [(keep, *whole), (got, *whole)],
        [(half[0], dtype, *half) for dtype in (F32, BF16)],
    )


def finish(chain, me, halves, by_rows):
    four, rows, width = halves[0][0].shape[1:]
    tile = width * len(halves)

    def body(s, *refs):
        outs = refs[2 * len(halves) :]
        for h in range(len(halves)):
            total = refs[2 * h][0] + refs[2 * h + 1][0].astype(F32)
            columns = slice(h * width, (h + 1) * width)
            for i, g in enumerate(ORDER):
                rounded = total[i].astype(BF16)
                if by_rows:
                    outs[0][s[0] ^ g, :, columns] = rounded
                else:
                    outs[g][:, columns] = rounded

    ins = []
    for own, got in halves:
        ins += [(x, (1, four, rows, width), lambda j, s: (0, 0, 0, 0)) for x in (own, got)]
    if by_rows:
        outs = [((four, rows, tile), BF16, (four, rows, tile), lambda j, s: (0, 0, 0))]
    else:
        outs = [((rows, tile), BF16, (rows, tile), lambda j, s: (0, 0))] * 4
    res = chain(body, (1,), ins, outs, scalar=me)
    return res[0].reshape(four * rows, tile) if by_rows else res


def place_columns(chain, me, groups):
    rows, tile = groups[0].shape

    def body(s, *refs):
        for g in range(4):

            @pl.when(pl.program_id(0) == g)
            def _():
                refs[4][...] = refs[g][...]

    (out,) = chain(
        body,
        (4,),
        [(x, (rows, tile), lambda g, s: (0, 0)) for x in groups],
        [((rows, 4 * tile), BF16, (rows, tile), lambda g, s: (0, s[0] ^ g))],
        scalar=me,
    )
    return out


def spread(own):
    far = swap(own, 2)
    return [own, swap(own, 1), far, swap(far, 1)]


def chunk_sizes(total):
    last = max(1, total // 6)
    rest = total - last
    return [rest // 3, (rest + 2) // 3, (rest + 1) // 3, last]


def local_eight(activations, cotangent, gate_proj, up_proj, down_proj):
    place = jnp.stack([lax.axis_index("narrow"), lax.axis_index("wide")]).astype(jnp.int32)
    rows = activations.shape[0]
    tile, units = gate_proj.shape
    sizes = chunk_sizes(units // BLOCK)
    chunks = [(sum(sizes[:c]), sizes[c]) for c in range(4)]
    backs = [(0, chunks[2][0]), (chunks[2][0], sizes[2] + sizes[3])]
    back_of = [(0, 0), (0, sizes[0]), (1, 0), (1, sizes[2])]
    chain = Chain()

    keep_b, got_b, far_b = {}, {}, {}
    keep_gu, got_gu, far_gu = {}, {}, {}
    own, near = {}, {}
    out = grad = grads = None

    def back(p):
        keep_b[p], send = back_part(chain, cot, down_proj, *backs[p])
        got_b[p] = swap(send, 1)

    def back_x(p):
        far_b[p] = swap(add_away(chain, keep_b[p], got_b[p]), 2)

    def gate_up(c):
        keep_gu[c], send = gate_up_part(chain, act, gate_proj, up_proj, *chunks[c])
        got_gu[c] = swap(send, 1)

    def gate_up_x(c):
        far_gu[c] = swap(add_away(chain, keep_gu[c], got_gu[c]), 2)

    def elementwise(c):
        p, off = back_of[c]
        own[c] = activate(
            chain, keep_gu[c], got_gu[c], far_gu[c], keep_b[p], got_b[p], far_b[p], off, sizes[c]
        )
        near[c] = swap(own[c], 1)

    def out_term():
        return (2, [down_proj], NN, out)

    def grad_term():
        return (0, [gate_proj, up_proj], NT, grad)

    def add_both(c):
        nonlocal out, grad
        out, grad = summed(chain, (own[c], near[c]), [out_term(), grad_term()], *chunks[c])

    def all_grads(c):
        nonlocal grads
        grads = gradients(chain, act_t, cot, (own[c], near[c]), *chunks[c], grads, units)

    def last_part(term, half):
        keep, send = summed(chain, (own[3], near[3]), [term], *chunks[3], 2, half, True)
        return keep, swap_wide(send, 1)

    def over_z(pair, mask):
        keep, send = pass_on(chain, *pair)
        return keep, swap_wide(send, mask)

    cot_all = lax.all_gather(cotangent, "wide", axis=0, tiled=True)
    tiles = lax.all_to_all(activations, "narrow", split_axis=1, concat_axis=0, tiled=True)
    pieces = {0: tiles, 1: swap_wide(tiles, 1)}
    for k in (2, 4, 6):
        pieces[k] = swap_wide(tiles, k)
        pieces[k + 1] = swap_wide(pieces[k], 1)
    slots = [(pieces[k], lambda s: 0) for k in range(8)]
    act, act_t = arrange(chain, place, slots, rows, tile, True)
    gate_up(0)
    gate_up(1)
    slots = [(cot_all, functools.partial(lambda k, s: (s[1] ^ k) * 4, k)) for k in range(8)]
    (cot,) = arrange(chain, place, slots, rows, tile)
    gate_up_x(0)
    back(0)
    gate_up_x(1)
    gate_up(2)
    chain.after(far_gu[0])
    back_x(0)
    back(1)
    gate_up_x(2)
    chain.after(far_gu[1])
    gate_up(3)
    back_x(1)
    elementwise(0)
    elementwise(1)
    gate_up_x(3)
    add_both(0)
    all_grads(0)
    chain.after(far_gu[2])
    add_both(1)
    elementwise(2)
    all_grads(1)
    elementwise(3)
    add_both(2)
    parts = [last_part(out_term(), 0)]
    parts.append(last_part(out_term(), 1))
    parts.append(last_part(grad_term(), 0))
    parts[0] = over_z(parts[0], 2)
    parts.append(last_part(grad_term(), 1))
    parts[1] = over_z(parts[1], 2)
    parts[0] = over_z(parts[0], 4)
    all_grads(2)
    parts[2] = over_z(parts[2], 2)
    parts[1] = over_z(parts[1], 4)
    all_grads(3)
    parts[3] = over_z(parts[3], 2)
    parts[2] = over_z(parts[2], 4)
    block_output = finish(chain, place, parts[:2], True)
    parts[3] = over_z(parts[3], 4)
    groups = finish(chain, place, parts[2:], False)
    groups = [groups[0]] + [swap(groups[g], g) for g in range(1, 4)]
    input_gradient = place_columns(chain, place, groups)
    return (block_output, input_gradient, *grads)


def scatter_sum(part):
    split = part.reshape(-1, 4, part.shape[0] // 4 // lax.axis_size("wide"), part.shape[-1])
    got = swap(jnp.stack([split[:, 1], split[:, 3]]), 1)
    away = (split[:, 2] + got[1]).astype(BF16)
    return (split[:, 0] + got[0]) + swap(away, 2).astype(F32)


def spread_rows(own):
    return jnp.stack(spread(own), axis=1).reshape(-1, own.shape[-1])


def local_any(activations, cotangent, gate_proj, up_proj, down_proj):
    me = lax.axis_index("narrow")
    rows = activations.shape[0]
    tile = gate_proj.shape[0]
    pieces = [lax.dynamic_slice_in_dim(activations, (me ^ g) * tile, tile, 1) for g in range(4)]
    pieces = [pieces[0]] + [swap(pieces[g], g) for g in range(1, 4)]
    cots = [lax.dynamic_slice_in_dim(cotangent, (me ^ g) * rows, rows, 0) for g in range(4)]

    def gathered(parts):
        return lax.all_gather(jnp.stack(parts), "wide", axis=0, tiled=True).reshape(-1, tile)

    features, upstream = gathered(pieces), gathered(cots)
    gate = scatter_sum(dot(features, gate_proj, NN))
    up = scatter_sum(dot(features, up_proj, NN))
    back = scatter_sum(dot(upstream, down_proj, NT))
    active, slope = silu_parts(gate)
    gate_delta = spread_rows((back * up * slope).astype(BF16))
    up_delta = spread_rows((back * active).astype(BF16))
    hidden = spread_rows((active * up).astype(BF16))

    def landed(total):
        got = lax.psum_scatter(total, "wide", scatter_dimension=0, tiled=True)
        return got.astype(BF16).reshape(4, rows, tile)

    grad = landed(dot(gate_delta, gate_proj, NT) + dot(up_delta, up_proj, NT))
    out = landed(dot(hidden, down_proj, NN))
    gate_gradient = dot(features, gate_delta, TN).astype(BF16)
    up_gradient = dot(features, up_delta, TN).astype(BF16)
    down_gradient = dot(hidden, upstream, TN).astype(BF16)

    block_output = jnp.concatenate(
        [lax.dynamic_index_in_dim(out, me ^ g, 0, keepdims=False) for g in range(4)]
    )
    grads = jnp.stack([grad[0]] + [swap(grad[g], g) for g in range(1, 4)])
    input_gradient = jnp.concatenate(
        [lax.dynamic_index_in_dim(grads, me ^ g, 0, keepdims=False) for g in range(4)], axis=1
    )
    return (block_output, input_gradient, gate_gradient, up_gradient, down_gradient)


def local(activations, cotangent, gate_proj, up_proj, down_proj):
    args = (activations, cotangent, gate_proj, up_proj, down_proj)
    rows, (tile, units) = activations.shape[0], gate_proj.shape
    fits = lax.axis_size("wide") == 8 and rows % 16 == 0
    if fits and tile % (2 * BLOCK) == 0 and units % BLOCK == 0 and units >= 6 * BLOCK:
        return local_eight(*args)
    return local_any(*args)


def solution(mesh):
    placed = (
        P(("wide", "narrow"), None),
        P("wide", "narrow"),
        P("narrow", "wide"),
        P("narrow", "wide"),
        P("wide", "narrow"),
    )
    return jax.shard_map(
        local,
        mesh=mesh,
        in_specs=placed,
        out_specs=(
            P("wide", "narrow"),
            P(("wide", "narrow"), None),
            P("narrow", "wide"),
            P("narrow", "wide"),
            P("wide", "narrow"),
        ),
        check_vma=False,
    )
```

```python
import functools

import jax
import jax.numpy as jnp
from jax import lax
from jax.experimental import pallas as pl
from jax.experimental.pallas import tpu as pltpu
from jax.sharding import PartitionSpec as P

BF16, F32 = jnp.bfloat16, jnp.float32
BLOCK = 256
VMEM_LIMIT = 64 * 1024 * 1024 - 256 * 1024
ORDER = (0, 2, 1, 3)
NN = (((1,), (0,)), ((), ()))
NT = (((1,), (1,)), ((), ()))
TN = (((0,), (0,)), ((), ()))


def dot(left, right, dims):
    return lax.dot_general(left, right, dims, preferred_element_type=F32)


def silu_parts(gate):
    sigma = jax.nn.sigmoid(gate)
    return (gate * sigma, sigma * (1.0 + gate * (1.0 - sigma)))


def swap(value, mask):
    return lax.ppermute(value, "narrow", [(i, i ^ mask) for i in range(4)])


def swap_wide(value, mask):
    return lax.ppermute(value, "wide", [(i, i ^ mask) for i in range(8)])


class Chain:
    def __init__(self):
        self.token = None
        self.waits = []

    def after(self, *arrays):
        self.waits += arrays

    def __call__(self, body, grid, ins, outs, scratch=(), flops=0, alias=None, scalar=None):
        lead = 0 if scalar is None else 1
        arrays = [a for a, _, _ in ins]
        specs = [pl.BlockSpec(block, index) for _, block, index in ins]
        unread = self.waits + ([] if self.token is None else [self.token])
        self.waits = []
        arrays += unread
        specs += [pl.BlockSpec(memory_space=pltpu.HBM)] * len(unread)
        shapes = [jax.ShapeDtypeStruct(shape, dtype) for shape, dtype, _, _ in outs]
        out_specs = [pl.BlockSpec(block, index) for _, _, block, index in outs]
        shapes.append(jax.ShapeDtypeStruct((8, 128), F32))
        out_specs.append(pl.BlockSpec((8, 128), lambda *i: (0, 0)))
        n_in, n_out = len(ins), len(outs)

        def kernel(*refs):
            head, refs = refs[:lead], refs[lead:]
            in_refs = refs[:n_in]
            rest = refs[n_in + len(unread) :]
            out_refs, token, scratch_refs = rest[:n_out], rest[n_out], rest[n_out + 1 :]
            token[...] = jnp.zeros(token.shape, F32)
            body(*head, *in_refs, *out_refs, *scratch_refs)

        res = pl.pallas_call(
            kernel,
            grid_spec=pltpu.PrefetchScalarGridSpec(
                num_scalar_prefetch=lead,
                grid=grid,
                in_specs=specs,
                out_specs=out_specs,
                scratch_shapes=list(scratch),
            ),
            out_shape=shapes,
            input_output_aliases={k + lead: v for k, v in (alias or {}).items()},
            compiler_params=pltpu.CompilerParams(vmem_limit_bytes=VMEM_LIMIT),
            cost_estimate=pl.CostEstimate(flops=1, bytes_accessed=1, transcendentals=0),
        )(*(() if scalar is None else (scalar,)), *arrays)
        self.token = res[-1]
        return res[:-1]


def group(i):
    return (i & 1) * 2 + (i >> 1)


def join(chain, parts):
    rows, tile = parts[0].shape
    count = len(parts)

    def body(*refs):
        for i in range(count):
            refs[count][i] = refs[i][...]

    (out,) = chain(
        body,
        (1,),
        [(p, (rows, tile), lambda j: (0, 0)) for p in parts],
        [((count, rows, tile), BF16, (count, rows, tile), lambda j: (0, 0, 0))],
    )
    return out


def arrange(chain, place, slots, rows, tile, turned=False):
    q = 8 * rows

    def body(_, *refs):
        out = refs[8]
        for k in range(8):
            out[0, k] = refs[k][...]
        if turned:
            refs[9][...] = out[0].reshape(q, tile).T

    outs = [((4, 8, rows, tile), BF16, (1, 8, rows, tile), lambda g, s: (g, 0, 0, 0))]
    if turned:
        outs.append(((tile, 4 * q), BF16, (tile, q), lambda g, s: (0, g)))
    out, *rest = chain(
        body,
        (4,),
        [
            (p, (rows, tile), functools.partial(lambda at, i, s: (at(s) + (s[0] ^ group(i)), 0), at))
            for p, at in slots
        ],
        outs,
        scalar=place,
    )
    return [out.reshape(4 * q, tile), *rest]


def back_part(chain, cot, down, base, blocks):
    tokens, tile = cot.shape
    half, n = tokens // 2, blocks * BLOCK

    def body(c, w, keep, send):
        acc = dot(c[...], w[...], NT)
        keep[...] = acc[:half]
        send[...] = acc[half:].astype(BF16)

    block, at = (half, BLOCK), lambda j: (0, j)
    outs = [((half, n), dtype, block, at) for dtype in (F32, BF16)]
    return chain(
        body,
        (blocks,),
        [(cot, cot.shape, lambda j: (0, 0)), (down, (BLOCK, tile), lambda j: (base + j, 0))],
        outs,
        flops=2 * tokens * tile * n,
    )


def gate_up_part(chain, act, gate, up, base, blocks):
    tokens, tile = act.shape
    half, n = tokens // 2, blocks * BLOCK

    def body(a, wg, wu, keep, send):
        for k, w in enumerate((wg, wu)):
            acc = dot(a[...], w[...], NN)
            keep[k] = acc[:half]
            send[k] = acc[half:].astype(BF16)

    weight = ((tile, BLOCK), lambda j: (0, base + j))
    block, at = (2, half, BLOCK), lambda j: (0, 0, j)
    outs = [((2, half, n), dtype, block, at) for dtype in (F32, BF16)]
    return chain(
        body,
        (blocks,),
        [(act, act.shape, lambda j: (0, 0)), (gate, *weight), (up, *weight)],
        outs,
        flops=4 * tokens * tile * n,
    )


def add_away(chain, keep, got):
    lead, (half, n) = keep.shape[:-2], keep.shape[-2:]
    zeros = (0,) * len(lead)
    block = (*lead, half // 2, n)

    def body(a, b, out):
        out[...] = (a[...] + b[...].astype(F32)).astype(BF16)

    (out,) = chain(
        body,
        (2,),
        [(x, block, lambda i: (*zeros, 1 - i, 0)) for x in (keep, got)],
        [(keep.shape, BF16, block, lambda i: (*zeros, i, 0))],
    )
    return out


def activate(chain, keep_gu, got_gu, far_gu, keep_b, got_b, far_b, off, blocks):
    half, n = far_gu.shape[1:]
    q = half // 2

    def body(kg, gg, fg, kb, gb, fb, out):
        gate = kg[0] + gg[0].astype(F32) + fg[0].astype(F32)
        up = kg[1] + gg[1].astype(F32) + fg[1].astype(F32)
        back = kb[...] + gb[...].astype(F32) + fb[...].astype(F32)
        active, slope = silu_parts(gate)
        out[0] = (back * up * slope).astype(BF16)
        out[1] = (back * active).astype(BF16)
        out[2] = (active * up).astype(BF16)

    two = ((2, half, BLOCK), lambda j: (0, 0, j))
    one = ((half, BLOCK), lambda j: (0, off + j))
    (out,) = chain(
        body,
        (n // BLOCK,),
        [(x, *two) for x in (keep_gu, got_gu, far_gu)] + [(x, *one) for x in (keep_b, got_b, far_b)],
        [((3, half, n), BF16, (3, half, BLOCK), lambda j: (0, 0, j))],
    )
    return out


def split_slots(acc, rows, keep, send):
    view = acc.reshape(4, 8, rows, acc.shape[-1])
    for s in range(4):
        keep[s] = view[:, 2 * s]
        send[s] = view[:, 2 * s + 1].astype(BF16)


def summed(chain, parts, terms, base, blocks, halves=1, half=0, split=False):
    kinds = parts[0].shape[0]
    half_rows, n = parts[0].shape[1:]
    q = half_rows // 2
    rows = q // 8
    first_weight, dims = terms[0][1][0], terms[0][2]
    tile = first_weight.shape[1 if dims is NN else 0]
    width = tile // halves
    step = min(2 * BLOCK, width)
    off = half * (width // step)
    ins = [(p, p.shape, lambda j: (0, 0, 0)) for p in parts]
    outs, alias, plan = [], {}, []
    for first, weights, dims, prev in terms:
        refs = []
        for w in weights:
            for i in range(blocks):
                refs.append(len(ins))
                if dims is NN:
                    index = functools.partial(lambda i, j: (base + i, off + j), i)
                    ins.append((w, (BLOCK, step), index))
                else:
                    index = functools.partial(lambda i, j: (off + j, base + i), i)
                    ins.append((w, (step, BLOCK), index))
        before = None
        if prev is not None:
            before = len(ins)
            ins.append((prev, (4 * q, step), lambda j: (0, off + j)))
            if not split:
                alias[before] = len(outs)
        plan.append((first, len(weights), dims, refs, before, len(outs)))
        if split:
            shape, block = (4, 4, rows, width), (4, 4, rows, step)
            outs.append((shape, F32, block, lambda j: (0, 0, 0, j)))
            outs.append((shape, BF16, block, lambda j: (0, 0, 0, j)))
        else:
            outs.append(((4 * q, tile), F32, (4 * q, step), lambda j: (0, j)))
    n_in = len(ins)

    def body(*refs):
        out_refs, scratch = refs[n_in:-1], refs[-1]

        @pl.when(pl.program_id(0) == 0)
        def _():
            for g in range(2):
                for k in range(kinds):
                    scratch[k, g * half_rows : (g + 1) * half_rows] = refs[g][k]

        for first, count, dims, at, before, out in plan:
            total = None if before is None else refs[before][...]
            for k in range(count):
                for i in range(blocks):
                    left = scratch[first + k, :, i * BLOCK : (i + 1) * BLOCK]
                    term = dot(left, refs[at[k * blocks + i]][...], dims)
                    total = term if total is None else total + term
            if split:
                split_slots(total, rows, out_refs[out], out_refs[out + 1])
            else:
                out_refs[out][...] = total

    return chain(
        body,
        (width // step,),
        ins,
        outs,
        scratch=[pltpu.VMEM((kinds, 4 * q, n), BF16)],
        flops=6 * 4 * q * n * width,
        alias=alias,
    )


def gradients(chain, act_t, cot, parts, base, blocks, prev, units):
    tile, tokens = act_t.shape
    half = tokens // 2
    lead = 4

    def body(*refs):
        a, c, own, near = refs[:lead]
        outs = refs[-3:]
        for k in range(2):
            right = jnp.concatenate([own[k], near[k]], axis=0)
            outs[k][...] = dot(a[...], right, NN).astype(BF16)
        left = jnp.concatenate([own[2], near[2]], axis=0)
        outs[2][...] = dot(left, c[...], TN).astype(BF16)

    ins = [(act_t, act_t.shape, lambda j: (0, 0)), (cot, cot.shape, lambda j: (0, 0))]
    ins += [(p, (3, half, BLOCK), lambda j: (0, 0, j)) for p in parts]
    column = ((tile, units), BF16, (tile, BLOCK), lambda j: (0, base + j))
    outs = [column, column, ((units, tile), BF16, (BLOCK, tile), lambda j: (base + j, 0))]
    alias = {}
    if prev is not None:
        ins += [(p, (16, 128), lambda j: (0, 0)) for p in prev]
        alias = {lead + i: i for i in range(3)}
    return chain(body, (blocks,), ins, outs, flops=6 * tokens * tile * blocks * BLOCK, alias=alias)


def pass_on(chain, keep, got):
    slots = keep.shape[0]
    rest = keep.shape[1:]
    zeros = (0,) * len(rest)

    def body(k, g, *outs):
        for i in range(slots // 2):
            for out, s in zip(outs, (2 * i, 2 * i + 1)):
                out[i] = (k[s] + g[s].astype(F32)).astype(out.dtype)

    whole = ((slots, *rest), lambda j: (0, *zeros))
    half = ((slots // 2, *rest), lambda j: (0, *zeros))
    return chain(
        body,
        (1,),
        [(keep, *whole), (got, *whole)],
        [(half[0], dtype, *half) for dtype in (F32, BF16)],
    )


def finish(chain, me, halves, by_rows):
    four, rows, width = halves[0][0].shape[1:]
    tile = width * len(halves)

    def body(s, *refs):
        outs = refs[2 * len(halves) :]
        for h in range(len(halves)):
            total = refs[2 * h][0] + refs[2 * h + 1][0].astype(F32)
            columns = slice(h * width, (h + 1) * width)
            for i, g in enumerate(ORDER):
                rounded = total[i].astype(BF16)
                if by_rows:
                    outs[0][s[0] ^ g, :, columns] = rounded
                else:
                    outs[g][:, columns] = rounded

    ins = []
    for own, got in halves:
        ins += [(x, (1, four, rows, width), lambda j, s: (0, 0, 0, 0)) for x in (own, got)]
    if by_rows:
        outs = [((four, rows, tile), BF16, (four, rows, tile), lambda j, s: (0, 0, 0))]
    else:
        outs = [((rows, tile), BF16, (rows, tile), lambda j, s: (0, 0))] * 4
    res = chain(body, (1,), ins, outs, scalar=me)
    return res[0].reshape(four * rows, tile) if by_rows else res


def place_columns(chain, me, groups):
    rows, tile = groups[0].shape

    def body(s, *refs):
        for g in range(4):

            @pl.when(pl.program_id(0) == g)
            def _():
                refs[4][...] = refs[g][...]

    (out,) = chain(
        body,
        (4,),
        [(x, (rows, tile), lambda g, s: (0, 0)) for x in groups],
        [((rows, 4 * tile), BF16, (rows, tile), lambda g, s: (0, s[0] ^ g))],
        scalar=me,
    )
    return out


def spread(own):
    far = swap(own, 2)
    return [own, swap(own, 1), far, swap(far, 1)]


def chunk_sizes(total):
    small = max(1, total // 6)
    rest = total - 2 * small
    return [small, (rest + 1) // 2, rest // 2, small]


def local_eight(activations, cotangent, gate_proj, up_proj, down_proj):
    place = jnp.stack([lax.axis_index("narrow"), lax.axis_index("wide")]).astype(jnp.int32)
    rows = activations.shape[0]
    tile, units = gate_proj.shape
    sizes = chunk_sizes(units // BLOCK)
    chunks = [(sum(sizes[:c]), sizes[c]) for c in range(4)]
    backs = [chunks[0], chunks[1], (chunks[2][0], sizes[2] + sizes[3])]
    back_of = [(0, 0), (1, 0), (2, 0), (2, sizes[2])]
    chain = Chain()

    keep_b, got_b, far_b = {}, {}, {}
    keep_gu, got_gu, far_gu = {}, {}, {}
    own, near = {}, {}
    out = grad = grads = None

    def back(p):
        keep_b[p], send = back_part(chain, cot, down_proj, *backs[p])
        got_b[p] = swap(send, 1)

    def back_x(p):
        far_b[p] = swap(add_away(chain, keep_b[p], got_b[p]), 2)

    def gate_up(c):
        keep_gu[c], send = gate_up_part(chain, act, gate_proj, up_proj, *chunks[c])
        got_gu[c] = swap(send, 1)

    def gate_up_x(c):
        far_gu[c] = swap(add_away(chain, keep_gu[c], got_gu[c]), 2)

    def elementwise(c):
        p, off = back_of[c]
        own[c] = activate(
            chain, keep_gu[c], got_gu[c], far_gu[c], keep_b[p], got_b[p], far_b[p], off, sizes[c]
        )
        near[c] = swap(own[c], 1)

    def out_term():
        return (2, [down_proj], NN, out)

    def grad_term():
        return (0, [gate_proj, up_proj], NT, grad)

    def add_both(c):
        nonlocal out, grad
        out, grad = summed(chain, (own[c], near[c]), [out_term(), grad_term()], *chunks[c])

    def all_grads(c):
        nonlocal grads
        grads = gradients(chain, act_t, cot, (own[c], near[c]), *chunks[c], grads, units)

    def last_part(term, halves=1, half=0):
        keep, send = summed(chain, (own[3], near[3]), [term], *chunks[3], halves, half, True)
        return keep, swap_wide(send, 1)

    def over_z(pair, mask):
        keep, send = pass_on(chain, *pair)
        return keep, swap_wide(send, mask)

    def gather_z(mine):
        return [mine] + [swap_wide(mine, k) for k in (2, 4, 6)]

    cot_even, cot_first = gather_z(cotangent), swap_wide(cotangent, 1)
    tiles = lax.all_to_all(activations, "narrow", split_axis=1, concat_axis=0, tiled=True)
    act_even, act_first = gather_z(tiles), swap_wide(tiles, 1)
    act_odd = [swap_wide(x, 1) for x in act_even[1:]]
    chain.after(tiles, cot_first, act_first)
    cot_odd = swap_wide(join(chain, cot_even[1:]), 1).reshape(12 * rows, tile)

    def slots(even, first, odd):
        res = [(even[0], 0), (first, 0)]
        for i in range(3):
            res += [(even[i + 1], 0), odd[i]]
        return [(x, functools.partial(lambda at, s: at, at)) for x, at in res]

    chain.after(*act_even[1:])
    cot_slots = slots(cot_even, cot_first, [(cot_odd, 4 * i) for i in range(3)])
    (cot,) = arrange(chain, place, cot_slots, rows, tile)
    back(0)
    chain.after(*act_odd)
    back(1)
    back_x(0)
    back(2)
    back_x(1)
    act_slots = slots(act_even, act_first, [(x, 0) for x in act_odd])
    act, act_t = arrange(chain, place, act_slots, rows, tile, True)
    chain.after(far_b[0])
    gate_up(0)
    back_x(2)
    chain.after(far_b[1], got_gu[0])
    gate_up(1)
    gate_up_x(0)
    chain.after(far_b[2])
    gate_up(2)
    gate_up_x(1)
    gate_up(3)
    gate_up_x(2)
    chain.after(got_gu[3])
    elementwise(0)
    gate_up_x(3)
    add_both(0)
    all_grads(0)
    elementwise(1)
    add_both(1)
    elementwise(2)
    all_grads(1)
    elementwise(3)
    add_both(2)
    grad_part = last_part(grad_term())
    out_parts = [last_part(out_term(), 2, 0), last_part(out_term(), 2, 1)]
    all_grads(2)
    all_grads(3)
    grad_part = over_z(grad_part, 2)
    out_parts[0] = over_z(out_parts[0], 2)
    grad_part = over_z(grad_part, 4)
    out_parts[1] = over_z(out_parts[1], 2)
    out_parts[0] = over_z(out_parts[0], 4)
    groups = finish(chain, place, [grad_part], False)
    groups = [groups[0]] + [swap(groups[g], g) for g in range(1, 4)]
    out_parts[1] = over_z(out_parts[1], 4)
    input_gradient = place_columns(chain, place, groups)
    block_output = finish(chain, place, out_parts, True)
    return (block_output, input_gradient, *grads)


def scatter_sum(part):
    split = part.reshape(-1, 4, part.shape[0] // 4 // lax.axis_size("wide"), part.shape[-1])
    got = swap(jnp.stack([split[:, 1], split[:, 3]]), 1)
    away = (split[:, 2] + got[1]).astype(BF16)
    return (split[:, 0] + got[0]) + swap(away, 2).astype(F32)


def spread_rows(own):
    return jnp.stack(spread(own), axis=1).reshape(-1, own.shape[-1])


def local_any(activations, cotangent, gate_proj, up_proj, down_proj):
    me = lax.axis_index("narrow")
    rows = activations.shape[0]
    tile = gate_proj.shape[0]
    pieces = [lax.dynamic_slice_in_dim(activations, (me ^ g) * tile, tile, 1) for g in range(4)]
    pieces = [pieces[0]] + [swap(pieces[g], g) for g in range(1, 4)]
    cots = [lax.dynamic_slice_in_dim(cotangent, (me ^ g) * rows, rows, 0) for g in range(4)]

    def gathered(parts):
        return lax.all_gather(jnp.stack(parts), "wide", axis=0, tiled=True).reshape(-1, tile)

    features, upstream = gathered(pieces), gathered(cots)
    gate = scatter_sum(dot(features, gate_proj, NN))
    up = scatter_sum(dot(features, up_proj, NN))
    back = scatter_sum(dot(upstream, down_proj, NT))
    active, slope = silu_parts(gate)
    gate_delta = spread_rows((back * up * slope).astype(BF16))
    up_delta = spread_rows((back * active).astype(BF16))
    hidden = spread_rows((active * up).astype(BF16))

    def landed(total):
        got = lax.psum_scatter(total, "wide", scatter_dimension=0, tiled=True)
        return got.astype(BF16).reshape(4, rows, tile)

    grad = landed(dot(gate_delta, gate_proj, NT) + dot(up_delta, up_proj, NT))
    out = landed(dot(hidden, down_proj, NN))
    gate_gradient = dot(features, gate_delta, TN).astype(BF16)
    up_gradient = dot(features, up_delta, TN).astype(BF16)
    down_gradient = dot(hidden, upstream, TN).astype(BF16)

    block_output = jnp.concatenate(
        [lax.dynamic_index_in_dim(out, me ^ g, 0, keepdims=False) for g in range(4)]
    )
    grads = jnp.stack([grad[0]] + [swap(grad[g], g) for g in range(1, 4)])
    input_gradient = jnp.concatenate(
        [lax.dynamic_index_in_dim(grads, me ^ g, 0, keepdims=False) for g in range(4)], axis=1
    )
    return (block_output, input_gradient, gate_gradient, up_gradient, down_gradient)


def local(activations, cotangent, gate_proj, up_proj, down_proj):
    args = (activations, cotangent, gate_proj, up_proj, down_proj)
    rows, (tile, units) = activations.shape[0], gate_proj.shape
    fits = lax.axis_size("wide") == 8 and rows % 16 == 0
    if fits and tile % (2 * BLOCK) == 0 and units % BLOCK == 0 and units >= 6 * BLOCK:
        return local_eight(*args)
    return local_any(*args)


def solution(mesh):
    placed = (
        P(("wide", "narrow"), None),
        P("wide", "narrow"),
        P("narrow", "wide"),
        P("narrow", "wide"),
        P("wide", "narrow"),
    )
    return jax.shard_map(
        local,
        mesh=mesh,
        in_specs=placed,
        out_specs=(
            P("wide", "narrow"),
            P(("wide", "narrow"), None),
            P("narrow", "wide"),
            P("narrow", "wide"),
            P("wide", "narrow"),
        ),
        check_vma=False,
    )
```

```python
import functools

import jax
import jax.numpy as jnp
from jax import lax
from jax.experimental import pallas as pl
from jax.experimental.pallas import tpu as pltpu
from jax.sharding import PartitionSpec as P

BF16, F32 = jnp.bfloat16, jnp.float32
BLOCK = 256
VMEM_LIMIT = 64 * 1024 * 1024 - 256 * 1024
ORDER = (0, 2, 1, 3)
NN = (((1,), (0,)), ((), ()))
NT = (((1,), (1,)), ((), ()))
TN = (((0,), (0,)), ((), ()))


def dot(left, right, dims):
    return lax.dot_general(left, right, dims, preferred_element_type=F32)


def silu_parts(gate):
    sigma = jax.nn.sigmoid(gate)
    return (gate * sigma, sigma * (1.0 + gate * (1.0 - sigma)))


def swap(value, mask):
    return lax.ppermute(value, "narrow", [(i, i ^ mask) for i in range(4)])


def swap_wide(value, mask):
    return lax.ppermute(value, "wide", [(i, i ^ mask) for i in range(8)])


class Chain:
    def __init__(self):
        self.token = None
        self.waits = []

    def after(self, *arrays):
        self.waits += arrays

    def __call__(self, body, grid, ins, outs, scratch=(), flops=0, alias=None, scalar=None):
        lead = 0 if scalar is None else 1
        arrays = [a for a, _, _ in ins]
        specs = [pl.BlockSpec(block, index) for _, block, index in ins]
        unread = self.waits + ([] if self.token is None else [self.token])
        self.waits = []
        arrays += unread
        specs += [pl.BlockSpec(memory_space=pltpu.HBM)] * len(unread)
        shapes = [jax.ShapeDtypeStruct(shape, dtype) for shape, dtype, _, _ in outs]
        out_specs = [pl.BlockSpec(block, index) for _, _, block, index in outs]
        shapes.append(jax.ShapeDtypeStruct((8, 128), F32))
        out_specs.append(pl.BlockSpec((8, 128), lambda *i: (0, 0)))
        n_in, n_out = len(ins), len(outs)

        def kernel(*refs):
            head, refs = refs[:lead], refs[lead:]
            in_refs = refs[:n_in]
            rest = refs[n_in + len(unread) :]
            out_refs, token, scratch_refs = rest[:n_out], rest[n_out], rest[n_out + 1 :]
            token[...] = jnp.zeros(token.shape, F32)
            body(*head, *in_refs, *out_refs, *scratch_refs)

        res = pl.pallas_call(
            kernel,
            grid_spec=pltpu.PrefetchScalarGridSpec(
                num_scalar_prefetch=lead,
                grid=grid,
                in_specs=specs,
                out_specs=out_specs,
                scratch_shapes=list(scratch),
            ),
            out_shape=shapes,
            input_output_aliases={k + lead: v for k, v in (alias or {}).items()},
            compiler_params=pltpu.CompilerParams(vmem_limit_bytes=VMEM_LIMIT),
            cost_estimate=pl.CostEstimate(flops=1, bytes_accessed=1, transcendentals=0),
        )(*(() if scalar is None else (scalar,)), *arrays)
        self.token = res[-1]
        return res[:-1]


def group(i):
    return (i & 1) * 2 + (i >> 1)


def cut_columns(chain, rows_in):
    rows, tile = rows_in.shape[0], rows_in.shape[1] // 4

    def body(x, out):
        out[0] = x[...]

    (out,) = chain(
        body,
        (4,),
        [(rows_in, (rows, tile), lambda j: (0, j))],
        [((4, rows, tile), BF16, (1, rows, tile), lambda j: (j, 0, 0))],
    )
    return out


def join(chain, parts):
    rows, tile = parts[0].shape
    count = len(parts)

    def body(*refs):
        for i in range(count):
            refs[count][i] = refs[i][...]

    (out,) = chain(
        body,
        (1,),
        [(p, (rows, tile), lambda j: (0, 0)) for p in parts],
        [((count, rows, tile), BF16, (count, rows, tile), lambda j: (0, 0, 0))],
    )
    return out


def arrange(chain, place, slots, rows, tile, turned=False):
    q = 8 * rows

    def body(_, *refs):
        out = refs[8]
        for k in range(8):
            out[0, k] = refs[k][...]
        if turned:
            refs[9][...] = out[0].reshape(q, tile).T

    outs = [((4, 8, rows, tile), BF16, (1, 8, rows, tile), lambda g, s: (g, 0, 0, 0))]
    if turned:
        outs.append(((tile, 4 * q), BF16, (tile, q), lambda g, s: (0, g)))
    out, *rest = chain(
        body,
        (4,),
        [
            (p, (rows, tile), functools.partial(lambda at, i, s: (at(s) + (s[0] ^ group(i)), 0), at))
            for p, at in slots
        ],
        outs,
        scalar=place,
    )
    return [out.reshape(4 * q, tile), *rest]


def back_part(chain, cot, down, base, blocks):
    tokens, tile = cot.shape
    half, n = tokens // 2, blocks * BLOCK

    def body(c, w, keep, send):
        acc = dot(c[...], w[...], NT)
        keep[...] = acc[:half]
        send[...] = acc[half:].astype(BF16)

    block, at = (half, BLOCK), lambda j: (0, j)
    outs = [((half, n), dtype, block, at) for dtype in (F32, BF16)]
    return chain(
        body,
        (blocks,),
        [(cot, cot.shape, lambda j: (0, 0)), (down, (BLOCK, tile), lambda j: (base + j, 0))],
        outs,
        flops=2 * tokens * tile * n,
    )


def gate_up_part(chain, act, gate, up, base, blocks):
    tokens, tile = act.shape
    half, n = tokens // 2, blocks * BLOCK

    def body(a, wg, wu, keep, send):
        for k, w in enumerate((wg, wu)):
            acc = dot(a[...], w[...], NN)
            keep[k] = acc[:half]
            send[k] = acc[half:].astype(BF16)

    weight = ((tile, BLOCK), lambda j: (0, base + j))
    block, at = (2, half, BLOCK), lambda j: (0, 0, j)
    outs = [((2, half, n), dtype, block, at) for dtype in (F32, BF16)]
    return chain(
        body,
        (blocks,),
        [(act, act.shape, lambda j: (0, 0)), (gate, *weight), (up, *weight)],
        outs,
        flops=4 * tokens * tile * n,
    )


def add_away(chain, keep, got):
    lead, (half, n) = keep.shape[:-2], keep.shape[-2:]
    zeros = (0,) * len(lead)
    block = (*lead, half // 2, n)

    def body(a, b, out):
        out[...] = (a[...] + b[...].astype(F32)).astype(BF16)

    (out,) = chain(
        body,
        (2,),
        [(x, block, lambda i: (*zeros, 1 - i, 0)) for x in (keep, got)],
        [(keep.shape, BF16, block, lambda i: (*zeros, i, 0))],
    )
    return out


def activate(chain, keep_gu, got_gu, far_gu, keep_b, got_b, far_b, off, blocks):
    half, n = far_gu.shape[1:]
    q = half // 2

    def body(kg, gg, fg, kb, gb, fb, out):
        gate = kg[0] + gg[0].astype(F32) + fg[0].astype(F32)
        up = kg[1] + gg[1].astype(F32) + fg[1].astype(F32)
        back = kb[...] + gb[...].astype(F32) + fb[...].astype(F32)
        active, slope = silu_parts(gate)
        out[0] = (back * up * slope).astype(BF16)
        out[1] = (back * active).astype(BF16)
        out[2] = (active * up).astype(BF16)

    two = ((2, half, BLOCK), lambda j: (0, 0, j))
    one = ((half, BLOCK), lambda j: (0, off + j))
    (out,) = chain(
        body,
        (n // BLOCK,),
        [(x, *two) for x in (keep_gu, got_gu, far_gu)] + [(x, *one) for x in (keep_b, got_b, far_b)],
        [((3, half, n), BF16, (3, half, BLOCK), lambda j: (0, 0, j))],
    )
    return out


def split_slots(acc, rows, keep, send):
    view = acc.reshape(4, 8, rows, acc.shape[-1])
    for s in range(4):
        keep[s] = view[:, 2 * s]
        send[s] = view[:, 2 * s + 1].astype(BF16)


def summed(chain, parts, terms, base, blocks, halves=1, half=0, split=False):
    kinds = parts[0].shape[0]
    half_rows, n = parts[0].shape[1:]
    q = half_rows // 2
    rows = q // 8
    first_weight, dims = terms[0][1][0], terms[0][2]
    tile = first_weight.shape[1 if dims is NN else 0]
    width = tile // halves
    step = min(2 * BLOCK, width)
    off = half * (width // step)
    ins = [(p, p.shape, lambda j: (0, 0, 0)) for p in parts]
    outs, alias, plan = [], {}, []
    for first, weights, dims, prev in terms:
        refs = []
        for w in weights:
            for i in range(blocks):
                refs.append(len(ins))
                if dims is NN:
                    index = functools.partial(lambda i, j: (base + i, off + j), i)
                    ins.append((w, (BLOCK, step), index))
                else:
                    index = functools.partial(lambda i, j: (off + j, base + i), i)
                    ins.append((w, (step, BLOCK), index))
        before = None
        if prev is not None:
            before = len(ins)
            ins.append((prev, (4 * q, step), lambda j: (0, off + j)))
            if not split:
                alias[before] = len(outs)
        plan.append((first, len(weights), dims, refs, before, len(outs)))
        if split:
            shape, block = (4, 4, rows, width), (4, 4, rows, step)
            outs.append((shape, F32, block, lambda j: (0, 0, 0, j)))
            outs.append((shape, BF16, block, lambda j: (0, 0, 0, j)))
        else:
            outs.append(((4 * q, tile), F32, (4 * q, step), lambda j: (0, j)))
    n_in = len(ins)

    def body(*refs):
        out_refs, scratch = refs[n_in:-1], refs[-1]

        @pl.when(pl.program_id(0) == 0)
        def _():
            for g in range(2):
                for k in range(kinds):
                    scratch[k, g * half_rows : (g + 1) * half_rows] = refs[g][k]

        for first, count, dims, at, before, out in plan:
            total = None if before is None else refs[before][...]
            for k in range(count):
                for i in range(blocks):
                    left = scratch[first + k, :, i * BLOCK : (i + 1) * BLOCK]
                    term = dot(left, refs[at[k * blocks + i]][...], dims)
                    total = term if total is None else total + term
            if split:
                split_slots(total, rows, out_refs[out], out_refs[out + 1])
            else:
                out_refs[out][...] = total

    return chain(
        body,
        (width // step,),
        ins,
        outs,
        scratch=[pltpu.VMEM((kinds, 4 * q, n), BF16)],
        flops=6 * 4 * q * n * width,
        alias=alias,
    )


def gradients(chain, act_t, cot, parts, base, blocks, prev, units):
    tile, tokens = act_t.shape
    half = tokens // 2
    lead = 4

    def body(*refs):
        a, c, own, near = refs[:lead]
        outs = refs[-3:]
        for k in range(2):
            right = jnp.concatenate([own[k], near[k]], axis=0)
            outs[k][...] = dot(a[...], right, NN).astype(BF16)
        left = jnp.concatenate([own[2], near[2]], axis=0)
        outs[2][...] = dot(left, c[...], TN).astype(BF16)

    ins = [(act_t, act_t.shape, lambda j: (0, 0)), (cot, cot.shape, lambda j: (0, 0))]
    ins += [(p, (3, half, BLOCK), lambda j: (0, 0, j)) for p in parts]
    column = ((tile, units), BF16, (tile, BLOCK), lambda j: (0, base + j))
    outs = [column, column, ((units, tile), BF16, (BLOCK, tile), lambda j: (base + j, 0))]
    alias = {}
    if prev is not None:
        ins += [(p, (16, 128), lambda j: (0, 0)) for p in prev]
        alias = {lead + i: i for i in range(3)}
    return chain(body, (blocks,), ins, outs, flops=6 * tokens * tile * blocks * BLOCK, alias=alias)


def pass_on(chain, keep, got):
    slots = keep.shape[0]
    rest = keep.shape[1:]
    zeros = (0,) * len(rest)

    def body(k, g, *outs):
        for i in range(slots // 2):
            for out, s in zip(outs, (2 * i, 2 * i + 1)):
                out[i] = (k[s] + g[s].astype(F32)).astype(out.dtype)

    whole = ((slots, *rest), lambda j: (0, *zeros))
    half = ((slots // 2, *rest), lambda j: (0, *zeros))
    return chain(
        body,
        (1,),
        [(keep, *whole), (got, *whole)],
        [(half[0], dtype, *half) for dtype in (F32, BF16)],
    )


def finish(chain, me, halves, by_rows):
    four, rows, width = halves[0][0].shape[1:]
    tile = width * len(halves)

    def body(s, *refs):
        outs = refs[2 * len(halves) :]
        for h in range(len(halves)):
            total = refs[2 * h][0] + refs[2 * h + 1][0].astype(F32)
            columns = slice(h * width, (h + 1) * width)
            for i, g in enumerate(ORDER):
                rounded = total[i].astype(BF16)
                if by_rows:
                    outs[0][s[0] ^ g, :, columns] = rounded
                else:
                    outs[g][:, columns] = rounded

    ins = []
    for own, got in halves:
        ins += [(x, (1, four, rows, width), lambda j, s: (0, 0, 0, 0)) for x in (own, got)]
    if by_rows:
        outs = [((four, rows, tile), BF16, (four, rows, tile), lambda j, s: (0, 0, 0))]
    else:
        outs = [((rows, tile), BF16, (rows, tile), lambda j, s: (0, 0))] * 4
    res = chain(body, (1,), ins, outs, scalar=me)
    return res[0].reshape(four * rows, tile) if by_rows else res


def place_columns(chain, me, groups):
    rows, tile = groups[0].shape

    def body(s, *refs):
        for g in range(4):

            @pl.when(pl.program_id(0) == g)
            def _():
                refs[4][...] = refs[g][...]

    (out,) = chain(
        body,
        (4,),
        [(x, (rows, tile), lambda g, s: (0, 0)) for x in groups],
        [((rows, 4 * tile), BF16, (rows, tile), lambda g, s: (0, s[0] ^ g))],
        scalar=me,
    )
    return out


def spread(own):
    far = swap(own, 2)
    return [own, swap(own, 1), far, swap(far, 1)]


def chunk_sizes(total):
    small = max(1, total // 6)
    rest = total - 2 * small
    return [small, (rest + 1) // 2, rest // 2, small]


def local_eight(activations, cotangent, gate_proj, up_proj, down_proj):
    place = jnp.stack([lax.axis_index("narrow"), lax.axis_index("wide")]).astype(jnp.int32)
    rows = activations.shape[0]
    tile, units = gate_proj.shape
    sizes = chunk_sizes(units // BLOCK)
    chunks = [(sum(sizes[:c]), sizes[c]) for c in range(4)]
    backs = [chunks[0], chunks[1], (chunks[2][0], sizes[2] + sizes[3])]
    back_of = [(0, 0), (1, 0), (2, 0), (2, sizes[2])]
    chain = Chain()

    keep_b, got_b, far_b = {}, {}, {}
    keep_gu, got_gu, far_gu = {}, {}, {}
    own, near = {}, {}
    out = grad = grads = None

    def back(p):
        keep_b[p], send = back_part(chain, cot, down_proj, *backs[p])
        got_b[p] = swap(send, 1)

    def back_x(p):
        far_b[p] = swap(add_away(chain, keep_b[p], got_b[p]), 2)

    def gate_up(c):
        keep_gu[c], send = gate_up_part(chain, act, gate_proj, up_proj, *chunks[c])
        got_gu[c] = swap(send, 1)

    def gate_up_x(c):
        far_gu[c] = swap(add_away(chain, keep_gu[c], got_gu[c]), 2)

    def elementwise(c):
        p, off = back_of[c]
        own[c] = activate(
            chain, keep_gu[c], got_gu[c], far_gu[c], keep_b[p], got_b[p], far_b[p], off, sizes[c]
        )
        near[c] = swap(own[c], 1)

    def out_term():
        return (2, [down_proj], NN, out)

    def grad_term():
        return (0, [gate_proj, up_proj], NT, grad)

    def add_both(c):
        nonlocal out, grad
        out, grad = summed(chain, (own[c], near[c]), [out_term(), grad_term()], *chunks[c])

    def all_grads(c):
        nonlocal grads
        grads = gradients(chain, act_t, cot, (own[c], near[c]), *chunks[c], grads, units)

    def last_part(term, halves=1, half=0):
        keep, send = summed(chain, (own[3], near[3]), [term], *chunks[3], halves, half, True)
        return keep, swap_wide(send, 1)

    def over_z(pair, mask):
        keep, send = pass_on(chain, *pair)
        return keep, swap_wide(send, mask)

    def gather_z(mine):
        neighbour, across = swap_wide(mine, 2), swap_wide(mine, 4)
        return [mine, neighbour, across, swap_wide(across, 2)]

    cot_even, cot_first = gather_z(cotangent), swap_wide(cotangent, 1)
    chain.after(cot_first)
    tiles = cut_columns(chain, activations)
    tiles = lax.all_to_all(tiles, "narrow", split_axis=0, concat_axis=0, tiled=True)
    tiles = tiles.reshape(4 * rows, tile)
    act_even, act_first = gather_z(tiles), swap_wide(tiles, 1)
    act_odd = [swap_wide(x, 1) for x in act_even[1:]]
    chain.after(tiles, act_first)
    cot_odd = swap_wide(join(chain, cot_even[1:]), 1).reshape(12 * rows, tile)

    def slots(even, first, odd):
        res = [(even[0], 0), (first, 0)]
        for i in range(3):
            res += [(even[i + 1], 0), odd[i]]
        return [(x, functools.partial(lambda at, s: at, at)) for x, at in res]

    chain.after(*act_even[1:])
    cot_slots = slots(cot_even, cot_first, [(cot_odd, 4 * i) for i in range(3)])
    (cot,) = arrange(chain, place, cot_slots, rows, tile)
    back(0)
    chain.after(*act_odd)
    back(1)
    back_x(0)
    back(2)
    back_x(1)
    act_slots = slots(act_even, act_first, [(x, 0) for x in act_odd])
    act, act_t = arrange(chain, place, act_slots, rows, tile, True)
    chain.after(far_b[0])
    gate_up(0)
    back_x(2)
    chain.after(far_b[1], got_gu[0])
    gate_up(1)
    gate_up_x(0)
    chain.after(far_b[2])
    gate_up(2)
    gate_up_x(1)
    gate_up(3)
    gate_up_x(2)
    chain.after(got_gu[3])
    elementwise(0)
    gate_up_x(3)
    add_both(0)
    all_grads(0)
    elementwise(1)
    add_both(1)
    elementwise(2)
    add_both(2)
    elementwise(3)
    all_grads(1)
    grad_part = last_part(grad_term())
    out_parts = [last_part(out_term(), 2, 0), last_part(out_term(), 2, 1)]
    all_grads(2)
    grad_part = over_z(grad_part, 2)
    all_grads(3)
    out_parts[0] = over_z(out_parts[0], 2)
    grad_part = over_z(grad_part, 4)
    out_parts[1] = over_z(out_parts[1], 2)
    out_parts[0] = over_z(out_parts[0], 4)
    groups = finish(chain, place, [grad_part], False)
    groups = [groups[0]] + [swap(groups[g], g) for g in range(1, 4)]
    out_parts[1] = over_z(out_parts[1], 4)
    input_gradient = place_columns(chain, place, groups)
    block_output = finish(chain, place, out_parts, True)
    return (block_output, input_gradient, *grads)


def scatter_sum(part):
    split = part.reshape(-1, 4, part.shape[0] // 4 // lax.axis_size("wide"), part.shape[-1])
    got = swap(jnp.stack([split[:, 1], split[:, 3]]), 1)
    away = (split[:, 2] + got[1]).astype(BF16)
    return (split[:, 0] + got[0]) + swap(away, 2).astype(F32)


def spread_rows(own):
    return jnp.stack(spread(own), axis=1).reshape(-1, own.shape[-1])


def local_any(activations, cotangent, gate_proj, up_proj, down_proj):
    me = lax.axis_index("narrow")
    rows = activations.shape[0]
    tile = gate_proj.shape[0]
    pieces = [lax.dynamic_slice_in_dim(activations, (me ^ g) * tile, tile, 1) for g in range(4)]
    pieces = [pieces[0]] + [swap(pieces[g], g) for g in range(1, 4)]
    cots = [lax.dynamic_slice_in_dim(cotangent, (me ^ g) * rows, rows, 0) for g in range(4)]

    def gathered(parts):
        return lax.all_gather(jnp.stack(parts), "wide", axis=0, tiled=True).reshape(-1, tile)

    features, upstream = gathered(pieces), gathered(cots)
    gate = scatter_sum(dot(features, gate_proj, NN))
    up = scatter_sum(dot(features, up_proj, NN))
    back = scatter_sum(dot(upstream, down_proj, NT))
    active, slope = silu_parts(gate)
    gate_delta = spread_rows((back * up * slope).astype(BF16))
    up_delta = spread_rows((back * active).astype(BF16))
    hidden = spread_rows((active * up).astype(BF16))

    def landed(total):
        got = lax.psum_scatter(total, "wide", scatter_dimension=0, tiled=True)
        return got.astype(BF16).reshape(4, rows, tile)

    grad = landed(dot(gate_delta, gate_proj, NT) + dot(up_delta, up_proj, NT))
    out = landed(dot(hidden, down_proj, NN))
    gate_gradient = dot(features, gate_delta, TN).astype(BF16)
    up_gradient = dot(features, up_delta, TN).astype(BF16)
    down_gradient = dot(hidden, upstream, TN).astype(BF16)

    block_output = jnp.concatenate(
        [lax.dynamic_index_in_dim(out, me ^ g, 0, keepdims=False) for g in range(4)]
    )
    grads = jnp.stack([grad[0]] + [swap(grad[g], g) for g in range(1, 4)])
    input_gradient = jnp.concatenate(
        [lax.dynamic_index_in_dim(grads, me ^ g, 0, keepdims=False) for g in range(4)], axis=1
    )
    return (block_output, input_gradient, gate_gradient, up_gradient, down_gradient)


def local(activations, cotangent, gate_proj, up_proj, down_proj):
    args = (activations, cotangent, gate_proj, up_proj, down_proj)
    rows, (tile, units) = activations.shape[0], gate_proj.shape
    fits = lax.axis_size("wide") == 8 and rows % 16 == 0
    if fits and tile % (2 * BLOCK) == 0 and units % BLOCK == 0 and units >= 6 * BLOCK:
        return local_eight(*args)
    return local_any(*args)


def solution(mesh):
    placed = (
        P(("wide", "narrow"), None),
        P("wide", "narrow"),
        P("narrow", "wide"),
        P("narrow", "wide"),
        P("wide", "narrow"),
    )
    return jax.shard_map(
        local,
        mesh=mesh,
        in_specs=placed,
        out_specs=(
            P("wide", "narrow"),
            P(("wide", "narrow"), None),
            P("narrow", "wide"),
            P("narrow", "wide"),
            P("wide", "narrow"),
        ),
        check_vma=False,
    )
```

```python
import functools

import jax
import jax.numpy as jnp
from jax import lax
from jax.experimental import pallas as pl
from jax.experimental.pallas import tpu as pltpu
from jax.sharding import PartitionSpec as P

BF16, F32 = jnp.bfloat16, jnp.float32
BLOCK = 256
VMEM_LIMIT = 64 * 1024 * 1024 - 256 * 1024
ORDER = (0, 2, 1, 3)
NN = (((1,), (0,)), ((), ()))
NT = (((1,), (1,)), ((), ()))
TN = (((0,), (0,)), ((), ()))


def dot(left, right, dims):
    return lax.dot_general(left, right, dims, preferred_element_type=F32)


def silu_parts(gate):
    sigma = jax.nn.sigmoid(gate)
    return (gate * sigma, sigma * (1.0 + gate * (1.0 - sigma)))


def swap(value, mask):
    return lax.ppermute(value, "narrow", [(i, i ^ mask) for i in range(4)])


def swap_wide(value, mask):
    return lax.ppermute(value, "wide", [(i, i ^ mask) for i in range(8)])


class Chain:
    def __init__(self):
        self.token = None
        self.waits = []

    def after(self, *arrays):
        self.waits += arrays

    def __call__(self, body, grid, ins, outs, scratch=(), flops=0, alias=None, scalar=None):
        lead = 0 if scalar is None else 1
        arrays = [a for a, _, _ in ins]
        specs = [pl.BlockSpec(block, index) for _, block, index in ins]
        unread = self.waits + ([] if self.token is None else [self.token])
        self.waits = []
        arrays += unread
        specs += [pl.BlockSpec(memory_space=pltpu.HBM)] * len(unread)
        shapes = [jax.ShapeDtypeStruct(shape, dtype) for shape, dtype, _, _ in outs]
        out_specs = [pl.BlockSpec(block, index) for _, _, block, index in outs]
        shapes.append(jax.ShapeDtypeStruct((8, 128), F32))
        out_specs.append(pl.BlockSpec((8, 128), lambda *i: (0, 0)))
        n_in, n_out = len(ins), len(outs)

        def kernel(*refs):
            head, refs = refs[:lead], refs[lead:]
            in_refs = refs[:n_in]
            rest = refs[n_in + len(unread) :]
            out_refs, token, scratch_refs = rest[:n_out], rest[n_out], rest[n_out + 1 :]
            token[...] = jnp.zeros(token.shape, F32)
            body(*head, *in_refs, *out_refs, *scratch_refs)

        res = pl.pallas_call(
            kernel,
            grid_spec=pltpu.PrefetchScalarGridSpec(
                num_scalar_prefetch=lead,
                grid=grid,
                in_specs=specs,
                out_specs=out_specs,
                scratch_shapes=list(scratch),
            ),
            out_shape=shapes,
            input_output_aliases={k + lead: v for k, v in (alias or {}).items()},
            compiler_params=pltpu.CompilerParams(vmem_limit_bytes=VMEM_LIMIT),
            cost_estimate=pl.CostEstimate(flops=1, bytes_accessed=1, transcendentals=0),
        )(*(() if scalar is None else (scalar,)), *arrays)
        self.token = res[-1]
        return res[:-1]


def group(i):
    return (i & 1) * 2 + (i >> 1)


def cut_columns(chain, rows_in):
    rows, tile = rows_in.shape[0], rows_in.shape[1] // 4

    def body(x, out):
        out[0] = x[...]

    (out,) = chain(
        body,
        (4,),
        [(rows_in, (rows, tile), lambda j: (0, j))],
        [((4, rows, tile), BF16, (1, rows, tile), lambda j: (j, 0, 0))],
    )
    return out


def join(chain, parts):
    rows, tile = parts[0].shape
    count = len(parts)

    def body(*refs):
        for i in range(count):
            refs[count][i] = refs[i][...]

    (out,) = chain(
        body,
        (1,),
        [(p, (rows, tile), lambda j: (0, 0)) for p in parts],
        [((count, rows, tile), BF16, (count, rows, tile), lambda j: (0, 0, 0))],
    )
    return out


def arrange(chain, place, slots, rows, tile, turned=False):
    q = 8 * rows

    def body(_, *refs):
        out = refs[8]
        for k in range(8):
            out[0, k] = refs[k][...]
        if turned:
            refs[9][...] = out[0].reshape(q, tile).T

    outs = [((4, 8, rows, tile), BF16, (1, 8, rows, tile), lambda g, s: (g, 0, 0, 0))]
    if turned:
        outs.append(((tile, 4 * q), BF16, (tile, q), lambda g, s: (0, g)))
    out, *rest = chain(
        body,
        (4,),
        [
            (p, (rows, tile), functools.partial(lambda at, i, s: (at(s) + (s[0] ^ group(i)), 0), at))
            for p, at in slots
        ],
        outs,
        scalar=place,
    )
    return [out.reshape(4 * q, tile), *rest]


def back_part(chain, cot, down, base, blocks):
    tokens, tile = cot.shape
    half, n = tokens // 2, blocks * BLOCK

    def body(c, w, keep, send):
        acc = dot(c[...], w[...], NT)
        keep[...] = acc[:half]
        send[...] = acc[half:].astype(BF16)

    block, at = (half, BLOCK), lambda j: (0, j)
    outs = [((half, n), dtype, block, at) for dtype in (F32, BF16)]
    return chain(
        body,
        (blocks,),
        [(cot, cot.shape, lambda j: (0, 0)), (down, (BLOCK, tile), lambda j: (base + j, 0))],
        outs,
        flops=2 * tokens * tile * n,
    )


def gate_up_part(chain, act, gate, up, base, blocks):
    tokens, tile = act.shape
    half, n = tokens // 2, blocks * BLOCK

    def body(a, wg, wu, keep, send):
        for k, w in enumerate((wg, wu)):
            acc = dot(a[...], w[...], NN)
            keep[k] = acc[:half]
            send[k] = acc[half:].astype(BF16)

    weight = ((tile, BLOCK), lambda j: (0, base + j))
    block, at = (2, half, BLOCK), lambda j: (0, 0, j)
    outs = [((2, half, n), dtype, block, at) for dtype in (F32, BF16)]
    return chain(
        body,
        (blocks,),
        [(act, act.shape, lambda j: (0, 0)), (gate, *weight), (up, *weight)],
        outs,
        flops=4 * tokens * tile * n,
    )


def add_away(chain, keep, got):
    lead, (half, n) = keep.shape[:-2], keep.shape[-2:]
    zeros = (0,) * len(lead)
    block = (*lead, half // 2, n)

    def body(a, b, out):
        out[...] = (a[...] + b[...].astype(F32)).astype(BF16)

    (out,) = chain(
        body,
        (2,),
        [(x, block, lambda i: (*zeros, 1 - i, 0)) for x in (keep, got)],
        [(keep.shape, BF16, block, lambda i: (*zeros, i, 0))],
    )
    return out


def activate(chain, keep_gu, got_gu, far_gu, keep_b, got_b, far_b, off, blocks):
    half, n = far_gu.shape[1:]
    q = half // 2

    def body(kg, gg, fg, kb, gb, fb, out):
        gate = kg[0] + gg[0].astype(F32) + fg[0].astype(F32)
        up = kg[1] + gg[1].astype(F32) + fg[1].astype(F32)
        back = kb[...] + gb[...].astype(F32) + fb[...].astype(F32)
        active, slope = silu_parts(gate)
        out[0] = (back * up * slope).astype(BF16)
        out[1] = (back * active).astype(BF16)
        out[2] = (active * up).astype(BF16)

    two = ((2, half, BLOCK), lambda j: (0, 0, j))
    one = ((half, BLOCK), lambda j: (0, off + j))
    (out,) = chain(
        body,
        (n // BLOCK,),
        [(x, *two) for x in (keep_gu, got_gu, far_gu)] + [(x, *one) for x in (keep_b, got_b, far_b)],
        [((3, half, n), BF16, (3, half, BLOCK), lambda j: (0, 0, j))],
    )
    return out


def split_slots(acc, rows, keep, send):
    view = acc.reshape(4, 8, rows, acc.shape[-1])
    for s in range(4):
        keep[s] = view[:, 2 * s]
        send[s] = view[:, 2 * s + 1].astype(BF16)


def summed(chain, parts, terms, base, blocks, halves=1, half=0, split=False):
    kinds = parts[0].shape[0]
    half_rows, n = parts[0].shape[1:]
    q = half_rows // 2
    rows = q // 8
    first_weight, dims = terms[0][1][0], terms[0][2]
    tile = first_weight.shape[1 if dims is NN else 0]
    width = tile // halves
    step = min(2 * BLOCK, width)
    off = half * (width // step)
    ins = [(p, p.shape, lambda j: (0, 0, 0)) for p in parts]
    outs, alias, plan = [], {}, []
    for first, weights, dims, prev in terms:
        refs = []
        for w in weights:
            for i in range(blocks):
                refs.append(len(ins))
                if dims is NN:
                    index = functools.partial(lambda i, j: (base + i, off + j), i)
                    ins.append((w, (BLOCK, step), index))
                else:
                    index = functools.partial(lambda i, j: (off + j, base + i), i)
                    ins.append((w, (step, BLOCK), index))
        before = None
        if prev is not None:
            before = len(ins)
            ins.append((prev, (4 * q, step), lambda j: (0, off + j)))
            if not split:
                alias[before] = len(outs)
        plan.append((first, len(weights), dims, refs, before, len(outs)))
        if split:
            shape, block = (4, 4, rows, width), (4, 4, rows, step)
            outs.append((shape, F32, block, lambda j: (0, 0, 0, j)))
            outs.append((shape, BF16, block, lambda j: (0, 0, 0, j)))
        else:
            outs.append(((4 * q, tile), F32, (4 * q, step), lambda j: (0, j)))
    n_in = len(ins)

    def body(*refs):
        out_refs, scratch = refs[n_in:-1], refs[-1]

        @pl.when(pl.program_id(0) == 0)
        def _():
            for g in range(2):
                for k in range(kinds):
                    scratch[k, g * half_rows : (g + 1) * half_rows] = refs[g][k]

        for first, count, dims, at, before, out in plan:
            total = None if before is None else refs[before][...]
            for k in range(count):
                for i in range(blocks):
                    left = scratch[first + k, :, i * BLOCK : (i + 1) * BLOCK]
                    term = dot(left, refs[at[k * blocks + i]][...], dims)
                    total = term if total is None else total + term
            if split:
                split_slots(total, rows, out_refs[out], out_refs[out + 1])
            else:
                out_refs[out][...] = total

    return chain(
        body,
        (width // step,),
        ins,
        outs,
        scratch=[pltpu.VMEM((kinds, 4 * q, n), BF16)],
        flops=6 * 4 * q * n * width,
        alias=alias,
    )


def gradients(chain, act_t, cot, parts, base, blocks, prev, units):
    tile, tokens = act_t.shape
    half = tokens // 2
    lead = 4

    def body(*refs):
        a, c, own, near = refs[:lead]
        outs = refs[-3:]
        for k in range(2):
            right = jnp.concatenate([own[k], near[k]], axis=0)
            outs[k][...] = dot(a[...], right, NN).astype(BF16)
        left = jnp.concatenate([own[2], near[2]], axis=0)
        outs[2][...] = dot(left, c[...], TN).astype(BF16)

    ins = [(act_t, act_t.shape, lambda j: (0, 0)), (cot, cot.shape, lambda j: (0, 0))]
    ins += [(p, (3, half, BLOCK), lambda j: (0, 0, j)) for p in parts]
    column = ((tile, units), BF16, (tile, BLOCK), lambda j: (0, base + j))
    outs = [column, column, ((units, tile), BF16, (BLOCK, tile), lambda j: (base + j, 0))]
    alias = {}
    if prev is not None:
        ins += [(p, (16, 128), lambda j: (0, 0)) for p in prev]
        alias = {lead + i: i for i in range(3)}
    return chain(body, (blocks,), ins, outs, flops=6 * tokens * tile * blocks * BLOCK, alias=alias)


def pass_on(chain, keep, got):
    slots = keep.shape[0]
    rest = keep.shape[1:]
    zeros = (0,) * len(rest)

    def body(k, g, *outs):
        for i in range(slots // 2):
            for out, s in zip(outs, (2 * i, 2 * i + 1)):
                out[i] = (k[s] + g[s].astype(F32)).astype(out.dtype)

    whole = ((slots, *rest), lambda j: (0, *zeros))
    half = ((slots // 2, *rest), lambda j: (0, *zeros))
    return chain(
        body,
        (1,),
        [(keep, *whole), (got, *whole)],
        [(half[0], dtype, *half) for dtype in (F32, BF16)],
    )


def finish(chain, me, halves, by_rows):
    four, rows, width = halves[0][0].shape[1:]
    tile = width * len(halves)

    def body(s, *refs):
        outs = refs[2 * len(halves) :]
        for h in range(len(halves)):
            total = refs[2 * h][0] + refs[2 * h + 1][0].astype(F32)
            columns = slice(h * width, (h + 1) * width)
            for i, g in enumerate(ORDER):
                rounded = total[i].astype(BF16)
                if by_rows:
                    outs[0][s[0] ^ g, :, columns] = rounded
                else:
                    outs[g][:, columns] = rounded

    ins = []
    for own, got in halves:
        ins += [(x, (1, four, rows, width), lambda j, s: (0, 0, 0, 0)) for x in (own, got)]
    if by_rows:
        outs = [((four, rows, tile), BF16, (four, rows, tile), lambda j, s: (0, 0, 0))]
    else:
        outs = [((rows, tile), BF16, (rows, tile), lambda j, s: (0, 0))] * 4
    res = chain(body, (1,), ins, outs, scalar=me)
    return res[0].reshape(four * rows, tile) if by_rows else res


def place_columns(chain, me, groups):
    rows, tile = groups[0].shape

    def body(s, *refs):
        for g in range(4):

            @pl.when(pl.program_id(0) == g)
            def _():
                refs[4][...] = refs[g][...]

    (out,) = chain(
        body,
        (4,),
        [(x, (rows, tile), lambda g, s: (0, 0)) for x in groups],
        [((rows, 4 * tile), BF16, (rows, tile), lambda g, s: (0, s[0] ^ g))],
        scalar=me,
    )
    return out


def spread(own):
    far = swap(own, 2)
    return [own, swap(own, 1), far, swap(far, 1)]


def chunk_sizes(total):
    small = max(1, total // 6)
    rest = total - 2 * small
    return [small, (rest + 1) // 2, rest // 2, small]


def local_eight(activations, cotangent, gate_proj, up_proj, down_proj):
    place = jnp.stack([lax.axis_index("narrow"), lax.axis_index("wide")]).astype(jnp.int32)
    rows = activations.shape[0]
    tile, units = gate_proj.shape
    sizes = chunk_sizes(units // BLOCK)
    chunks = [(sum(sizes[:c]), sizes[c]) for c in range(4)]
    backs = [chunks[0], chunks[1], (chunks[2][0], sizes[2] + sizes[3])]
    back_of = [(0, 0), (1, 0), (2, 0), (2, sizes[2])]
    chain = Chain()

    keep_b, got_b, far_b = {}, {}, {}
    keep_gu, got_gu, far_gu = {}, {}, {}
    own, near = {}, {}
    out = grad = grads = None

    def back(p):
        keep_b[p], send = back_part(chain, cot, down_proj, *backs[p])
        got_b[p] = swap(send, 1)

    def back_x(p):
        far_b[p] = swap(add_away(chain, keep_b[p], got_b[p]), 2)

    def gate_up(c):
        keep_gu[c], send = gate_up_part(chain, act, gate_proj, up_proj, *chunks[c])
        got_gu[c] = swap(send, 1)

    def gate_up_x(c):
        far_gu[c] = swap(add_away(chain, keep_gu[c], got_gu[c]), 2)

    def elementwise(c):
        p, off = back_of[c]
        own[c] = activate(
            chain, keep_gu[c], got_gu[c], far_gu[c], keep_b[p], got_b[p], far_b[p], off, sizes[c]
        )
        near[c] = swap(own[c], 1)

    def out_term():
        return (2, [down_proj], NN, out)

    def grad_term():
        return (0, [gate_proj, up_proj], NT, grad)

    def add_both(c):
        nonlocal out, grad
        out, grad = summed(chain, (own[c], near[c]), [out_term(), grad_term()], *chunks[c])

    def all_grads(c):
        nonlocal grads
        grads = gradients(chain, act_t, cot, (own[c], near[c]), *chunks[c], grads, units)

    def last_part(term, halves=1, half=0):
        keep, send = summed(chain, (own[3], near[3]), [term], *chunks[3], halves, half, True)
        return keep, swap_wide(send, 1)

    def over_z(pair, mask):
        keep, send = pass_on(chain, *pair)
        return keep, swap_wide(send, mask)

    def gather_z(mine):
        neighbour, across = swap_wide(mine, 2), swap_wide(mine, 4)
        return [mine, neighbour, across, swap_wide(across, 2)]

    cot_even, cot_first = gather_z(cotangent), swap_wide(cotangent, 1)
    chain.after(cot_first)
    tiles = cut_columns(chain, activations)
    tiles = lax.all_to_all(tiles, "narrow", split_axis=0, concat_axis=0, tiled=True)
    tiles = tiles.reshape(4 * rows, tile)
    act_even, act_first = gather_z(tiles), swap_wide(tiles, 1)
    act_odd = [swap_wide(x, 1) for x in act_even[1:]]
    chain.after(tiles, act_first)
    cot_odd = swap_wide(join(chain, cot_even[1:]), 1).reshape(12 * rows, tile)

    def slots(even, first, odd):
        res = [(even[0], 0), (first, 0)]
        for i in range(3):
            res += [(even[i + 1], 0), odd[i]]
        return [(x, functools.partial(lambda at, s: at, at)) for x, at in res]

    chain.after(*act_even[1:])
    cot_slots = slots(cot_even, cot_first, [(cot_odd, 4 * i) for i in range(3)])
    (cot,) = arrange(chain, place, cot_slots, rows, tile)
    back(0)
    chain.after(*act_odd)
    back(1)
    back_x(0)
    back(2)
    back_x(1)
    act_slots = slots(act_even, act_first, [(x, 0) for x in act_odd])
    act, act_t = arrange(chain, place, act_slots, rows, tile, True)
    chain.after(far_b[0])
    gate_up(0)
    back_x(2)
    chain.after(far_b[1], got_gu[0])
    gate_up(1)
    gate_up_x(0)
    chain.after(far_b[2])
    gate_up(2)
    gate_up_x(1)
    gate_up(3)
    gate_up_x(2)
    chain.after(got_gu[3])
    elementwise(0)
    gate_up_x(3)
    add_both(0)
    all_grads(0)
    elementwise(1)
    add_both(1)
    elementwise(2)
    add_both(2)
    elementwise(3)
    grad_part = last_part(grad_term())
    out_parts = [last_part(out_term(), 2, 0), last_part(out_term(), 2, 1)]
    all_grads(1)
    grad_part = over_z(grad_part, 2)
    all_grads(2)
    out_parts[0] = over_z(out_parts[0], 2)
    grad_part = over_z(grad_part, 4)
    out_parts[1] = over_z(out_parts[1], 2)
    out_parts[0] = over_z(out_parts[0], 4)
    all_grads(3)
    groups = finish(chain, place, [grad_part], False)
    groups = [groups[0]] + [swap(groups[g], g) for g in range(1, 4)]
    out_parts[1] = over_z(out_parts[1], 4)
    input_gradient = place_columns(chain, place, groups)
    block_output = finish(chain, place, out_parts, True)
    return (block_output, input_gradient, *grads)


def scatter_sum(part):
    split = part.reshape(-1, 4, part.shape[0] // 4 // lax.axis_size("wide"), part.shape[-1])
    got = swap(jnp.stack([split[:, 1], split[:, 3]]), 1)
    away = (split[:, 2] + got[1]).astype(BF16)
    return (split[:, 0] + got[0]) + swap(away, 2).astype(F32)


def spread_rows(own):
    return jnp.stack(spread(own), axis=1).reshape(-1, own.shape[-1])


def local_any(activations, cotangent, gate_proj, up_proj, down_proj):
    me = lax.axis_index("narrow")
    rows = activations.shape[0]
    tile = gate_proj.shape[0]
    pieces = [lax.dynamic_slice_in_dim(activations, (me ^ g) * tile, tile, 1) for g in range(4)]
    pieces = [pieces[0]] + [swap(pieces[g], g) for g in range(1, 4)]
    cots = [lax.dynamic_slice_in_dim(cotangent, (me ^ g) * rows, rows, 0) for g in range(4)]

    def gathered(parts):
        return lax.all_gather(jnp.stack(parts), "wide", axis=0, tiled=True).reshape(-1, tile)

    features, upstream = gathered(pieces), gathered(cots)
    gate = scatter_sum(dot(features, gate_proj, NN))
    up = scatter_sum(dot(features, up_proj, NN))
    back = scatter_sum(dot(upstream, down_proj, NT))
    active, slope = silu_parts(gate)
    gate_delta = spread_rows((back * up * slope).astype(BF16))
    up_delta = spread_rows((back * active).astype(BF16))
    hidden = spread_rows((active * up).astype(BF16))

    def landed(total):
        got = lax.psum_scatter(total, "wide", scatter_dimension=0, tiled=True)
        return got.astype(BF16).reshape(4, rows, tile)

    grad = landed(dot(gate_delta, gate_proj, NT) + dot(up_delta, up_proj, NT))
    out = landed(dot(hidden, down_proj, NN))
    gate_gradient = dot(features, gate_delta, TN).astype(BF16)
    up_gradient = dot(features, up_delta, TN).astype(BF16)
    down_gradient = dot(hidden, upstream, TN).astype(BF16)

    block_output = jnp.concatenate(
        [lax.dynamic_index_in_dim(out, me ^ g, 0, keepdims=False) for g in range(4)]
    )
    grads = jnp.stack([grad[0]] + [swap(grad[g], g) for g in range(1, 4)])
    input_gradient = jnp.concatenate(
        [lax.dynamic_index_in_dim(grads, me ^ g, 0, keepdims=False) for g in range(4)], axis=1
    )
    return (block_output, input_gradient, gate_gradient, up_gradient, down_gradient)


def local(activations, cotangent, gate_proj, up_proj, down_proj):
    args = (activations, cotangent, gate_proj, up_proj, down_proj)
    rows, (tile, units) = activations.shape[0], gate_proj.shape
    fits = lax.axis_size("wide") == 8 and rows % 16 == 0
    if fits and tile % (2 * BLOCK) == 0 and units % BLOCK == 0 and units >= 6 * BLOCK:
        return local_eight(*args)
    return local_any(*args)


def solution(mesh):
    placed = (
        P(("wide", "narrow"), None),
        P("wide", "narrow"),
        P("narrow", "wide"),
        P("narrow", "wide"),
        P("wide", "narrow"),
    )
    return jax.shard_map(
        local,
        mesh=mesh,
        in_specs=placed,
        out_specs=(
            P("wide", "narrow"),
            P(("wide", "narrow"), None),
            P("narrow", "wide"),
            P("narrow", "wide"),
            P("wide", "narrow"),
        ),
        check_vma=False,
    )
```

```python
import functools

import jax
import jax.numpy as jnp
from jax import lax
from jax.experimental import pallas as pl
from jax.experimental.pallas import tpu as pltpu
from jax.sharding import PartitionSpec as P

BF16, F32 = jnp.bfloat16, jnp.float32
BLOCK = 256
VMEM_LIMIT = 64 * 1024 * 1024 - 256 * 1024
ORDER = (0, 2, 1, 3)
NN = (((1,), (0,)), ((), ()))
NT = (((1,), (1,)), ((), ()))
TN = (((0,), (0,)), ((), ()))


def dot(left, right, dims):
    return lax.dot_general(left, right, dims, preferred_element_type=F32)


def silu_parts(gate):
    sigma = jax.nn.sigmoid(gate)
    return (gate * sigma, sigma * (1.0 + gate * (1.0 - sigma)))


def swap(value, mask):
    return lax.ppermute(value, "narrow", [(i, i ^ mask) for i in range(4)])


def swap_wide(value, mask):
    return lax.ppermute(value, "wide", [(i, i ^ mask) for i in range(8)])


class Chain:
    def __init__(self):
        self.token = None
        self.waits = []

    def after(self, *arrays):
        self.waits += arrays

    def __call__(self, body, grid, ins, outs, scratch=(), flops=0, alias=None, scalar=None):
        lead = 0 if scalar is None else 1
        arrays = [a for a, _, _ in ins]
        specs = [pl.BlockSpec(block, index) for _, block, index in ins]
        unread = self.waits + ([] if self.token is None else [self.token])
        self.waits = []
        arrays += unread
        specs += [pl.BlockSpec(memory_space=pltpu.HBM)] * len(unread)
        shapes = [jax.ShapeDtypeStruct(shape, dtype) for shape, dtype, _, _ in outs]
        out_specs = [pl.BlockSpec(block, index) for _, _, block, index in outs]
        shapes.append(jax.ShapeDtypeStruct((8, 128), F32))
        out_specs.append(pl.BlockSpec((8, 128), lambda *i: (0, 0)))
        n_in, n_out = len(ins), len(outs)

        def kernel(*refs):
            head, refs = refs[:lead], refs[lead:]
            in_refs = refs[:n_in]
            rest = refs[n_in + len(unread) :]
            out_refs, token, scratch_refs = rest[:n_out], rest[n_out], rest[n_out + 1 :]
            token[...] = jnp.zeros(token.shape, F32)
            body(*head, *in_refs, *out_refs, *scratch_refs)

        res = pl.pallas_call(
            kernel,
            grid_spec=pltpu.PrefetchScalarGridSpec(
                num_scalar_prefetch=lead,
                grid=grid,
                in_specs=specs,
                out_specs=out_specs,
                scratch_shapes=list(scratch),
            ),
            out_shape=shapes,
            input_output_aliases={k + lead: v for k, v in (alias or {}).items()},
            compiler_params=pltpu.CompilerParams(vmem_limit_bytes=VMEM_LIMIT),
            cost_estimate=pl.CostEstimate(flops=1, bytes_accessed=1, transcendentals=0),
        )(*(() if scalar is None else (scalar,)), *arrays)
        self.token = res[-1]
        return res[:-1]


def group(i):
    return (i & 1) * 2 + (i >> 1)


def cut_columns(chain, rows_in):
    rows, tile = rows_in.shape[0], rows_in.shape[1] // 4

    def body(x, out):
        out[0] = x[...]

    (out,) = chain(
        body,
        (4,),
        [(rows_in, (rows, tile), lambda j: (0, j))],
        [((4, rows, tile), BF16, (1, rows, tile), lambda j: (j, 0, 0))],
    )
    return out


def join(chain, parts):
    rows, tile = parts[0].shape
    count = len(parts)

    def body(*refs):
        for i in range(count):
            refs[count][i] = refs[i][...]

    (out,) = chain(
        body,
        (1,),
        [(p, (rows, tile), lambda j: (0, 0)) for p in parts],
        [((count, rows, tile), BF16, (count, rows, tile), lambda j: (0, 0, 0))],
    )
    return out


def arrange(chain, place, slots, rows, tile, turned=False):
    q = 8 * rows

    def body(_, *refs):
        out = refs[8]
        for k in range(8):
            out[0, k] = refs[k][...]
        if turned:
            refs[9][...] = out[0].reshape(q, tile).T

    outs = [((4, 8, rows, tile), BF16, (1, 8, rows, tile), lambda g, s: (g, 0, 0, 0))]
    if turned:
        outs.append(((tile, 4 * q), BF16, (tile, q), lambda g, s: (0, g)))
    out, *rest = chain(
        body,
        (4,),
        [
            (p, (rows, tile), functools.partial(lambda at, i, s: (at(s) + (s[0] ^ group(i)), 0), at))
            for p, at in slots
        ],
        outs,
        scalar=place,
    )
    return [out.reshape(4 * q, tile), *rest]


def back_part(chain, cot, down, base, blocks):
    tokens, tile = cot.shape
    half, n = tokens // 2, blocks * BLOCK

    def body(c, w, keep, send):
        acc = dot(c[...], w[...], NT)
        keep[...] = acc[:half]
        send[...] = acc[half:].astype(BF16)

    block, at = (half, BLOCK), lambda j: (0, j)
    outs = [((half, n), dtype, block, at) for dtype in (F32, BF16)]
    return chain(
        body,
        (blocks,),
        [(cot, cot.shape, lambda j: (0, 0)), (down, (BLOCK, tile), lambda j: (base + j, 0))],
        outs,
        flops=2 * tokens * tile * n,
    )


def gate_up_part(chain, act, gate, up, base, blocks):
    tokens, tile = act.shape
    half, n = tokens // 2, blocks * BLOCK

    def body(a, wg, wu, keep, send):
        for k, w in enumerate((wg, wu)):
            acc = dot(a[...], w[...], NN)
            keep[k] = acc[:half]
            send[k] = acc[half:].astype(BF16)

    weight = ((tile, BLOCK), lambda j: (0, base + j))
    block, at = (2, half, BLOCK), lambda j: (0, 0, j)
    outs = [((2, half, n), dtype, block, at) for dtype in (F32, BF16)]
    return chain(
        body,
        (blocks,),
        [(act, act.shape, lambda j: (0, 0)), (gate, *weight), (up, *weight)],
        outs,
        flops=4 * tokens * tile * n,
    )


def add_away(chain, keep, got):
    lead, (half, n) = keep.shape[:-2], keep.shape[-2:]
    zeros = (0,) * len(lead)
    block = (*lead, half // 2, n)

    def body(a, b, out):
        out[...] = (a[...] + b[...].astype(F32)).astype(BF16)

    (out,) = chain(
        body,
        (2,),
        [(x, block, lambda i: (*zeros, 1 - i, 0)) for x in (keep, got)],
        [(keep.shape, BF16, block, lambda i: (*zeros, i, 0))],
    )
    return out


def activate(chain, keep_gu, got_gu, far_gu, keep_b, got_b, far_b, off, blocks):
    half, n = far_gu.shape[1:]
    q = half // 2

    def body(kg, gg, fg, kb, gb, fb, out):
        gate = kg[0] + gg[0].astype(F32) + fg[0].astype(F32)
        up = kg[1] + gg[1].astype(F32) + fg[1].astype(F32)
        back = kb[...] + gb[...].astype(F32) + fb[...].astype(F32)
        active, slope = silu_parts(gate)
        out[0] = (back * up * slope).astype(BF16)
        out[1] = (back * active).astype(BF16)
        out[2] = (active * up).astype(BF16)

    two = ((2, half, BLOCK), lambda j: (0, 0, j))
    one = ((half, BLOCK), lambda j: (0, off + j))
    (out,) = chain(
        body,
        (n // BLOCK,),
        [(x, *two) for x in (keep_gu, got_gu, far_gu)] + [(x, *one) for x in (keep_b, got_b, far_b)],
        [((3, half, n), BF16, (3, half, BLOCK), lambda j: (0, 0, j))],
    )
    return out


def split_slots(acc, rows, keep, send):
    view = acc.reshape(4, 8, rows, acc.shape[-1])
    for s in range(4):
        keep[s] = view[:, 2 * s]
        send[s] = view[:, 2 * s + 1].astype(BF16)


def summed(chain, parts, terms, base, blocks, halves=1, half=0, split=False):
    kinds = parts[0].shape[0]
    half_rows, n = parts[0].shape[1:]
    q = half_rows // 2
    rows = q // 8
    first_weight, dims = terms[0][1][0], terms[0][2]
    tile = first_weight.shape[1 if dims is NN else 0]
    width = tile // halves
    step = min(2 * BLOCK, width)
    off = half * (width // step)
    ins = [(p, p.shape, lambda j: (0, 0, 0)) for p in parts]
    outs, alias, plan = [], {}, []
    for first, weights, dims, prev in terms:
        refs = []
        for w in weights:
            for i in range(blocks):
                refs.append(len(ins))
                if dims is NN:
                    index = functools.partial(lambda i, j: (base + i, off + j), i)
                    ins.append((w, (BLOCK, step), index))
                else:
                    index = functools.partial(lambda i, j: (off + j, base + i), i)
                    ins.append((w, (step, BLOCK), index))
        before = None
        if prev is not None:
            before = len(ins)
            ins.append((prev, (4 * q, step), lambda j: (0, off + j)))
            if not split:
                alias[before] = len(outs)
        plan.append((first, len(weights), dims, refs, before, len(outs)))
        if split:
            shape, block = (4, 4, rows, width), (4, 4, rows, step)
            outs.append((shape, F32, block, lambda j: (0, 0, 0, j)))
            outs.append((shape, BF16, block, lambda j: (0, 0, 0, j)))
        else:
            outs.append(((4 * q, tile), F32, (4 * q, step), lambda j: (0, j)))
    n_in = len(ins)

    def body(*refs):
        out_refs, scratch = refs[n_in:-1], refs[-1]

        @pl.when(pl.program_id(0) == 0)
        def _():
            for g in range(2):
                for k in range(kinds):
                    scratch[k, g * half_rows : (g + 1) * half_rows] = refs[g][k]

        for first, count, dims, at, before, out in plan:
            total = None if before is None else refs[before][...]
            for k in range(count):
                for i in range(blocks):
                    left = scratch[first + k, :, i * BLOCK : (i + 1) * BLOCK]
                    term = dot(left, refs[at[k * blocks + i]][...], dims)
                    total = term if total is None else total + term
            if split:
                split_slots(total, rows, out_refs[out], out_refs[out + 1])
            else:
                out_refs[out][...] = total

    return chain(
        body,
        (width // step,),
        ins,
        outs,
        scratch=[pltpu.VMEM((kinds, 4 * q, n), BF16)],
        flops=6 * 4 * q * n * width,
        alias=alias,
    )


def gradients(chain, act_t, cot, parts, base, blocks, prev, units):
    tile, tokens = act_t.shape
    half = tokens // 2
    lead = 4

    def body(*refs):
        a, c, own, near = refs[:lead]
        outs = refs[-3:]
        for k in range(2):
            right = jnp.concatenate([own[k], near[k]], axis=0)
            outs[k][...] = dot(a[...], right, NN).astype(BF16)
        left = jnp.concatenate([own[2], near[2]], axis=0)
        outs[2][...] = dot(left, c[...], TN).astype(BF16)

    ins = [(act_t, act_t.shape, lambda j: (0, 0)), (cot, cot.shape, lambda j: (0, 0))]
    ins += [(p, (3, half, BLOCK), lambda j: (0, 0, j)) for p in parts]
    column = ((tile, units), BF16, (tile, BLOCK), lambda j: (0, base + j))
    outs = [column, column, ((units, tile), BF16, (BLOCK, tile), lambda j: (base + j, 0))]
    alias = {}
    if prev is not None:
        ins += [(p, (16, 128), lambda j: (0, 0)) for p in prev]
        alias = {lead + i: i for i in range(3)}
    return chain(body, (blocks,), ins, outs, flops=6 * tokens * tile * blocks * BLOCK, alias=alias)


def pass_on(chain, keep, got):
    slots = keep.shape[0]
    rest = keep.shape[1:]
    zeros = (0,) * len(rest)

    def body(k, g, *outs):
        for i in range(slots // 2):
            for out, s in zip(outs, (2 * i, 2 * i + 1)):
                out[i] = (k[s] + g[s].astype(F32)).astype(out.dtype)

    whole = ((slots, *rest), lambda j: (0, *zeros))
    half = ((slots // 2, *rest), lambda j: (0, *zeros))
    return chain(
        body,
        (1,),
        [(keep, *whole), (got, *whole)],
        [(half[0], dtype, *half) for dtype in (F32, BF16)],
    )


def finish(chain, me, halves, by_rows):
    four, rows, width = halves[0][0].shape[1:]
    tile = width * len(halves)

    def body(s, *refs):
        outs = refs[2 * len(halves) :]
        for h in range(len(halves)):
            total = refs[2 * h][0] + refs[2 * h + 1][0].astype(F32)
            columns = slice(h * width, (h + 1) * width)
            for i, g in enumerate(ORDER):
                rounded = total[i].astype(BF16)
                if by_rows:
                    outs[0][s[0] ^ g, :, columns] = rounded
                else:
                    outs[g][:, columns] = rounded

    ins = []
    for own, got in halves:
        ins += [(x, (1, four, rows, width), lambda j, s: (0, 0, 0, 0)) for x in (own, got)]
    if by_rows:
        outs = [((four, rows, tile), BF16, (four, rows, tile), lambda j, s: (0, 0, 0))]
    else:
        outs = [((rows, tile), BF16, (rows, tile), lambda j, s: (0, 0))] * 4
    res = chain(body, (1,), ins, outs, scalar=me)
    return res[0].reshape(four * rows, tile) if by_rows else res


def place_columns(chain, me, groups):
    rows, tile = groups[0].shape

    def body(s, *refs):
        for g in range(4):

            @pl.when(pl.program_id(0) == g)
            def _():
                refs[4][...] = refs[g][...]

    (out,) = chain(
        body,
        (4,),
        [(x, (rows, tile), lambda g, s: (0, 0)) for x in groups],
        [((rows, 4 * tile), BF16, (rows, tile), lambda g, s: (0, s[0] ^ g))],
        scalar=me,
    )
    return out


def spread(own):
    far = swap(own, 2)
    return [own, swap(own, 1), far, swap(far, 1)]


def chunk_sizes(total):
    small = max(1, total // 6)
    rest = total - 2 * small
    return [small, (rest + 1) // 2, rest // 2, small]


def local_eight(activations, cotangent, gate_proj, up_proj, down_proj):
    place = jnp.stack([lax.axis_index("narrow"), lax.axis_index("wide")]).astype(jnp.int32)
    rows = activations.shape[0]
    tile, units = gate_proj.shape
    sizes = chunk_sizes(units // BLOCK)
    chunks = [(sum(sizes[:c]), sizes[c]) for c in range(4)]
    backs = [chunks[0], chunks[1], (chunks[2][0], sizes[2] + sizes[3])]
    back_of = [(0, 0), (1, 0), (2, 0), (2, sizes[2])]
    chain = Chain()

    keep_b, got_b, far_b = {}, {}, {}
    keep_gu, got_gu, far_gu = {}, {}, {}
    own, near = {}, {}
    out = grad = grads = None

    def back(p):
        keep_b[p], send = back_part(chain, cot, down_proj, *backs[p])
        got_b[p] = swap(send, 1)

    def back_x(p):
        far_b[p] = swap(add_away(chain, keep_b[p], got_b[p]), 2)

    def gate_up(c):
        keep_gu[c], send = gate_up_part(chain, act, gate_proj, up_proj, *chunks[c])
        got_gu[c] = swap(send, 1)

    def gate_up_x(c):
        far_gu[c] = swap(add_away(chain, keep_gu[c], got_gu[c]), 2)

    def elementwise(c):
        p, off = back_of[c]
        own[c] = activate(
            chain, keep_gu[c], got_gu[c], far_gu[c], keep_b[p], got_b[p], far_b[p], off, sizes[c]
        )
        near[c] = swap(own[c], 1)

    def out_term():
        return (2, [down_proj], NN, out)

    def grad_term():
        return (0, [gate_proj, up_proj], NT, grad)

    def add_both(c):
        nonlocal out, grad
        out, grad = summed(chain, (own[c], near[c]), [out_term(), grad_term()], *chunks[c])

    def all_grads(c):
        nonlocal grads
        grads = gradients(chain, act_t, cot, (own[c], near[c]), *chunks[c], grads, units)

    def last_part(term, halves=1, half=0):
        keep, send = summed(chain, (own[3], near[3]), [term], *chunks[3], halves, half, True)
        return keep, swap_wide(send, 1)

    def over_z(pair, mask):
        keep, send = pass_on(chain, *pair)
        return keep, swap_wide(send, mask)

    def gather_z(mine):
        neighbour, across = swap_wide(mine, 2), swap_wide(mine, 4)
        return [mine, neighbour, across, swap_wide(across, 2)]

    cot_even, cot_first = gather_z(cotangent), swap_wide(cotangent, 1)
    chain.after(cot_first)
    tiles = cut_columns(chain, activations)
    tiles = lax.all_to_all(tiles, "narrow", split_axis=0, concat_axis=0, tiled=True)
    tiles = tiles.reshape(4 * rows, tile)
    act_even, act_first = gather_z(tiles), swap_wide(tiles, 1)
    act_odd = [swap_wide(x, 1) for x in act_even[1:]]
    chain.after(tiles, act_first)
    cot_odd = swap_wide(join(chain, cot_even[1:]), 1).reshape(12 * rows, tile)

    def slots(even, first, odd):
        res = [(even[0], 0), (first, 0)]
        for i in range(3):
            res += [(even[i + 1], 0), odd[i]]
        return [(x, functools.partial(lambda at, s: at, at)) for x, at in res]

    chain.after(*act_even[1:])
    cot_slots = slots(cot_even, cot_first, [(cot_odd, 4 * i) for i in range(3)])
    (cot,) = arrange(chain, place, cot_slots, rows, tile)
    back(0)
    chain.after(*act_odd)
    back(1)
    back_x(0)
    back(2)
    back_x(1)
    act_slots = slots(act_even, act_first, [(x, 0) for x in act_odd])
    act, act_t = arrange(chain, place, act_slots, rows, tile, True)
    chain.after(far_b[0])
    gate_up(0)
    back_x(2)
    chain.after(far_b[1], got_gu[0])
    gate_up(1)
    gate_up_x(0)
    chain.after(far_b[2])
    gate_up(2)
    gate_up_x(1)
    gate_up(3)
    gate_up_x(2)
    chain.after(got_gu[3])
    elementwise(0)
    gate_up_x(3)
    add_both(0)
    all_grads(0)
    elementwise(1)
    add_both(1)
    elementwise(2)
    add_both(2)
    elementwise(3)
    grad_part = last_part(grad_term())
    out_part = last_part(out_term())
    all_grads(1)
    grad_part = over_z(grad_part, 2)
    all_grads(2)
    out_part = over_z(out_part, 2)
    grad_part = over_z(grad_part, 4)
    all_grads(3)
    out_part = over_z(out_part, 4)
    groups = finish(chain, place, [grad_part], False)
    groups = [groups[0]] + [swap(groups[g], g) for g in range(1, 4)]
    input_gradient = place_columns(chain, place, groups)
    block_output = finish(chain, place, [out_part], True)
    return (block_output, input_gradient, *grads)


def scatter_sum(part):
    split = part.reshape(-1, 4, part.shape[0] // 4 // lax.axis_size("wide"), part.shape[-1])
    got = swap(jnp.stack([split[:, 1], split[:, 3]]), 1)
    away = (split[:, 2] + got[1]).astype(BF16)
    return (split[:, 0] + got[0]) + swap(away, 2).astype(F32)


def spread_rows(own):
    return jnp.stack(spread(own), axis=1).reshape(-1, own.shape[-1])


def local_any(activations, cotangent, gate_proj, up_proj, down_proj):
    me = lax.axis_index("narrow")
    rows = activations.shape[0]
    tile = gate_proj.shape[0]
    pieces = [lax.dynamic_slice_in_dim(activations, (me ^ g) * tile, tile, 1) for g in range(4)]
    pieces = [pieces[0]] + [swap(pieces[g], g) for g in range(1, 4)]
    cots = [lax.dynamic_slice_in_dim(cotangent, (me ^ g) * rows, rows, 0) for g in range(4)]

    def gathered(parts):
        return lax.all_gather(jnp.stack(parts), "wide", axis=0, tiled=True).reshape(-1, tile)

    features, upstream = gathered(pieces), gathered(cots)
    gate = scatter_sum(dot(features, gate_proj, NN))
    up = scatter_sum(dot(features, up_proj, NN))
    back = scatter_sum(dot(upstream, down_proj, NT))
    active, slope = silu_parts(gate)
    gate_delta = spread_rows((back * up * slope).astype(BF16))
    up_delta = spread_rows((back * active).astype(BF16))
    hidden = spread_rows((active * up).astype(BF16))

    def landed(total):
        got = lax.psum_scatter(total, "wide", scatter_dimension=0, tiled=True)
        return got.astype(BF16).reshape(4, rows, tile)

    grad = landed(dot(gate_delta, gate_proj, NT) + dot(up_delta, up_proj, NT))
    out = landed(dot(hidden, down_proj, NN))
    gate_gradient = dot(features, gate_delta, TN).astype(BF16)
    up_gradient = dot(features, up_delta, TN).astype(BF16)
    down_gradient = dot(hidden, upstream, TN).astype(BF16)

    block_output = jnp.concatenate(
        [lax.dynamic_index_in_dim(out, me ^ g, 0, keepdims=False) for g in range(4)]
    )
    grads = jnp.stack([grad[0]] + [swap(grad[g], g) for g in range(1, 4)])
    input_gradient = jnp.concatenate(
        [lax.dynamic_index_in_dim(grads, me ^ g, 0, keepdims=False) for g in range(4)], axis=1
    )
    return (block_output, input_gradient, gate_gradient, up_gradient, down_gradient)


def local(activations, cotangent, gate_proj, up_proj, down_proj):
    args = (activations, cotangent, gate_proj, up_proj, down_proj)
    rows, (tile, units) = activations.shape[0], gate_proj.shape
    fits = lax.axis_size("wide") == 8 and rows % 16 == 0
    if fits and tile % (2 * BLOCK) == 0 and units % BLOCK == 0 and units >= 6 * BLOCK:
        return local_eight(*args)
    return local_any(*args)


def solution(mesh):
    placed = (
        P(("wide", "narrow"), None),
        P("wide", "narrow"),
        P("narrow", "wide"),
        P("narrow", "wide"),
        P("wide", "narrow"),
    )
    return jax.shard_map(
        local,
        mesh=mesh,
        in_specs=placed,
        out_specs=(
            P("wide", "narrow"),
            P(("wide", "narrow"), None),
            P("narrow", "wide"),
            P("narrow", "wide"),
            P("wide", "narrow"),
        ),
        check_vma=False,
    )
```

```python
import functools

import jax
import jax.numpy as jnp
from jax import lax
from jax.experimental import pallas as pl
from jax.experimental.pallas import tpu as pltpu
from jax.sharding import PartitionSpec as P

BF16, F32 = jnp.bfloat16, jnp.float32
BLOCK = 256
VMEM_LIMIT = 64 * 1024 * 1024 - 256 * 1024
ORDER = (0, 2, 1, 3)
NN = (((1,), (0,)), ((), ()))
NT = (((1,), (1,)), ((), ()))
TN = (((0,), (0,)), ((), ()))


def dot(left, right, dims):
    return lax.dot_general(left, right, dims, preferred_element_type=F32)


def silu_parts(gate):
    sigma = jax.nn.sigmoid(gate)
    return (gate * sigma, sigma * (1.0 + gate * (1.0 - sigma)))


def swap(value, mask):
    return lax.ppermute(value, "narrow", [(i, i ^ mask) for i in range(4)])


def swap_wide(value, mask):
    return lax.ppermute(value, "wide", [(i, i ^ mask) for i in range(8)])


class Chain:
    def __init__(self):
        self.token = None
        self.waits = []

    def after(self, *arrays):
        self.waits += arrays

    def __call__(self, body, grid, ins, outs, scratch=(), flops=0, alias=None, scalar=None):
        lead = 0 if scalar is None else 1
        arrays = [a for a, _, _ in ins]
        specs = [pl.BlockSpec(block, index) for _, block, index in ins]
        unread = self.waits + ([] if self.token is None else [self.token])
        self.waits = []
        arrays += unread
        specs += [pl.BlockSpec(memory_space=pltpu.HBM)] * len(unread)
        shapes = [jax.ShapeDtypeStruct(shape, dtype) for shape, dtype, _, _ in outs]
        out_specs = [pl.BlockSpec(block, index) for _, _, block, index in outs]
        shapes.append(jax.ShapeDtypeStruct((8, 128), F32))
        out_specs.append(pl.BlockSpec((8, 128), lambda *i: (0, 0)))
        n_in, n_out = len(ins), len(outs)

        def kernel(*refs):
            head, refs = refs[:lead], refs[lead:]
            in_refs = refs[:n_in]
            rest = refs[n_in + len(unread) :]
            out_refs, token, scratch_refs = rest[:n_out], rest[n_out], rest[n_out + 1 :]
            token[...] = jnp.zeros(token.shape, F32)
            body(*head, *in_refs, *out_refs, *scratch_refs)

        res = pl.pallas_call(
            kernel,
            grid_spec=pltpu.PrefetchScalarGridSpec(
                num_scalar_prefetch=lead,
                grid=grid,
                in_specs=specs,
                out_specs=out_specs,
                scratch_shapes=list(scratch),
            ),
            out_shape=shapes,
            input_output_aliases={k + lead: v for k, v in (alias or {}).items()},
            compiler_params=pltpu.CompilerParams(vmem_limit_bytes=VMEM_LIMIT),
            cost_estimate=pl.CostEstimate(flops=1, bytes_accessed=1, transcendentals=0),
        )(*(() if scalar is None else (scalar,)), *arrays)
        self.token = res[-1]
        return res[:-1]


def group(i):
    return (i & 1) * 2 + (i >> 1)


def cut_columns(chain, rows_in):
    rows, tile = rows_in.shape[0], rows_in.shape[1] // 4

    def body(x, out):
        out[0] = x[...]

    (out,) = chain(
        body,
        (4,),
        [(rows_in, (rows, tile), lambda j: (0, j))],
        [((4, rows, tile), BF16, (1, rows, tile), lambda j: (j, 0, 0))],
    )
    return out


def join(chain, parts):
    rows, tile = parts[0].shape
    count = len(parts)

    def body(*refs):
        for i in range(count):
            refs[count][i] = refs[i][...]

    (out,) = chain(
        body,
        (1,),
        [(p, (rows, tile), lambda j: (0, 0)) for p in parts],
        [((count, rows, tile), BF16, (count, rows, tile), lambda j: (0, 0, 0))],
    )
    return out


def arrange(chain, place, slots, rows, tile, turned=False):
    q = 8 * rows

    def body(_, *refs):
        out = refs[8]
        for k in range(8):
            out[0, k] = refs[k][...]
        if turned:
            refs[9][...] = out[0].reshape(q, tile).T

    outs = [((4, 8, rows, tile), BF16, (1, 8, rows, tile), lambda g, s: (g, 0, 0, 0))]
    if turned:
        outs.append(((tile, 4 * q), BF16, (tile, q), lambda g, s: (0, g)))
    out, *rest = chain(
        body,
        (4,),
        [
            (p, (rows, tile), functools.partial(lambda at, i, s: (at(s) + (s[0] ^ group(i)), 0), at))
            for p, at in slots
        ],
        outs,
        scalar=place,
    )
    return [out.reshape(4 * q, tile), *rest]


def back_part(chain, cot, down, base, blocks):
    tokens, tile = cot.shape
    half, n = tokens // 2, blocks * BLOCK

    def body(c, w, keep, send):
        acc = dot(c[...], w[...], NT)
        keep[...] = acc[:half]
        send[...] = acc[half:].astype(BF16)

    block, at = (half, BLOCK), lambda j: (0, j)
    outs = [((half, n), dtype, block, at) for dtype in (F32, BF16)]
    return chain(
        body,
        (blocks,),
        [(cot, cot.shape, lambda j: (0, 0)), (down, (BLOCK, tile), lambda j: (base + j, 0))],
        outs,
        flops=2 * tokens * tile * n,
    )


def gate_up_part(chain, act, gate, up, base, blocks):
    tokens, tile = act.shape
    half, n = tokens // 2, blocks * BLOCK

    def body(a, wg, wu, keep, send):
        for k, w in enumerate((wg, wu)):
            acc = dot(a[...], w[...], NN)
            keep[k] = acc[:half]
            send[k] = acc[half:].astype(BF16)

    weight = ((tile, BLOCK), lambda j: (0, base + j))
    block, at = (2, half, BLOCK), lambda j: (0, 0, j)
    outs = [((2, half, n), dtype, block, at) for dtype in (F32, BF16)]
    return chain(
        body,
        (blocks,),
        [(act, act.shape, lambda j: (0, 0)), (gate, *weight), (up, *weight)],
        outs,
        flops=4 * tokens * tile * n,
    )


def add_away(chain, keep, got):
    lead, (half, n) = keep.shape[:-2], keep.shape[-2:]
    zeros = (0,) * len(lead)
    block = (*lead, half // 2, n)

    def body(a, b, out):
        out[...] = (a[...] + b[...].astype(F32)).astype(BF16)

    (out,) = chain(
        body,
        (2,),
        [(x, block, lambda i: (*zeros, 1 - i, 0)) for x in (keep, got)],
        [(keep.shape, BF16, block, lambda i: (*zeros, i, 0))],
    )
    return out


def activate(chain, keep_gu, got_gu, far_gu, keep_b, got_b, far_b, off, blocks):
    half, n = far_gu.shape[1:]
    q = half // 2

    def body(kg, gg, fg, kb, gb, fb, out):
        gate = kg[0] + gg[0].astype(F32) + fg[0].astype(F32)
        up = kg[1] + gg[1].astype(F32) + fg[1].astype(F32)
        back = kb[...] + gb[...].astype(F32) + fb[...].astype(F32)
        active, slope = silu_parts(gate)
        out[0] = (back * up * slope).astype(BF16)
        out[1] = (back * active).astype(BF16)
        out[2] = (active * up).astype(BF16)

    two = ((2, half, BLOCK), lambda j: (0, 0, j))
    one = ((half, BLOCK), lambda j: (0, off + j))
    (out,) = chain(
        body,
        (n // BLOCK,),
        [(x, *two) for x in (keep_gu, got_gu, far_gu)] + [(x, *one) for x in (keep_b, got_b, far_b)],
        [((3, half, n), BF16, (3, half, BLOCK), lambda j: (0, 0, j))],
    )
    return out


def split_slots(acc, rows, keep, send):
    view = acc.reshape(4, 8, rows, acc.shape[-1])
    for s in range(4):
        keep[s] = view[:, 2 * s]
        send[s] = view[:, 2 * s + 1].astype(BF16)


def summed(chain, parts, terms, base, blocks, halves=1, half=0, split=False):
    kinds = parts[0].shape[0]
    half_rows, n = parts[0].shape[1:]
    q = half_rows // 2
    rows = q // 8
    first_weight, dims = terms[0][1][0], terms[0][2]
    tile = first_weight.shape[1 if dims is NN else 0]
    width = tile // halves
    step = min(2 * BLOCK, width)
    off = half * (width // step)
    ins = [(p, p.shape, lambda j: (0, 0, 0)) for p in parts]
    outs, alias, plan = [], {}, []
    for first, weights, dims, prev in terms:
        refs = []
        for w in weights:
            for i in range(blocks):
                refs.append(len(ins))
                if dims is NN:
                    index = functools.partial(lambda i, j: (base + i, off + j), i)
                    ins.append((w, (BLOCK, step), index))
                else:
                    index = functools.partial(lambda i, j: (off + j, base + i), i)
                    ins.append((w, (step, BLOCK), index))
        before = None
        if prev is not None:
            before = len(ins)
            ins.append((prev, (4 * q, step), lambda j: (0, off + j)))
            if not split:
                alias[before] = len(outs)
        plan.append((first, len(weights), dims, refs, before, len(outs)))
        if split:
            shape, block = (4, 4, rows, width), (4, 4, rows, step)
            outs.append((shape, F32, block, lambda j: (0, 0, 0, j)))
            outs.append((shape, BF16, block, lambda j: (0, 0, 0, j)))
        else:
            outs.append(((4 * q, tile), F32, (4 * q, step), lambda j: (0, j)))
    n_in = len(ins)

    def body(*refs):
        out_refs, scratch = refs[n_in:-1], refs[-1]

        @pl.when(pl.program_id(0) == 0)
        def _():
            for g in range(2):
                for k in range(kinds):
                    scratch[k, g * half_rows : (g + 1) * half_rows] = refs[g][k]

        for first, count, dims, at, before, out in plan:
            total = None if before is None else refs[before][...]
            for k in range(count):
                for i in range(blocks):
                    left = scratch[first + k, :, i * BLOCK : (i + 1) * BLOCK]
                    term = dot(left, refs[at[k * blocks + i]][...], dims)
                    total = term if total is None else total + term
            if split:
                split_slots(total, rows, out_refs[out], out_refs[out + 1])
            else:
                out_refs[out][...] = total

    return chain(
        body,
        (width // step,),
        ins,
        outs,
        scratch=[pltpu.VMEM((kinds, 4 * q, n), BF16)],
        flops=6 * 4 * q * n * width,
        alias=alias,
    )


def gradients(chain, act_t, cot, parts, base, blocks, prev, units):
    tile, tokens = act_t.shape
    half = tokens // 2
    lead = 4

    def body(*refs):
        a, c, own, near = refs[:lead]
        outs = refs[-3:]
        for k in range(2):
            right = jnp.concatenate([own[k], near[k]], axis=0)
            outs[k][...] = dot(a[...], right, NN).astype(BF16)
        left = jnp.concatenate([own[2], near[2]], axis=0)
        outs[2][...] = dot(left, c[...], TN).astype(BF16)

    ins = [(act_t, act_t.shape, lambda j: (0, 0)), (cot, cot.shape, lambda j: (0, 0))]
    ins += [(p, (3, half, BLOCK), lambda j: (0, 0, j)) for p in parts]
    column = ((tile, units), BF16, (tile, BLOCK), lambda j: (0, base + j))
    outs = [column, column, ((units, tile), BF16, (BLOCK, tile), lambda j: (base + j, 0))]
    alias = {}
    if prev is not None:
        ins += [(p, (16, 128), lambda j: (0, 0)) for p in prev]
        alias = {lead + i: i for i in range(3)}
    return chain(body, (blocks,), ins, outs, flops=6 * tokens * tile * blocks * BLOCK, alias=alias)


def pass_on(chain, keep, got):
    slots = keep.shape[0]
    rest = keep.shape[1:]
    zeros = (0,) * len(rest)

    def body(k, g, *outs):
        for i in range(slots // 2):
            for out, s in zip(outs, (2 * i, 2 * i + 1)):
                out[i] = (k[s] + g[s].astype(F32)).astype(out.dtype)

    whole = ((slots, *rest), lambda j: (0, *zeros))
    half = ((slots // 2, *rest), lambda j: (0, *zeros))
    return chain(
        body,
        (1,),
        [(keep, *whole), (got, *whole)],
        [(half[0], dtype, *half) for dtype in (F32, BF16)],
    )


def finish(chain, me, halves, by_rows):
    four, rows, width = halves[0][0].shape[1:]
    tile = width * len(halves)

    def body(s, *refs):
        outs = refs[2 * len(halves) :]
        for h in range(len(halves)):
            total = refs[2 * h][0] + refs[2 * h + 1][0].astype(F32)
            columns = slice(h * width, (h + 1) * width)
            for i, g in enumerate(ORDER):
                rounded = total[i].astype(BF16)
                if by_rows:
                    outs[0][s[0] ^ g, :, columns] = rounded
                else:
                    outs[g][:, columns] = rounded

    ins = []
    for own, got in halves:
        ins += [(x, (1, four, rows, width), lambda j, s: (0, 0, 0, 0)) for x in (own, got)]
    if by_rows:
        outs = [((four, rows, tile), BF16, (four, rows, tile), lambda j, s: (0, 0, 0))]
    else:
        outs = [((rows, tile), BF16, (rows, tile), lambda j, s: (0, 0))] * 4
    res = chain(body, (1,), ins, outs, scalar=me)
    return res[0].reshape(four * rows, tile) if by_rows else res


def place_columns(chain, me, groups):
    rows, tile = groups[0].shape

    def body(s, *refs):
        for g in range(4):

            @pl.when(pl.program_id(0) == g)
            def _():
                refs[4][...] = refs[g][...]

    (out,) = chain(
        body,
        (4,),
        [(x, (rows, tile), lambda g, s: (0, 0)) for x in groups],
        [((rows, 4 * tile), BF16, (rows, tile), lambda g, s: (0, s[0] ^ g))],
        scalar=me,
    )
    return out


def spread(own):
    far = swap(own, 2)
    return [own, swap(own, 1), far, swap(far, 1)]


def chunk_sizes(total):
    small = max(1, total // 6)
    rest = total - 2 * small
    return [small, (rest + 1) // 2, rest // 2, small]


def local_eight(activations, cotangent, gate_proj, up_proj, down_proj):
    place = jnp.stack([lax.axis_index("narrow"), lax.axis_index("wide")]).astype(jnp.int32)
    rows = activations.shape[0]
    tile, units = gate_proj.shape
    sizes = chunk_sizes(units // BLOCK)
    chunks = [(sum(sizes[:c]), sizes[c]) for c in range(4)]
    backs = [chunks[0], chunks[1], (chunks[2][0], sizes[2] + sizes[3])]
    back_of = [(0, 0), (1, 0), (2, 0), (2, sizes[2])]
    chain = Chain()

    keep_b, got_b, far_b = {}, {}, {}
    keep_gu, got_gu, far_gu = {}, {}, {}
    own, near = {}, {}
    out = grad = grads = None

    def back(p):
        keep_b[p], send = back_part(chain, cot, down_proj, *backs[p])
        got_b[p] = swap(send, 1)

    def back_x(p):
        far_b[p] = swap(add_away(chain, keep_b[p], got_b[p]), 2)

    def gate_up(c):
        keep_gu[c], send = gate_up_part(chain, act, gate_proj, up_proj, *chunks[c])
        got_gu[c] = swap(send, 1)

    def gate_up_x(c):
        far_gu[c] = swap(add_away(chain, keep_gu[c], got_gu[c]), 2)

    def elementwise(c):
        p, off = back_of[c]
        own[c] = activate(
            chain, keep_gu[c], got_gu[c], far_gu[c], keep_b[p], got_b[p], far_b[p], off, sizes[c]
        )
        near[c] = swap(own[c], 1)

    def out_term():
        return (2, [down_proj], NN, out)

    def grad_term():
        return (0, [gate_proj, up_proj], NT, grad)

    def add_both(c):
        nonlocal out, grad
        out, grad = summed(chain, (own[c], near[c]), [out_term(), grad_term()], *chunks[c])

    def all_grads(c):
        nonlocal grads
        grads = gradients(chain, act_t, cot, (own[c], near[c]), *chunks[c], grads, units)

    def last_part(term, halves=1, half=0):
        keep, send = summed(chain, (own[3], near[3]), [term], *chunks[3], halves, half, True)
        return keep, swap_wide(send, 1)

    def over_z(pair, mask):
        keep, send = pass_on(chain, *pair)
        return keep, swap_wide(send, mask)

    def gather_z(mine):
        neighbour, across = swap_wide(mine, 2), swap_wide(mine, 4)
        return [mine, neighbour, across, swap_wide(across, 2)]

    cot_even, cot_first = gather_z(cotangent), swap_wide(cotangent, 1)
    chain.after(cot_first)
    tiles = cut_columns(chain, activations)
    tiles = lax.all_to_all(tiles, "narrow", split_axis=0, concat_axis=0, tiled=True)
    tiles = tiles.reshape(4 * rows, tile)
    act_even, act_first = gather_z(tiles), swap_wide(tiles, 1)
    act_odd = [swap_wide(x, 1) for x in act_even[1:]]
    chain.after(tiles, act_first)
    cot_odd = swap_wide(join(chain, cot_even[1:]), 1).reshape(12 * rows, tile)

    def slots(even, first, odd):
        res = [(even[0], 0), (first, 0)]
        for i in range(3):
            res += [(even[i + 1], 0), odd[i]]
        return [(x, functools.partial(lambda at, s: at, at)) for x, at in res]

    chain.after(*act_even[1:])
    cot_slots = slots(cot_even, cot_first, [(cot_odd, 4 * i) for i in range(3)])
    (cot,) = arrange(chain, place, cot_slots, rows, tile)
    back(0)
    chain.after(*act_odd)
    back(1)
    back_x(0)
    back(2)
    back_x(1)
    act_slots = slots(act_even, act_first, [(x, 0) for x in act_odd])
    act, act_t = arrange(chain, place, act_slots, rows, tile, True)
    chain.after(far_b[0])
    gate_up(0)
    back_x(2)
    chain.after(far_b[1], got_gu[0])
    gate_up(1)
    gate_up_x(0)
    chain.after(far_b[2])
    gate_up(2)
    gate_up_x(1)
    gate_up(3)
    gate_up_x(2)
    chain.after(got_gu[3])
    elementwise(0)
    gate_up_x(3)
    add_both(0)
    all_grads(0)
    elementwise(1)
    add_both(1)
    all_grads(1)
    elementwise(2)
    add_both(2)
    elementwise(3)
    grad_part = last_part(grad_term())
    out_parts = [last_part(out_term(), 2, 0), last_part(out_term(), 2, 1)]
    grad_part = over_z(grad_part, 2)
    all_grads(2)
    out_parts[0] = over_z(out_parts[0], 2)
    grad_part = over_z(grad_part, 4)
    out_parts[1] = over_z(out_parts[1], 2)
    out_parts[0] = over_z(out_parts[0], 4)
    all_grads(3)
    groups = finish(chain, place, [grad_part], False)
    groups = [groups[0]] + [swap(groups[g], g) for g in range(1, 4)]
    out_parts[1] = over_z(out_parts[1], 4)
    input_gradient = place_columns(chain, place, groups)
    block_output = finish(chain, place, out_parts, True)
    return (block_output, input_gradient, *grads)


def scatter_sum(part):
    split = part.reshape(-1, 4, part.shape[0] // 4 // lax.axis_size("wide"), part.shape[-1])
    got = swap(jnp.stack([split[:, 1], split[:, 3]]), 1)
    away = (split[:, 2] + got[1]).astype(BF16)
    return (split[:, 0] + got[0]) + swap(away, 2).astype(F32)


def spread_rows(own):
    return jnp.stack(spread(own), axis=1).reshape(-1, own.shape[-1])


def local_any(activations, cotangent, gate_proj, up_proj, down_proj):
    me = lax.axis_index("narrow")
    rows = activations.shape[0]
    tile = gate_proj.shape[0]
    pieces = [lax.dynamic_slice_in_dim(activations, (me ^ g) * tile, tile, 1) for g in range(4)]
    pieces = [pieces[0]] + [swap(pieces[g], g) for g in range(1, 4)]
    cots = [lax.dynamic_slice_in_dim(cotangent, (me ^ g) * rows, rows, 0) for g in range(4)]

    def gathered(parts):
        return lax.all_gather(jnp.stack(parts), "wide", axis=0, tiled=True).reshape(-1, tile)

    features, upstream = gathered(pieces), gathered(cots)
    gate = scatter_sum(dot(features, gate_proj, NN))
    up = scatter_sum(dot(features, up_proj, NN))
    back = scatter_sum(dot(upstream, down_proj, NT))
    active, slope = silu_parts(gate)
    gate_delta = spread_rows((back * up * slope).astype(BF16))
    up_delta = spread_rows((back * active).astype(BF16))
    hidden = spread_rows((active * up).astype(BF16))

    def landed(total):
        got = lax.psum_scatter(total, "wide", scatter_dimension=0, tiled=True)
        return got.astype(BF16).reshape(4, rows, tile)

    grad = landed(dot(gate_delta, gate_proj, NT) + dot(up_delta, up_proj, NT))
    out = landed(dot(hidden, down_proj, NN))
    gate_gradient = dot(features, gate_delta, TN).astype(BF16)
    up_gradient = dot(features, up_delta, TN).astype(BF16)
    down_gradient = dot(hidden, upstream, TN).astype(BF16)

    block_output = jnp.concatenate(
        [lax.dynamic_index_in_dim(out, me ^ g, 0, keepdims=False) for g in range(4)]
    )
    grads = jnp.stack([grad[0]] + [swap(grad[g], g) for g in range(1, 4)])
    input_gradient = jnp.concatenate(
        [lax.dynamic_index_in_dim(grads, me ^ g, 0, keepdims=False) for g in range(4)], axis=1
    )
    return (block_output, input_gradient, gate_gradient, up_gradient, down_gradient)


def local(activations, cotangent, gate_proj, up_proj, down_proj):
    args = (activations, cotangent, gate_proj, up_proj, down_proj)
    rows, (tile, units) = activations.shape[0], gate_proj.shape
    fits = lax.axis_size("wide") == 8 and rows % 16 == 0
    if fits and tile % (2 * BLOCK) == 0 and units % BLOCK == 0 and units >= 6 * BLOCK:
        return local_eight(*args)
    return local_any(*args)


def solution(mesh):
    placed = (
        P(("wide", "narrow"), None),
        P("wide", "narrow"),
        P("narrow", "wide"),
        P("narrow", "wide"),
        P("wide", "narrow"),
    )
    return jax.shard_map(
        local,
        mesh=mesh,
        in_specs=placed,
        out_specs=(
            P("wide", "narrow"),
            P(("wide", "narrow"), None),
            P("narrow", "wide"),
            P("narrow", "wide"),
            P("wide", "narrow"),
        ),
        check_vma=False,
    )
```
